512 devices in a mesh: ctx: 64 (over z_lo, x, core), mem: 8 (over z_hi, y).
Axes of the slice: x: 4, y: 4, z: 16 (z_hi: 2, z_lo: 8; z = z_hi * 8 + z_lo), core: 2. Of those that a mesh axis runs over, the one named last changes fastest.
Arguments:
- queries: bfloat16 [16384, 4096], P('ctx', 'mem'), may hold values from -5 to 5
- keys: bfloat16 [16384, 4096], P('ctx', 'mem'), may hold values from -5 to 5
- values: bfloat16 [16384, 4096], P('ctx', 'mem'), may hold values from -400 to 400
- memory_keys: bfloat16 [512, 64, 4096], P('ctx', None, 'mem'), may hold values from -5 to 5
- memory_values: bfloat16 [512, 64, 4096], P('ctx', None, 'mem'), may hold values from -400 to 400
- retrieval: int32 [128, 4], P('ctx'), may hold values from 0 to 511, as said below
- gate: float32 [32], P('mem'), may hold values from -2 to 2
- gain: float32 [4096], P('mem'), may hold values from 0.5 to 2
Outputs:
- attended: bfloat16 [16384, 4096], P('ctx', 'mem')
The draws below stay inside these ranges and needn't reach their ends.
Inputs may be any that keep to these rules, and one draw needn't show every extreme that they name: `retrieval`: block b belongs to owner b // 8. Among the 8 ids of the 2 tiles of one index of ctx, no owner is named more than once. There is one owner (the same for all) that every index of ctx names exactly once. The 4 ids of a tile differ.
All inputs are finite; a program needn't handle non-finite values.
Results may differ from the reference program's by a relative error of at most 0.015.
Values may be sent and summed in bfloat16 or wider, within the bound.
A program may use at most 128 MiB of HBM per device.

```python
import math
import jax
import jax.numpy as jnp
from jax import lax

HEADS = 32
HEAD_DIM = 128
TOK_DEV = 256
MBLK_DEV = 8
QTILE = 128
MBLOCK = 64
TOPK = 4
FEATURES = 4096
TOKENS = 16384
TILES = 128
TILE_DEV = 2
MEM_BLOCKS = 512
CAP = 1
WINDOW = 512


def head_scales():
    head_of = (jnp.arange(FEATURES) // HEAD_DIM).astype(jnp.float32)
    return 10.0 ** (head_of / (HEADS - 1))


def draw_queries(key, part):
    key = jax.random.fold_in(key, 1)
    entries = jnp.clip(jax.random.normal(key, (TOKENS, FEATURES), jnp.float32), -4.5, 4.5)
    return entries.astype(jnp.bfloat16)


def draw_keys(key, part):
    key = jax.random.fold_in(key, 2)
    entries = jnp.clip(jax.random.normal(key, (TOKENS, FEATURES), jnp.float32), -4.5, 4.5)
    return entries.astype(jnp.bfloat16)


def draw_memory_keys(key, part):
    key = jax.random.fold_in(key, 3)
    entries = jnp.clip(jax.random.normal(key, (MEM_BLOCKS, MBLOCK, FEATURES), jnp.float32), -4.5, 4.5)
    return entries.astype(jnp.bfloat16)


def draw_values(key, part):
    key = jax.random.fold_in(key, 4)
    row_key, entry_key = jax.random.split(key)
    row_scale = 10.0 ** jax.random.uniform(row_key, (TOKENS, 1), jnp.float32)
    entries = jnp.clip(jax.random.normal(entry_key, (TOKENS, FEATURES), jnp.float32), -4.0, 4.0)
    return (entries * row_scale * head_scales()[None, :]).astype(jnp.bfloat16)


def draw_memory_values(key, part):
    key = jax.random.fold_in(key, 5)
    row_key, entry_key = jax.random.split(key)
    row_scale = 10.0 ** jax.random.uniform(row_key, (MEM_BLOCKS, MBLOCK, 1), jnp.float32)
    entries = jnp.clip(jax.random.normal(entry_key, (MEM_BLOCKS, MBLOCK, FEATURES), jnp.float32), -4.0, 4.0)
    return (entries * row_scale * head_scales()[None, None, :]).astype(jnp.bfloat16)


def draw_retrieval(key, part):
    key = jax.random.fold_in(key, 7)
    owner_count = MEM_BLOCKS // MBLK_DEV
    groups = TILE_DEV * TOPK // CAP
    devices = TILES // TILE_DEV
    hot_key, rest_key = jax.random.split(key)
    hot_owner = jax.random.randint(hot_key, (), 0, owner_count)

    def one_device(device_key):
        perm_key, order_key, block_key = jax.random.split(device_key, 3)
        others = (hot_owner + 1 + jax.random.permutation(perm_key, owner_count - 1)) % owner_count
        chosen = jnp.concatenate([hot_owner[None], others])[:groups]
        chosen = jax.random.permutation(order_key, chosen)
        base_block = jax.random.randint(block_key, (groups,), 0, MBLK_DEV)
        within = (base_block[:, None] + jnp.arange(CAP)[None, :]) % MBLK_DEV
        return (chosen[:, None] * MBLK_DEV + within).reshape(TILE_DEV, TOPK)
    drawn = jax.vmap(one_device)(jax.random.split(rest_key, devices))
    return drawn.reshape(TILES, TOPK).astype(jnp.int32)


def block_scale(rng, extent, cuts, low, largest):
    level = 1.0
    for dim, shards_of in cuts:
        draws = jax.random.uniform(jax.random.fold_in(jax.random.fold_in(rng, 6), dim), (shards_of,), jnp.float32, low / len(cuts), largest / len(cuts))
        level = level * jnp.repeat(jnp.exp(draws), extent[dim] // shards_of).reshape((-1,) + (1,) * (len(extent) - 1 - dim))
    return level


def setup_inputs(seed: int = 0) -> dict:
    key_of = jax.random.split(jax.random.key(seed), 9)
    return {
        "queries": draw_queries(jax.random.fold_in(key_of[8], 71), 0),
        "keys": draw_keys(jax.random.fold_in(key_of[8], 71), 0),
        "values": draw_values(jax.random.fold_in(key_of[8], 71), 0),
        "memory_keys": draw_memory_keys(jax.random.fold_in(key_of[8], 71), 0),
        "memory_values": draw_memory_values(jax.random.fold_in(key_of[8], 71), 0),
        "retrieval": draw_retrieval(jax.random.fold_in(key_of[8], 71), 0),
        "gate": jnp.clip(jax.random.uniform(key_of[6], (HEADS,), jnp.float32, -2.0, 2.0) * block_scale(key_of[6], (HEADS,), ((0, 8),), -0.4, 0.0), -2.0, 2.0),
        "gain": jnp.clip(jnp.exp(math.log(2.0) - 1.3862944 * jax.random.uniform(key_of[7], (FEATURES,), jnp.float32) ** block_scale(key_of[7], (FEATURES,), ((0, 8),), -0.2, 0.2)), 0.5, 2.0),
    }


def window_attention(queries, near_keys, near_values, first_query, first_key, head_count, head_dim, window):
    query_rows = queries.shape[0]
    key_rows = near_keys.shape[0]
    query_pos = first_query + jnp.arange(query_rows, dtype=jnp.int32)
    key_pos = first_key + jnp.arange(key_rows, dtype=jnp.int32)
    offsets = query_pos[:, None] - key_pos[None, :]
    allowed = (offsets >= 0) & (offsets < window) & (key_pos >= 0)[None, :]
    score_scale = 1.0 / math.sqrt(head_dim)
    head_outputs = []
    for head_index in range(head_count):
        column = head_index * head_dim
        query_heads = queries[:, column:column + head_dim]
        key_heads = near_keys[:, column:column + head_dim]
        value_heads = near_values[:, column:column + head_dim]
        scores = jnp.dot(query_heads, key_heads.T, preferred_element_type=jnp.float32) * score_scale
        scores = jnp.where(allowed, scores, -jnp.inf)
        row_peak = lax.optimization_barrier(jnp.max(scores, axis=1, keepdims=True))
        weights = jnp.exp(scores - row_peak)
        row_total = lax.optimization_barrier(jnp.sum(weights, axis=1, keepdims=True))
        product = jnp.dot(weights.astype(jnp.bfloat16), value_heads, preferred_element_type=jnp.float32)
        head_outputs.append(product / row_total)
    return jnp.concatenate(head_outputs, axis=1)

def block_partial(tile_queries, block_keys, block_values, head_count, head_dim):
    query_rows = tile_queries.shape[0]
    blocks, key_rows = (block_keys.shape[0], block_keys.shape[1])
    query_heads = tile_queries.astype(jnp.float32).reshape(query_rows, head_count, head_dim)
    key_heads = block_keys.astype(jnp.float32).reshape(blocks, key_rows, head_count, head_dim)
    value_heads = block_values.astype(jnp.float32).reshape(blocks, key_rows, head_count, head_dim)
    score_scale = 1.0 / math.sqrt(head_dim)
    scores = jnp.einsum('qhd,bkhd->bhqk', query_heads, key_heads) * score_scale
    block_peak = lax.optimization_barrier(jnp.max(scores, axis=-1))
    weights = jnp.exp(scores - block_peak[..., None])
    block_total = lax.optimization_barrier(jnp.sum(weights, axis=-1))
    rounded = lax.optimization_barrier(weights.astype(jnp.bfloat16)).astype(jnp.float32)
    product = jnp.einsum('bhqk,bkhd->bqhd', rounded, value_heads)
    product = product / jnp.swapaxes(block_total, -1, -2)[..., None]
    return (product.astype(jnp.bfloat16).reshape(blocks, query_rows, head_count * head_dim), block_peak, block_total)

def combine_blocks(block_out, block_peak, block_total, head_count, head_dim):
    tile_peak = lax.optimization_barrier(jnp.max(block_peak, axis=0, keepdims=True))
    mix_weight = block_total * jnp.exp(block_peak - tile_peak)
    mix_total = lax.optimization_barrier(jnp.sum(mix_weight, axis=0))
    blocks, query_rows = (block_out.shape[0], block_out.shape[1])
    outputs = block_out.astype(jnp.float32).reshape(blocks, query_rows, head_count, head_dim)
    summed = lax.optimization_barrier(jnp.sum(jnp.swapaxes(mix_weight, -1, -2)[..., None] * outputs, axis=0))
    mixed = summed / jnp.swapaxes(mix_total, -1, -2)[..., None]
    return mixed.reshape(query_rows, head_count * head_dim)

def reference(queries, keys, values, memory_keys, memory_values, retrieval, gate, gain):
    padding = jnp.zeros((WINDOW, FEATURES), keys.dtype)
    padded_keys = jnp.concatenate([padding, keys], axis=0)
    padded_values = jnp.concatenate([padding, values], axis=0)

    def one_block(block_index):
        start = block_index * TOK_DEV
        block_queries = lax.dynamic_slice_in_dim(queries, start, TOK_DEV, 0)
        block_keys = lax.dynamic_slice_in_dim(padded_keys, start, WINDOW + TOK_DEV, 0)
        block_values = lax.dynamic_slice_in_dim(padded_values, start, WINDOW + TOK_DEV, 0)
        return window_attention(block_queries, block_keys, block_values, start, start - WINDOW, HEADS, HEAD_DIM, WINDOW)
    local_out = lax.map(one_block, jnp.arange(TOKENS // TOK_DEV, dtype=jnp.int32)).reshape(TOKENS, FEATURES)

    def one_tile(tile_index):
        tile_queries = lax.dynamic_slice_in_dim(queries, tile_index * QTILE, QTILE, 0)
        chosen = retrieval[tile_index]
        found_keys = memory_keys[chosen]
        found_values = memory_values[chosen]
        block_out, block_peak, block_total = block_partial(tile_queries, found_keys, found_values, HEADS, HEAD_DIM)
        return combine_blocks(block_out, block_peak, block_total, HEADS, HEAD_DIM)
    memory_out = lax.map(one_tile, jnp.arange(TILES, dtype=jnp.int32)).reshape(TOKENS, FEATURES)
    factor = jnp.repeat(jax.nn.sigmoid(gate), HEAD_DIM)
    combined = factor * memory_out + (1.0 - factor) * local_out
    square_sum = lax.optimization_barrier(jnp.sum(combined * combined, axis=1, keepdims=True))
    return (combined * gain * lax.rsqrt(square_sum / FEATURES + 1e-06)).astype(jnp.bfloat16)
```

```python
import functools
import math

import jax
import jax.numpy as jnp
from jax import lax
from jax.experimental import pallas as pl
from jax.experimental.pallas import tpu as pltpu
from jax.sharding import PartitionSpec as P

MESH = pl.DeviceIdType.MESH
ANY = pl.BlockSpec(memory_space=pl.ANY)
VMEM = pl.BlockSpec(memory_space=pltpu.VMEM)
SMEM = pl.BlockSpec(memory_space=pltpu.SMEM)
F32 = jnp.float32
BF16 = jnp.bfloat16

HD = 128
HEADS_HERE = 4
FEATURES = 4096
PLANES = 8
PLANE = 8
REQ = 8
BLK = 64
LOCAL = 64
SLOTS = 256
TOK = 256
CHUNKS = 2
ROWS = BLK // CHUNKS
SCALE = 1.0 / math.sqrt(HD)

SHORT_CAPS = (56, 88, 112, 120)
LONG_CAPS = (64, 128, 192, 256)


def iota(shape, dim):
    return lax.broadcasted_iota(jnp.int32, shape, dim).astype(F32)


def greet(peers):
    barrier = pltpu.get_barrier_semaphore()
    total = 0
    for device, present in peers:
        if present is None:
            pl.semaphore_signal(barrier, inc=1, device_id=device, device_id_type=MESH)
            total = total + 1
        else:

            @pl.when(present)
            def _(device=device):
                pl.semaphore_signal(barrier, inc=1, device_id=device, device_id_type=MESH)

            total = total + present.astype(jnp.int32)
    pl.semaphore_wait(barrier, total)


def schedule(lists, my_z, table_ref):
    block = iota((1, PLANES * LOCAL), 1)
    asker_z = jnp.floor(iota((PLANES * PLANE, 1), 0) / PLANE)
    top = jnp.full((1, PLANES * LOCAL), -1.0, F32)
    low = jnp.full((1, PLANES * LOCAL), 8.0, F32)
    for j in range(REQ):
        hit = lists[:, j : j + 1] == block
        top = jnp.maximum(top, jnp.max(jnp.where(hit, asker_z, -1.0), axis=0, keepdims=True))
        low = jnp.minimum(low, jnp.min(jnp.where(hit, asker_z, 8.0), axis=0, keepdims=True))
    before_lane = (iota((LOCAL, LOCAL), 0) < iota((LOCAL, LOCAL), 1)).astype(BF16)
    before_row = (iota((SLOTS, SLOTS), 1) < iota((SLOTS, SLOTS), 0)).astype(BF16)
    lane = iota((1, LOCAL), 1)
    fits = jnp.ones((1, 1), F32)
    injected, arrived = [], []
    for up in (True, False):
        end = jnp.full((SLOTS, 1), -1.0, F32)
        held = jnp.full((SLOTS, 1), -1.0, F32)
        mine_in = jnp.full((SLOTS, 1), -1.0, F32)
        mine_arrived = jnp.full((SLOTS, 1), -1.0, F32)
        for step in range(PLANES - 1):
            z = step if up else PLANES - 1 - step
            reach = top[:, z * LOCAL : (z + 1) * LOCAL]
            if not up:
                reach = (PLANES - 1) - low[:, z * LOCAL : (z + 1) * LOCAL]
            fresh = (reach > step).astype(F32)
            fresh_rank = jnp.dot(
                jnp.broadcast_to(fresh, (8, LOCAL)).astype(BF16), before_lane, preferred_element_type=F32
            )[0:1]
            free = (end <= step).astype(F32)
            free_rank = jnp.dot(
                before_row, jnp.broadcast_to(free, (SLOTS, HD)).astype(BF16), preferred_element_type=F32
            )[:, 0:1]
            pair = (free_rank == fresh_rank) & (free > 0.5) & (fresh > 0.5)
            code = jnp.sum(jnp.where(pair, 1.0 + lane + LOCAL * reach, 0.0), axis=1, keepdims=True)
            taken = code > 0.5
            new_end = jnp.floor((code - 1.0) / LOCAL)
            new_block = code - 1.0 - LOCAL * new_end
            inject = jnp.where(taken, new_block, -1.0)
            held = jnp.where(taken, z * LOCAL + new_block, jnp.where(free > 0.5, -1.0, held))
            end = jnp.where(taken, new_end, end)
            load = jnp.sum((end > step).astype(F32), axis=0, keepdims=True)
            fits = fits * (load <= SHORT_CAPS[min(step, 3)]).astype(F32)
            mine_in = jnp.where(my_z == z, inject, mine_in)
            mine_arrived = jnp.where(my_z == (z + 1 if up else z - 1), held, mine_arrived)
        injected.append(mine_in)
        arrived.append(mine_arrived)
    diagonal = iota((SLOTS, SLOTS), 0) == iota((SLOTS, SLOTS), 1)

    def as_row(column):
        return jnp.sum(jnp.where(diagonal, column, 0.0), axis=0, keepdims=True)

    in_up, in_down = as_row(injected[0]), as_row(injected[1])
    at_up, at_down = as_row(arrived[0]), as_row(arrived[1])
    rows = iota((8, HD), 0)
    out = jnp.where(rows == 0, in_up[:, :HD], 0.0)
    out = jnp.where(rows == 1, in_up[:, HD:], out)
    out = jnp.where(rows == 2, in_down[:, :HD], out)
    out = jnp.where(rows == 3, in_down[:, HD:], out)
    out = jnp.where(rows == 4, fits, out)
    table_ref[1] = out.astype(jnp.int32)

    slot = iota((1, SLOTS), 1)
    mine = jnp.zeros((PLANE, HD), F32)
    for z in range(PLANES):
        mine = jnp.where(my_z == z, lists[z * PLANE : (z + 1) * PLANE], mine)
    place = jnp.zeros((PLANE, HD), F32)
    lanes = iota((PLANE, HD), 1)
    z_here = my_z.astype(F32)
    for j in range(REQ):
        wanted = mine[:, j : j + 1]
        owner_z = jnp.floor(wanted / LOCAL)
        slot_up = jnp.sum(jnp.where(at_up == wanted, slot, 0.0), axis=1, keepdims=True)
        slot_down = jnp.sum(jnp.where(at_down == wanted, slot, 0.0), axis=1, keepdims=True)
        found = jnp.where(owner_z == z_here, wanted - LOCAL * owner_z, LOCAL + SLOTS + slot_down)
        found = jnp.where(owner_z < z_here, LOCAL + slot_up, found)
        place = jnp.where(lanes == j, found, place)
    table_ref[0] = place.astype(jnp.int32)


def spread_kernel(
    ids_ref, mk_ref, mv_ref, *rest
):
    pools = rest[:CHUNKS]
    table_ref, line, lists, send1, recv1, send2, recv2, send_a, recv_a, own_sem = rest[CHUNKS:]
    me = lax.axis_index("ctx")
    z, p = me // PLANE, me % PLANE
    x, core = p // 2, p % 2

    def in_plane(r):
        return {"ctx": z * PLANE + (p + r) % PLANE}

    def on_line(r):
        return {"ctx": ((z + r) % PLANES) * PLANE + p}

    greet([(in_plane(r), None) for r in range(1, 8)] + [(on_line(r), None) for r in range(1, 8)])

    lanes = lax.broadcasted_iota(jnp.int32, (8, HD), 1)
    row = jnp.zeros((8, HD), jnp.int32)
    for j in range(REQ):
        row = jnp.where(lanes == j, ids_ref[j // 4, j % 4], row)
    line[p] = row

    def copy1(r):
        return pltpu.make_async_remote_copy(
            src_ref=line.at[p],
            dst_ref=line.at[p],
            send_sem=send1.at[r],
            recv_sem=recv1.at[p],
            device_id=in_plane(r),
            device_id_type=MESH,
        )

    def arrival1(r):
        q = (p + r) % PLANE
        return pltpu.make_async_remote_copy(
            src_ref=line.at[q],
            dst_ref=line.at[q],
            send_sem=send1.at[r],
            recv_sem=recv1.at[q],
            device_id=in_plane(r),
            device_id_type=MESH,
        )

    for r in range(1, 8):
        copy1(r).start()

    def part(r, chunk, ref):
        q = (p + r) % PLANE
        return ref.at[:, pl.ds(chunk * ROWS, ROWS), pl.ds(pl.multiple_of((q // 2) * HD, HD), HD)]

    def copy_a(r, chunk, ref):
        return pltpu.make_async_remote_copy(
            src_ref=part(r, chunk, ref),
            dst_ref=pools[chunk].at[pl.ds(p * 8, 8)],
            send_sem=send_a.at[chunk, r],
            recv_sem=recv_a.at[chunk, p],
            device_id=in_plane(r),
            device_id_type=MESH,
        )

    def arrival_a(r, chunk):
        q = (p + r) % PLANE
        return pltpu.make_async_remote_copy(
            src_ref=part(r, chunk, mk_ref),
            dst_ref=pools[chunk].at[pl.ds(q * 8, 8)],
            send_sem=send_a.at[chunk, r],
            recv_sem=recv_a.at[chunk, q],
            device_id=in_plane(r),
            device_id_type=MESH,
        )

    for chunk in range(CHUNKS):
        for r in (4, 3, 5, 2, 6, 1, 7):
            to_core = (core + r) % 2

            @pl.when(to_core == 0)
            def _():
                copy_a(r, chunk, mk_ref).start()

            @pl.when(to_core == 1)
            def _():
                copy_a(r, chunk, mv_ref).start()

        def own(ref, chunk=chunk):
            return pltpu.make_async_copy(
                part(0, chunk, ref), pools[chunk].at[pl.ds(p * 8, 8)], own_sem.at[chunk]
            )

        @pl.when(core == 0)
        def _():
            own(mk_ref).start()

        @pl.when(core == 1)
        def _():
            own(mv_ref).start()

    for r in range(1, 8):
        arrival1(r).wait_recv()
    rows = lax.broadcasted_iota(jnp.int32, (8, HD), 0)
    whole = jnp.zeros((8, HD), jnp.int32)
    for q in range(PLANE):
        whole = jnp.where(rows == q, line[q], whole)
    lists[z] = whole

    def copy2(r):
        return pltpu.make_async_remote_copy(
            src_ref=lists.at[z],
            dst_ref=lists.at[z],
            send_sem=send2.at[r],
            recv_sem=recv2.at[z],
            device_id=on_line(r),
            device_id_type=MESH,
        )

    def arrival2(r):
        q = (z + r) % PLANES
        return pltpu.make_async_remote_copy(
            src_ref=lists.at[q],
            dst_ref=lists.at[q],
            send_sem=send2.at[r],
            recv_sem=recv2.at[q],
            device_id=on_line(r),
            device_id_type=MESH,
        )

    for r in range(1, 8):
        copy2(r).start()
    for r in range(1, 8):
        arrival2(r).wait_recv()
    schedule(lists[...].reshape(PLANES * PLANE, HD).astype(F32), z, table_ref)

    for r in range(1, 8):
        copy1(r).wait_send()
        copy2(r).wait_send()
    for chunk in range(CHUNKS):
        pltpu.make_async_copy(
            part(0, chunk, mk_ref), pools[chunk].at[pl.ds(p * 8, 8)], own_sem.at[chunk]
        ).wait()
        for r in range(1, 8):
            copy_a(r, chunk, mk_ref).wait_send()
            arrival_a(r, chunk).wait_recv()


def spread(retrieval, mk, mv):
    return pl.pallas_call(
        spread_kernel,
        out_shape=[jax.ShapeDtypeStruct((LOCAL, ROWS, HD), BF16)] * CHUNKS
        + [jax.ShapeDtypeStruct((2, 8, HD), jnp.int32)],
        in_specs=[SMEM, ANY, ANY],
        out_specs=[ANY] * CHUNKS + [VMEM],
        scratch_shapes=[
            pltpu.VMEM((PLANE, 8, HD), jnp.int32),
            pltpu.VMEM((PLANES, 8, HD), jnp.int32),
            pltpu.SemaphoreType.DMA((8,)),
            pltpu.SemaphoreType.DMA((8,)),
            pltpu.SemaphoreType.DMA((8,)),
            pltpu.SemaphoreType.DMA((8,)),
            pltpu.SemaphoreType.DMA((CHUNKS, 8)),
            pltpu.SemaphoreType.DMA((CHUNKS, 8)),
            pltpu.SemaphoreType.DMA((CHUNKS,)),
        ],
        compiler_params=pltpu.CompilerParams(
            collective_id=0, has_side_effects=True, vmem_limit_bytes=32 << 20
        ),
        name="spread_blocks",
    )(retrieval, mk, mv)


def attend_kernel(caps, group, delay, *refs):
    slots = caps[-1]
    groups = slots // group
    table, gate_ref, q_ref, k_ref, v_ref, gain_ref = refs[:6]
    rest = list(refs[6:])

    def take(n):
        got = rest[:n]
        del rest[:n]
        return got

    given = take(CHUNKS)
    (out_ref,) = take(1)
    near_k, near_v, mixed = take(3)
    pools, ups, downs = take(CHUNKS), take(CHUNKS), take(CHUNKS)
    ups_out, downs_out = take(CHUNKS), take(CHUNKS)
    parts_out, parts = take(CHUNKS), take(CHUNKS)
    squares_out, squares = take(2)
    (
        pool_sem,
        own_sem,
        halo_send,
        halo_recv,
        up_send,
        up_recv,
        down_send,
        down_recv,
        part_send,
        part_recv,
        sq_send,
        sq_recv,
    ) = rest

    me = lax.axis_index("ctx")
    mem = lax.axis_index("mem")
    z, p = me // PLANE, me % PLANE
    last = PLANES * PLANE - 1

    def in_plane(r):
        return {"ctx": z * PLANE + (p + r) % PLANE}

    def mem_peer(r):
        return {"mem": (mem + r) % 8}

    above, below = {"ctx": me + PLANE}, {"ctx": me - PLANE}
    loads = [
        pltpu.make_async_copy(given[c], pools[c], pool_sem.at[c]) for c in range(CHUNKS)
    ] + [
        pltpu.make_async_copy(k_ref, near_k.at[pl.ds(2 * TOK, TOK)], own_sem.at[0]),
        pltpu.make_async_copy(v_ref, near_v.at[pl.ds(2 * TOK, TOK)], own_sem.at[1]),
    ]
    for load in loads:
        load.start()

    greet(
        [(in_plane(r), None) for r in range(1, 8)]
        + [(mem_peer(r), None) for r in range(1, 8)]
        + [(above, z < PLANES - 1), (below, z > 0)]
        + [({"ctx": me + d}, me + d <= last) for d in (1, 2)]
        + [({"ctx": me - d}, me - d >= 0) for d in (1, 2)]
    )

    def halo(d, which):
        ref, near = ((k_ref, near_k), (v_ref, near_v))[which]
        return pltpu.make_async_remote_copy(
            src_ref=ref,
            dst_ref=near.at[pl.ds((2 - d) * TOK, TOK)],
            send_sem=halo_send.at[2 * d - 2 + which],
            recv_sem=halo_recv.at[2 * d - 2 + which],
            device_id={"ctx": me + d},
            device_id_type=MESH,
        )

    for d in (1, 2):

        @pl.when(me + d <= last)
        def _():
            halo(d, 0).start()
            halo(d, 1).start()

        @pl.when(me - d < 0)
        def _():
            near_k[pl.ds((2 - d) * TOK, TOK)] = jnp.zeros((TOK, HEADS_HERE * HD), BF16)
            near_v[pl.ds((2 - d) * TOK, TOK)] = jnp.zeros((TOK, HEADS_HERE * HD), BF16)

    for load in loads:
        load.wait()

    caps_g = [c // group for c in caps]

    def cap_at(step):
        value = jnp.int32(caps_g[3])
        for i in (2, 1, 0):
            value = jnp.where(step == i, caps_g[i], value)
        return value

    def conveyor(k, step, target, pool, into, onward, send, recv, row):
        cap = cap_at(step)
        position = jnp.where(step <= 3, k + groups - cap, k - delay * (step - 3))
        inside = (position >= 0) & (position < CHUNKS * groups)
        at = jnp.maximum(position, 0)
        chunk = at // groups
        g = groups - 1 - at % groups
        active = inside & (g < cap)
        incoming = (step > 0) & (g < cap_at(step - 1))

        def copy(c):
            span = pl.ds(g * group, group)
            return pltpu.make_async_remote_copy(
                src_ref=onward[c].at[span],
                dst_ref=into[c].at[span],
                send_sem=send.at[c, g],
                recv_sem=recv.at[c, g],
                device_id=target,
                device_id_type=MESH,
            )

        for c in range(CHUNKS):

            @pl.when(active & (chunk == c))
            def _(c=c):
                @pl.when(incoming)
                def _():
                    copy(c).wait_recv()

                @pl.when(step < PLANES - 1)
                def _():
                    for i in range(group):
                        slot = g * group + i
                        inject = table[1, row + slot // HD, slot % HD]
                        local = pool[c][jnp.maximum(inject, 0)]
                        onward[c][slot] = jnp.where(inject >= 0, local, into[c][slot])
                    copy(c).start()

    def part_copy(c, r):
        q = (p + r) % PLANE
        return pltpu.make_async_remote_copy(
            src_ref=parts_out[c].at[q],
            dst_ref=parts[c].at[p],
            send_sem=part_send.at[c, r],
            recv_sem=part_recv.at[c, p],
            device_id=in_plane(r),
            device_id_type=MESH,
        )

    def part_arrival(c, r):
        q = (p + r) % PLANE
        return pltpu.make_async_remote_copy(
            src_ref=parts_out[c].at[q],
            dst_ref=parts[c].at[q],
            send_sem=part_send.at[c, r],
            recv_sem=part_recv.at[c, q],
            device_id=in_plane(r),
            device_id_type=MESH,
        )

    def hand_out(c):
        def pick(q, j):
            place = table[0, q, j]
            own = pools[c][jnp.minimum(place, LOCAL - 1)]
            from_below = ups[c][jnp.clip(place - LOCAL, 0, slots - 1)]
            from_above = downs[c][jnp.clip(place - LOCAL - SLOTS, 0, slots - 1)]
            return jnp.where(
                place < LOCAL, own, jnp.where(place < LOCAL + SLOTS, from_below, from_above)
            )

        for r in (4, 3, 5, 2, 6, 1, 7):
            q = (p + r) % PLANE
            for j in range(REQ):
                parts_out[c][q, j] = pick(q, j)
            part_copy(c, r).start()
        for j in range(REQ):
            parts[c][p, j] = pick(p, j)

    def window_piece(head, tile):
        columns = pl.ds(pl.multiple_of(head * HD, HD), HD)
        rows = pl.ds(pl.multiple_of(tile * 128, 128), 128)
        near = pl.ds(pl.multiple_of(tile * 128, 128), 640)
        scores = lax.dot_general(
            q_ref[rows, columns],
            near_k[near, columns],
            (((1,), (1,)), ((), ())),
            preferred_element_type=F32,
        )
        key = lax.broadcasted_iota(jnp.int32, (128, 640), 1)
        ahead = key - lax.broadcasted_iota(jnp.int32, (128, 640), 0)
        first = me * TOK - 2 * TOK + tile * 128
        allowed = (ahead > 0) & (ahead <= 512) & (key >= -first)
        scores = jnp.where(allowed, scores * SCALE, -jnp.inf)
        weights = jnp.exp(scores - jnp.max(scores, axis=1, keepdims=True))
        total = jnp.sum(weights, axis=1, keepdims=True)
        product = jnp.dot(weights.astype(BF16), near_v[near, columns], preferred_element_type=F32)
        mixed[rows, columns] = product / total

    steps = CHUNKS * groups + 4 * delay
    far = jnp.maximum(z, PLANES - 1 - z) - 3
    pieces = 2 * HEADS_HERE
    every = max(1, (steps - 12) // (pieces + 2))
    first_piece = steps - 4 - every * pieces

    def step_body(k, carry):
        conveyor(k, z, above, pools, ups, ups_out, up_send, up_recv, 0)
        conveyor(k, PLANES - 1 - z, below, pools, downs, downs_out, down_send, down_recv, 2)
        for c in range(CHUNKS):

            @pl.when(k == (c + 1) * groups - 1 + delay * far)
            def _(c=c):
                hand_out(c)

        @pl.when(k == first_piece)
        def _():
            for d in (1, 2):

                @pl.when(me - d >= 0)
                def _():
                    halo(d, 0).wait_recv()
                    halo(d, 1).wait_recv()

        since = k - first_piece
        piece = jnp.maximum(since, 0) // every

        @pl.when((since >= 0) & (since % every == 0) & (piece < pieces))
        def _():
            window_piece(piece // 2, piece % 2)

        return carry

    lax.fori_loop(0, steps, step_body, 0)

    for c in range(CHUNKS):
        for r in range(1, 8):
            part_arrival(c, r).wait_recv()

    opened = 1.0 / (1.0 + jnp.exp(-gate_ref[...]))
    eye = lax.broadcasted_iota(jnp.int32, (128, 128), 0) == lax.broadcasted_iota(
        jnp.int32, (128, 128), 1
    )
    for tile in range(2):
        rows = pl.ds(tile * 128, 128)
        total_square = jnp.zeros((128, 1), F32)
        for head in range(HEADS_HERE):
            columns = pl.ds(head * HD, HD)
            keys = [parts[c][2 * head, 4 * tile : 4 * tile + 4].reshape(4 * ROWS, HD) for c in range(CHUNKS)]
            vals = [parts[c][2 * head + 1, 4 * tile : 4 * tile + 4].reshape(4 * ROWS, HD) for c in range(CHUNKS)]
            scores = lax.dot_general(
                q_ref[rows, columns],
                jnp.concatenate(keys, axis=0),
                (((1,), (1,)), ((), ())),
                preferred_element_type=F32,
            ) * SCALE
            weights = jnp.exp(scores - jnp.max(scores, axis=1, keepdims=True))
            total = jnp.sum(weights, axis=1, keepdims=True)
            product = jnp.dot(
                weights.astype(BF16), jnp.concatenate(vals, axis=0), preferred_element_type=F32
            )
            share = opened[:, head : head + 1]
            both = share * (product / total) + (1.0 - share) * mixed[rows, columns]
            mixed[rows, columns] = both
            total_square += jnp.sum(both * both, axis=1, keepdims=True)
        squares_out[pl.ds(tile * 8, 8)] = jnp.broadcast_to(
            jnp.sum(jnp.where(eye, total_square, 0.0), axis=0, keepdims=True), (8, 128)
        )

    def square_copy(r):
        return pltpu.make_async_remote_copy(
            src_ref=squares_out,
            dst_ref=squares.at[mem],
            send_sem=sq_send.at[r],
            recv_sem=sq_recv.at[mem],
            device_id=mem_peer(r),
            device_id_type=MESH,
        )

    def square_arrival(r):
        return pltpu.make_async_remote_copy(
            src_ref=squares_out,
            dst_ref=squares.at[(mem + r) % 8],
            send_sem=sq_send.at[r],
            recv_sem=sq_recv.at[(mem + r) % 8],
            device_id=mem_peer(r),
            device_id_type=MESH,
        )

    for r in (4, 1, 2, 3, 5, 6, 7):
        square_copy(r).start()
    squares[mem] = squares_out[...]
    for r in range(1, 8):
        square_arrival(r).wait_recv()
    summed = squares[0]
    for m in range(1, 8):
        summed = summed + squares[m]
    for tile in range(2):
        rows = pl.ds(tile * 128, 128)
        column = jnp.sum(
            jnp.where(eye, summed[tile * 8 : tile * 8 + 1], 0.0), axis=1, keepdims=True
        )
        factor = lax.rsqrt(column / FEATURES + 1e-6)
        out_ref[rows] = (mixed[rows] * gain_ref[...] * factor).astype(BF16)

    for r in range(1, 8):
        square_copy(r).wait_send()
        for c in range(CHUNKS):
            part_copy(c, r).wait_send()
    for d in (1, 2):

        @pl.when(me + d <= last)
        def _():
            halo(d, 0).wait_send()
            halo(d, 1).wait_send()

    for step, into, onward, send, recv, target in (
        (z, ups, ups_out, up_send, up_recv, above),
        (PLANES - 1 - z, downs, downs_out, down_send, down_recv, below),
    ):

        @pl.when(step < PLANES - 1)
        def _():
            def sent(g, carry):
                span = pl.ds(g * group, group)
                for c in range(CHUNKS):
                    pltpu.make_async_remote_copy(
                        src_ref=onward[c].at[span],
                        dst_ref=into[c].at[span],
                        send_sem=send.at[c, g],
                        recv_sem=recv.at[c, g],
                        device_id=target,
                        device_id_type=MESH,
                    ).wait_send()
                return carry

            lax.fori_loop(0, cap_at(step), sent, 0)


def attend(caps, group, delay, collective_id, table, gate, q, k, v, gain, *pools):
    slots = caps[-1]
    groups = slots // group
    ring = [pltpu.VMEM((slots, ROWS, HD), BF16)] * CHUNKS
    hand = [pltpu.VMEM((PLANE, REQ, ROWS, HD), BF16)] * CHUNKS
    dma = pltpu.SemaphoreType.DMA
    return pl.pallas_call(
        functools.partial(attend_kernel, caps, group, delay),
        out_shape=jax.ShapeDtypeStruct((TOK, HEADS_HERE * HD), BF16),
        in_specs=[SMEM, VMEM, VMEM, ANY, ANY, VMEM] + [ANY] * CHUNKS,
        out_specs=VMEM,
        scratch_shapes=[
            pltpu.VMEM((3 * TOK, HEADS_HERE * HD), BF16),
            pltpu.VMEM((3 * TOK, HEADS_HERE * HD), BF16),
            pltpu.VMEM((TOK, HEADS_HERE * HD), F32),
            *[pltpu.VMEM((LOCAL, ROWS, HD), BF16)] * CHUNKS,
            *ring,
            *ring,
            *ring,
            *ring,
            *hand,
            *hand,
            pltpu.VMEM((16, HD), F32),
            pltpu.VMEM((8, 16, HD), F32),
            dma((CHUNKS,)),
            dma((2,)),
            dma((4,)),
            dma((4,)),
            dma((CHUNKS, groups)),
            dma((CHUNKS, groups)),
            dma((CHUNKS, groups)),
            dma((CHUNKS, groups)),
            dma((CHUNKS, 8)),
            dma((CHUNKS, 8)),
            dma((8,)),
            dma((8,)),
        ],
        compiler_params=pltpu.CompilerParams(
            collective_id=collective_id, has_side_effects=True, vmem_limit_bytes=48 << 20
        ),
        name="attend_" + str(slots),
    )(table, gate, q, k, v, gain, *pools)


def shards(queries, keys, values, memory_keys, memory_values, retrieval, gate, gain):
    *pools, table = spread(retrieval, memory_keys, memory_values)
    fits = table[1, 4, 0] > 0
    operands = (
        table,
        gate.reshape(1, -1),
        queries,
        keys,
        values,
        gain.reshape(1, -1),
        *pools,
    )
    return lax.cond(
        fits,
        functools.partial(attend, SHORT_CAPS, 8, 2, 1),
        functools.partial(attend, LONG_CAPS, 16, 2, 2),
        *operands,
    )


def solution(mesh):
    in_specs = (
        P("ctx", "mem"),
        P("ctx", "mem"),
        P("ctx", "mem"),
        P("ctx", None, "mem"),
        P("ctx", None, "mem"),
        P("ctx", None),
        P("mem"),
        P("mem"),
    )
    return jax.shard_map(
        shards, mesh=mesh, in_specs=in_specs, out_specs=P("ctx", "mem"), check_vma=False
    )
```

```python
import functools
import math

import jax
import jax.numpy as jnp
from jax import lax
from jax.experimental import pallas as pl
from jax.experimental.pallas import tpu as pltpu
from jax.sharding import PartitionSpec as P

MESH = pl.DeviceIdType.MESH
HBM = pl.BlockSpec(memory_space=pltpu.HBM)
VMEM = pl.BlockSpec(memory_space=pltpu.VMEM)
SMEM = pl.BlockSpec(memory_space=pltpu.SMEM)
F32 = jnp.float32
BF16 = jnp.bfloat16

HD = 128
HEADS_HERE = 4
FEATURES = 4096
PLANES = 8
PLANE = 8
REQ = 8
BLK = 64
LOCAL = 64
SLOTS = 256
TOK = 256
CHUNKS = 2
ROWS = BLK // CHUNKS
SCALE = 1.0 / math.sqrt(HD)

TIERS = (
    ((48, 80, 96, 104), 8, (3, 7, 10, 11), 16),
    ((56, 88, 104, 112), 8, (3, 7, 10, 11), 16),
    ((64, 128, 192, 256), 16, (2, 4, 6, 8), 0),
)
REACHES = (7, 1, 2, 3, 4, 5, 6)


def iota(shape, dim):
    return lax.broadcasted_iota(jnp.int32, shape, dim).astype(F32)


def greet(peers):
    barrier = pltpu.get_barrier_semaphore()
    total = 0
    for device, present in peers:
        if present is None:
            pl.semaphore_signal(barrier, inc=1, device_id=device, device_id_type=MESH)
            total = total + 1
        else:

            @pl.when(present)
            def _(device=device):
                pl.semaphore_signal(barrier, inc=1, device_id=device, device_id_type=MESH)

            total = total + present.astype(jnp.int32)
    pl.semaphore_wait(barrier, total)


def schedule(lists, my_z, table_ref):
    block = iota((1, PLANES * LOCAL), 1)
    asker_z = jnp.floor(iota((PLANES * PLANE, 1), 0) / PLANE)
    top = jnp.full((1, PLANES * LOCAL), -1.0, F32)
    low = jnp.full((1, PLANES * LOCAL), 8.0, F32)
    for j in range(REQ):
        hit = lists[:, j : j + 1] == block
        top = jnp.maximum(top, jnp.max(jnp.where(hit, asker_z, -1.0), axis=0, keepdims=True))
        low = jnp.minimum(low, jnp.min(jnp.where(hit, asker_z, 8.0), axis=0, keepdims=True))
    before_lane = (iota((LOCAL, LOCAL), 0) < iota((LOCAL, LOCAL), 1)).astype(BF16)
    after_row = (iota((SLOTS, SLOTS), 1) > iota((SLOTS, SLOTS), 0)).astype(BF16)
    before_kind = (iota((8, 8), 1) < iota((8, 8), 0)).astype(BF16)
    slot_column = iota((SLOTS, 1), 0)
    kind = jnp.full((8, 1), -1.0, F32)
    for i, reach in enumerate(REACHES):
        kind = jnp.where(iota((8, 1), 0) == i, reach, kind)
    lane = iota((1, LOCAL), 1)
    fits = [jnp.ones((1, 1), F32) for _ in TIERS[:-1]]
    injected, arrived = [], []
    for up in (True, False):
        height = jnp.zeros((1, 1), F32)
        end = jnp.full((SLOTS, 1), -1.0, F32)
        held = jnp.full((SLOTS, 1), -1.0, F32)
        mine_in = jnp.full((SLOTS, 1), -1.0, F32)
        mine_arrived = jnp.full((SLOTS, 1), -1.0, F32)
        for step in range(PLANES - 1):
            z = step if up else PLANES - 1 - step
            reach = top[:, z * LOCAL : (z + 1) * LOCAL]
            if not up:
                reach = (PLANES - 1) - low[:, z * LOCAL : (z + 1) * LOCAL]
            fresh = (reach > step).astype(F32)
            kinds = (reach == kind).astype(F32) * fresh
            of_kind = jnp.dot(kinds.astype(BF16), before_lane, preferred_element_type=F32)
            earlier = jnp.dot(
                before_kind,
                jnp.broadcast_to(jnp.sum(kinds, axis=1, keepdims=True), (8, HD)).astype(BF16),
                preferred_element_type=F32,
            )[:, 0:1]
            fresh_rank = jnp.sum(kinds * (of_kind + earlier), axis=0, keepdims=True)
            load = jnp.sum((end > step).astype(F32), axis=0, keepdims=True) + jnp.sum(
                fresh, axis=1, keepdims=True
            )
            height = jnp.maximum(height, load)
            free = ((end <= step) & (slot_column < height)).astype(F32)
            free_rank = jnp.dot(
                after_row, jnp.broadcast_to(free, (SLOTS, HD)).astype(BF16), preferred_element_type=F32
            )[:, 0:1]
            pair = (free_rank == fresh_rank) & (free > 0.5) & (fresh > 0.5)
            code = jnp.sum(jnp.where(pair, 1.0 + lane + LOCAL * reach, 0.0), axis=1, keepdims=True)
            taken = code > 0.5
            new_end = jnp.floor((code - 1.0) / LOCAL)
            new_block = code - 1.0 - LOCAL * new_end
            inject = jnp.where(taken, new_block, -1.0)
            held = jnp.where(taken, z * LOCAL + new_block, jnp.where(end <= step, -1.0, held))
            end = jnp.where(taken, new_end, end)
            fits = [
                fit * (load <= tier[0][min(step, 3)]).astype(F32)
                for fit, tier in zip(fits, TIERS)
            ]
            if step == PLANES - 2:
                lowest = jnp.min(
                    jnp.where(end > step, slot_column, SLOTS), axis=0, keepdims=True
                )
                fits = [
                    fit * (lowest >= tier[3]).astype(F32) for fit, tier in zip(fits, TIERS)
                ]
            mine_in = jnp.where(my_z == z, inject, mine_in)
            mine_arrived = jnp.where(my_z == (z + 1 if up else z - 1), held, mine_arrived)
        injected.append(mine_in)
        arrived.append(mine_arrived)
    diagonal = iota((SLOTS, SLOTS), 0) == iota((SLOTS, SLOTS), 1)

    def as_row(column):
        return jnp.sum(jnp.where(diagonal, column, 0.0), axis=0, keepdims=True)

    in_up, in_down = as_row(injected[0]), as_row(injected[1])
    at_up, at_down = as_row(arrived[0]), as_row(arrived[1])
    rows = iota((8, HD), 0)
    out = jnp.where(rows == 0, in_up[:, :HD], 0.0)
    out = jnp.where(rows == 1, in_up[:, HD:], out)
    out = jnp.where(rows == 2, in_down[:, :HD], out)
    out = jnp.where(rows == 3, in_down[:, HD:], out)
    out = jnp.where(rows == 4, len(fits) - sum(fits), out)
    table_ref[1] = out.astype(jnp.int32)

    slot = iota((1, SLOTS), 1)
    mine = jnp.zeros((PLANE, HD), F32)
    for z in range(PLANES):
        mine = jnp.where(my_z == z, lists[z * PLANE : (z + 1) * PLANE], mine)
    place = jnp.zeros((PLANE, HD), F32)
    lanes = iota((PLANE, HD), 1)
    z_here = my_z.astype(F32)
    for j in range(REQ):
        wanted = mine[:, j : j + 1]
        owner_z = jnp.floor(wanted / LOCAL)
        slot_up = jnp.sum(jnp.where(at_up == wanted, slot, 0.0), axis=1, keepdims=True)
        slot_down = jnp.sum(jnp.where(at_down == wanted, slot, 0.0), axis=1, keepdims=True)
        found = jnp.where(owner_z == z_here, wanted - LOCAL * owner_z, LOCAL + SLOTS + slot_down)
        found = jnp.where(owner_z < z_here, LOCAL + slot_up, found)
        place = jnp.where(lanes == j, found, place)
    table_ref[0] = place.astype(jnp.int32)


def spread_kernel(
    ids_ref, mk_ref, mv_ref, k_ref, v_ref, *rest
):
    pools = rest[:CHUNKS]
    (
        edge_ref,
        table_ref,
        line,
        lists,
        send1,
        recv1,
        send2,
        recv2,
        send_a,
        recv_a,
        own_sem,
        edge_send,
        edge_recv,
    ) = rest[CHUNKS:]
    me = lax.axis_index("ctx")
    z, p = me // PLANE, me % PLANE
    x, core = p // 2, p % 2

    def in_plane(r):
        return {"ctx": z * PLANE + (p + r) % PLANE}

    def on_line(r):
        return {"ctx": ((z + r) % PLANES) * PLANE + p}

    greet([(in_plane(r), None) for r in range(1, 8)] + [(on_line(r), None) for r in range(1, 8)])

    lanes = lax.broadcasted_iota(jnp.int32, (8, HD), 1)
    row = jnp.zeros((8, HD), jnp.int32)
    for j in range(REQ):
        row = jnp.where(lanes == j, ids_ref[j // 4, j % 4], row)
    line[p] = row

    def copy1(r):
        return pltpu.make_async_remote_copy(
            src_ref=line.at[p],
            dst_ref=line.at[p],
            send_sem=send1.at[r],
            recv_sem=recv1.at[p],
            device_id=in_plane(r),
            device_id_type=MESH,
        )

    def arrival1(r):
        q = (p + r) % PLANE
        return pltpu.make_async_remote_copy(
            src_ref=line.at[q],
            dst_ref=line.at[q],
            send_sem=send1.at[r],
            recv_sem=recv1.at[q],
            device_id=in_plane(r),
            device_id_type=MESH,
        )

    for r in range(1, 8):
        copy1(r).start()

    def part(r, chunk, ref):
        q = (p + r) % PLANE
        return ref.at[:, pl.ds(chunk * ROWS, ROWS), pl.ds(pl.multiple_of((q // 2) * HD, HD), HD)]

    def copy_a(r, chunk, ref):
        return pltpu.make_async_remote_copy(
            src_ref=part(r, chunk, ref),
            dst_ref=pools[chunk].at[pl.ds(p * 8, 8)],
            send_sem=send_a.at[chunk, r],
            recv_sem=recv_a.at[chunk, p],
            device_id=in_plane(r),
            device_id_type=MESH,
        )

    def arrival_a(r, chunk):
        q = (p + r) % PLANE
        return pltpu.make_async_remote_copy(
            src_ref=part(r, chunk, mk_ref),
            dst_ref=pools[chunk].at[pl.ds(q * 8, 8)],
            send_sem=send_a.at[chunk, r],
            recv_sem=recv_a.at[chunk, q],
            device_id=in_plane(r),
            device_id_type=MESH,
        )

    for chunk in range(CHUNKS):
        for r in (4, 3, 5, 2, 6, 1, 7):
            to_core = (core + r) % 2

            @pl.when(to_core == 0)
            def _():
                copy_a(r, chunk, mk_ref).start()

            @pl.when(to_core == 1)
            def _():
                copy_a(r, chunk, mv_ref).start()

        def own(ref, chunk=chunk):
            return pltpu.make_async_copy(
                part(0, chunk, ref), pools[chunk].at[pl.ds(p * 8, 8)], own_sem.at[chunk]
            )

        @pl.when(core == 0)
        def _():
            own(mk_ref).start()

        @pl.when(core == 1)
        def _():
            own(mv_ref).start()

    def edge_part(q):
        ref = v_ref if q % 2 else k_ref
        return ref.at[:, pl.ds(q // 2 * HD, HD)]

    def edge_copy(q):
        return pltpu.make_async_remote_copy(
            src_ref=edge_part(q),
            dst_ref=edge_ref.at[pl.ds(core * TOK, TOK)],
            send_sem=edge_send.at[q],
            recv_sem=edge_recv.at[core],
            device_id={"ctx": z * PLANE + q},
            device_id_type=MESH,
        )

    def edge_arrival(source):
        return pltpu.make_async_remote_copy(
            src_ref=edge_part(0),
            dst_ref=edge_ref.at[pl.ds(source * TOK, TOK)],
            send_sem=edge_send.at[0],
            recv_sem=edge_recv.at[source],
            device_id=in_plane(1),
            device_id_type=MESH,
        )

    def edge_own(q):
        return pltpu.make_async_copy(
            edge_part(q), edge_ref.at[pl.ds(core * TOK, TOK)], own_sem.at[CHUNKS]
        )

    sends_edge = (x == 3) & (z < PLANES - 1)
    for q in range(PLANE):

        @pl.when(sends_edge & (p != q))
        def _(q=q):
            edge_copy(q).start()

        @pl.when(sends_edge & (p == q))
        def _(q=q):
            edge_own(q).start()

    for r in range(1, 8):
        arrival1(r).wait_recv()
    rows = lax.broadcasted_iota(jnp.int32, (8, HD), 0)
    whole = jnp.zeros((8, HD), jnp.int32)
    for q in range(PLANE):
        whole = jnp.where(rows == q, line[q], whole)
    lists[z] = whole

    def copy2(r):
        return pltpu.make_async_remote_copy(
            src_ref=lists.at[z],
            dst_ref=lists.at[z],
            send_sem=send2.at[r],
            recv_sem=recv2.at[z],
            device_id=on_line(r),
            device_id_type=MESH,
        )

    def arrival2(r):
        q = (z + r) % PLANES
        return pltpu.make_async_remote_copy(
            src_ref=lists.at[q],
            dst_ref=lists.at[q],
            send_sem=send2.at[r],
            recv_sem=recv2.at[q],
            device_id=on_line(r),
            device_id_type=MESH,
        )

    for r in range(1, 8):
        copy2(r).start()
    for r in range(1, 8):
        arrival2(r).wait_recv()
    schedule(lists[...].reshape(PLANES * PLANE, HD).astype(F32), z, table_ref)

    for r in range(1, 8):
        copy1(r).wait_send()
        copy2(r).wait_send()
    for q in range(PLANE):

        @pl.when(sends_edge & (p != q))
        def _(q=q):
            edge_copy(q).wait_send()

        @pl.when(sends_edge & (p == q))
        def _(q=q):
            edge_own(q).wait()

    for source in range(2):

        @pl.when((z < PLANES - 1) & (p != 6 + source))
        def _(source=source):
            edge_arrival(source).wait_recv()

    for chunk in range(CHUNKS):
        pltpu.make_async_copy(
            part(0, chunk, mk_ref), pools[chunk].at[pl.ds(p * 8, 8)], own_sem.at[chunk]
        ).wait()
        for r in range(1, 8):
            copy_a(r, chunk, mk_ref).wait_send()
            arrival_a(r, chunk).wait_recv()


def spread(retrieval, mk, mv, k, v):
    return pl.pallas_call(
        spread_kernel,
        out_shape=[jax.ShapeDtypeStruct((LOCAL, ROWS, HD), BF16)] * CHUNKS
        + [
            jax.ShapeDtypeStruct((2 * TOK, HD), BF16),
            jax.ShapeDtypeStruct((2, 8, HD), jnp.int32),
        ],
        in_specs=[SMEM, HBM, HBM, HBM, HBM],
        out_specs=[pl.BlockSpec(memory_space=pl.ANY)] * (CHUNKS + 1) + [VMEM],
        scratch_shapes=[
            pltpu.VMEM((PLANE, 8, HD), jnp.int32),
            pltpu.VMEM((PLANES, 8, HD), jnp.int32),
            pltpu.SemaphoreType.DMA((8,)),
            pltpu.SemaphoreType.DMA((8,)),
            pltpu.SemaphoreType.DMA((8,)),
            pltpu.SemaphoreType.DMA((8,)),
            pltpu.SemaphoreType.DMA((CHUNKS, 8)),
            pltpu.SemaphoreType.DMA((CHUNKS, 8)),
            pltpu.SemaphoreType.DMA((CHUNKS + 1,)),
            pltpu.SemaphoreType.DMA((8,)),
            pltpu.SemaphoreType.DMA((2,)),
        ],
        compiler_params=pltpu.CompilerParams(
            collective_id=0, has_side_effects=True, vmem_limit_bytes=62 << 20
        ),
        name="spread_blocks",
    )(retrieval, mk, mv, k, v)


def attend_kernel(tier, *refs):
    caps, group, lags, left_out = tier
    slots = caps[-1]
    groups = slots // group
    table, gate_hbm, q_hbm, k_ref, v_ref, gain_hbm = refs[:6]
    rest = list(refs[6:])

    def take(n):
        got = rest[:n]
        del rest[:n]
        return got

    given = take(CHUNKS)
    (edge_ref,) = take(1)
    (out_ref,) = take(1)
    gate_ref, q_ref, gain_ref, near_k, near_v, mixed = take(6)
    pools, ups, downs = take(CHUNKS), take(CHUNKS), take(CHUNKS)
    ups_out, downs_out = take(CHUNKS), take(CHUNKS)
    parts_out, parts = take(CHUNKS), take(CHUNKS)
    squares_out, squares, edge_in = take(3)
    (
        pool_sem,
        own_sem,
        halo_send,
        halo_recv,
        up_send,
        up_recv,
        down_send,
        down_recv,
        part_send,
        part_recv,
        sq_send,
        sq_recv,
        edge_sem,
        pass_send,
        pass_recv,
    ) = rest

    me = lax.axis_index("ctx")
    mem = lax.axis_index("mem")
    z, p = me // PLANE, me % PLANE

    def in_plane(r):
        return {"ctx": z * PLANE + (p + r) % PLANE}

    def mem_peer(r):
        return {"mem": (mem + r) % 8}

    above, below = {"ctx": me + PLANE}, {"ctx": me - PLANE}
    loads = [
        pltpu.make_async_copy(given[c], pools[c], pool_sem.at[c]) for c in range(CHUNKS)
    ] + [
        pltpu.make_async_copy(k_ref, near_k.at[pl.ds(2 * TOK, TOK)], own_sem.at[0]),
        pltpu.make_async_copy(v_ref, near_v.at[pl.ds(2 * TOK, TOK)], own_sem.at[1]),
        pltpu.make_async_copy(q_hbm, q_ref, own_sem.at[2]),
        pltpu.make_async_copy(gate_hbm, gate_ref, own_sem.at[3]),
        pltpu.make_async_copy(gain_hbm, gain_ref, own_sem.at[4]),
    ]
    for load in loads:
        load.start()

    greet(
        [(in_plane(r), None) for r in range(1, 8)]
        + [(mem_peer(r), None) for r in range(1, 8)]
        + [(above, z < PLANES - 1), (below, z > 0)]
    )

    def edge_copy():
        return pltpu.make_async_remote_copy(
            src_ref=edge_ref,
            dst_ref=edge_in,
            send_sem=edge_sem.at[0],
            recv_sem=edge_sem.at[1],
            device_id=above,
            device_id_type=MESH,
        )

    @pl.when(z < PLANES - 1)
    def _():
        edge_copy().start()

    def passed(source, to):
        near = near_v if source % 2 else near_k
        columns = pl.ds(source // 2 * HD, HD)
        came = edge_in if to == 0 else edge_in.at[pl.ds(TOK, TOK)]
        return came, near.at[pl.ds(0, 2 * TOK if to == 0 else TOK), columns]

    def pass_copy(source, to):
        came, near = passed(source, to)
        return pltpu.make_async_remote_copy(
            src_ref=came,
            dst_ref=near,
            send_sem=pass_send.at[to],
            recv_sem=pass_recv.at[source],
            device_id={"ctx": z * PLANE + to},
            device_id_type=MESH,
        )

    def pass_own(source):
        came, near = passed(source, source)
        return pltpu.make_async_copy(came, near, pass_recv.at[source])

    def each_pass(source, remote, local):
        for to in range(2):
            if source == to:
                local(source)
            else:
                remote(source, to)

    def pass_on():
        edge_copy().wait_recv()
        for source in range(PLANE):

            @pl.when(p == source)
            def _(source=source):
                each_pass(
                    source,
                    lambda s, t: pass_copy(s, t).start(),
                    lambda s: pass_own(s).start(),
                )

    def halo(d, which):
        ref, near = ((k_ref, near_k), (v_ref, near_v))[which]
        return pltpu.make_async_remote_copy(
            src_ref=ref,
            dst_ref=near.at[pl.ds((2 - d) * TOK, TOK)],
            send_sem=halo_send.at[2 * d - 2 + which],
            recv_sem=halo_recv.at[2 * d - 2 + which],
            device_id={"ctx": me + d},
            device_id_type=MESH,
        )

    for d in (1, 2):

        @pl.when(p + d < PLANE)
        def _():
            halo(d, 0).start()
            halo(d, 1).start()

        @pl.when((z == 0) & (p < d))
        def _():
            near_k[pl.ds((2 - d) * TOK, TOK)] = jnp.zeros((TOK, HEADS_HERE * HD), BF16)
            near_v[pl.ds((2 - d) * TOK, TOK)] = jnp.zeros((TOK, HEADS_HERE * HD), BF16)

    for load in loads:
        load.wait()

    caps_g = [c // group for c in caps]

    def cap_at(step):
        value = jnp.int32(caps_g[3])
        for i in (2, 1, 0):
            value = jnp.where(step == i, caps_g[i], value)
        return value

    def floor_at(step):
        return jnp.where(step >= PLANES - 2, left_out // group, 0)

    def lag_at(step):
        value = jnp.int32(0)
        for i in range(4):
            value = jnp.where(step == 4 + i, lags[i], value)
        return value

    def conveyor(k, step, target, pool, into, onward, send, recv, row):
        cap = cap_at(step)
        position = jnp.where(step <= 3, k + groups - cap, k - lag_at(step))
        inside = (position >= 0) & (position < CHUNKS * groups)
        at = jnp.maximum(position, 0)
        chunk = at // groups
        g = groups - 1 - at % groups
        active = inside & (g < cap)
        incoming = (step > 0) & (g < cap_at(step - 1)) & (g >= floor_at(step - 1))

        def copy(c):
            span = pl.ds(g * group, group)
            return pltpu.make_async_remote_copy(
                src_ref=onward[c].at[span],
                dst_ref=into[c].at[span],
                send_sem=send.at[c, g],
                recv_sem=recv.at[c, g],
                device_id=target,
                device_id_type=MESH,
            )

        for c in range(CHUNKS):

            @pl.when(active & (chunk == c))
            def _(c=c):
                @pl.when(incoming)
                def _():
                    copy(c).wait_recv()

                @pl.when((step < PLANES - 1) & (g >= floor_at(step)))
                def _():
                    for i in range(group):
                        slot = g * group + i
                        inject = table[1, row + slot // HD, slot % HD]
                        local = pool[c][jnp.maximum(inject, 0)]
                        onward[c][slot] = jnp.where(inject >= 0, local, into[c][slot])
                    copy(c).start()

    def part_copy(c, r):
        q = (p + r) % PLANE
        return pltpu.make_async_remote_copy(
            src_ref=parts_out[c].at[q],
            dst_ref=parts[c].at[p],
            send_sem=part_send.at[c, r],
            recv_sem=part_recv.at[c, p],
            device_id=in_plane(r),
            device_id_type=MESH,
        )

    def part_arrival(c, r):
        q = (p + r) % PLANE
        return pltpu.make_async_remote_copy(
            src_ref=parts_out[c].at[q],
            dst_ref=parts[c].at[q],
            send_sem=part_send.at[c, r],
            recv_sem=part_recv.at[c, q],
            device_id=in_plane(r),
            device_id_type=MESH,
        )

    def hand_out(c):
        def pick(q, j):
            place = table[0, q, j]
            own = pools[c][jnp.minimum(place, LOCAL - 1)]
            from_below = ups[c][jnp.clip(place - LOCAL, 0, slots - 1)]
            from_above = downs[c][jnp.clip(place - LOCAL - SLOTS, 0, slots - 1)]
            return jnp.where(
                place < LOCAL, own, jnp.where(place < LOCAL + SLOTS, from_below, from_above)
            )

        for r in (4, 3, 5, 2, 6, 1, 7):
            q = (p + r) % PLANE
            for j in range(REQ):
                parts_out[c][q, j] = pick(q, j)
            part_copy(c, r).start()
        for j in range(REQ):
            parts[c][p, j] = pick(p, j)

    def window_piece(head, tile):
        columns = pl.ds(pl.multiple_of(head * HD, HD), HD)
        rows = pl.ds(pl.multiple_of(tile * 128, 128), 128)
        near = pl.ds(pl.multiple_of(tile * 128, 128), 640)
        scores = lax.dot_general(
            q_ref[rows, columns],
            near_k[near, columns],
            (((1,), (1,)), ((), ())),
            preferred_element_type=F32,
        )
        key = lax.broadcasted_iota(jnp.int32, (128, 640), 1)
        ahead = key - lax.broadcasted_iota(jnp.int32, (128, 640), 0)
        first = me * TOK - 2 * TOK + tile * 128
        allowed = (ahead > 0) & (ahead <= 512) & (key >= -first)
        scores = jnp.where(allowed, scores * SCALE, -jnp.inf)
        weights = jnp.exp(scores - jnp.max(scores, axis=1, keepdims=True))
        total = jnp.sum(weights, axis=1, keepdims=True)
        product = jnp.dot(weights.astype(BF16), near_v[near, columns], preferred_element_type=F32)
        mixed[rows, columns] = product / total

    steps = CHUNKS * groups + max(lags[2], lags[3] - left_out // group)
    far = jnp.maximum(z, PLANES - 1 - z)
    far = lag_at(far) - floor_at(far - 1)
    pieces = 2 * HEADS_HERE
    every = max(1, (steps - 12) // (pieces + 2))
    pass_step = 5
    first_piece = steps - 4 - every * pieces

    def step_body(k, carry):
        conveyor(k, z, above, pools, ups, ups_out, up_send, up_recv, 0)
        conveyor(k, PLANES - 1 - z, below, pools, downs, downs_out, down_send, down_recv, 2)
        for c in range(CHUNKS):

            @pl.when(k == (c + 1) * groups - 1 + far)
            def _(c=c):
                hand_out(c)

        @pl.when((k == pass_step) & (z > 0))
        def _():
            pass_on()

        @pl.when(k == first_piece)
        def _():
            for d in (1, 2):

                @pl.when(p >= d)
                def _():
                    halo(d, 0).wait_recv()
                    halo(d, 1).wait_recv()

            for to in range(2):

                @pl.when((z > 0) & (p == to))
                def _(to=to):
                    for source in range(PLANE):
                        if source == to:
                            pass_own(source).wait()
                        else:
                            pass_copy(source, to).wait_recv()

        since = k - first_piece
        piece = jnp.maximum(since, 0) // every

        @pl.when((since >= 0) & (since % every == 0) & (piece < pieces))
        def _():
            window_piece(piece // 2, piece % 2)

        return carry

    lax.fori_loop(0, steps, step_body, 0)

    for c in range(CHUNKS):
        for r in range(1, 8):
            part_arrival(c, r).wait_recv()

    opened = 1.0 / (1.0 + jnp.exp(-gate_ref[...]))
    eye = lax.broadcasted_iota(jnp.int32, (128, 128), 0) == lax.broadcasted_iota(
        jnp.int32, (128, 128), 1
    )
    for tile in range(2):
        rows = pl.ds(tile * 128, 128)
        total_square = jnp.zeros((128, 1), F32)
        for head in range(HEADS_HERE):
            columns = pl.ds(head * HD, HD)
            keys = [parts[c][2 * head, 4 * tile : 4 * tile + 4].reshape(4 * ROWS, HD) for c in range(CHUNKS)]
            vals = [parts[c][2 * head + 1, 4 * tile : 4 * tile + 4].reshape(4 * ROWS, HD) for c in range(CHUNKS)]
            scores = lax.dot_general(
                q_ref[rows, columns],
                jnp.concatenate(keys, axis=0),
                (((1,), (1,)), ((), ())),
                preferred_element_type=F32,
            ) * SCALE
            weights = jnp.exp(scores - jnp.max(scores, axis=1, keepdims=True))
            total = jnp.sum(weights, axis=1, keepdims=True)
            product = jnp.dot(
                weights.astype(BF16), jnp.concatenate(vals, axis=0), preferred_element_type=F32
            )
            share = opened[:, head : head + 1]
            both = share * (product / total) + (1.0 - share) * mixed[rows, columns]
            mixed[rows, columns] = both
            total_square += jnp.sum(both * both, axis=1, keepdims=True)
        squares_out[pl.ds(tile * 8, 8)] = jnp.broadcast_to(
            jnp.sum(jnp.where(eye, total_square, 0.0), axis=0, keepdims=True), (8, 128)
        )

    def square_copy(r):
        return pltpu.make_async_remote_copy(
            src_ref=squares_out,
            dst_ref=squares.at[mem],
            send_sem=sq_send.at[r],
            recv_sem=sq_recv.at[mem],
            device_id=mem_peer(r),
            device_id_type=MESH,
        )

    def square_arrival(r):
        return pltpu.make_async_remote_copy(
            src_ref=squares_out,
            dst_ref=squares.at[(mem + r) % 8],
            send_sem=sq_send.at[r],
            recv_sem=sq_recv.at[(mem + r) % 8],
            device_id=mem_peer(r),
            device_id_type=MESH,
        )

    for r in (4, 1, 2, 3, 5, 6, 7):
        square_copy(r).start()
    squares[mem] = squares_out[...]
    for r in range(1, 8):
        square_arrival(r).wait_recv()
    summed = squares[0]
    for m in range(1, 8):
        summed = summed + squares[m]
    for tile in range(2):
        rows = pl.ds(tile * 128, 128)
        column = jnp.sum(
            jnp.where(eye, summed[tile * 8 : tile * 8 + 1], 0.0), axis=1, keepdims=True
        )
        factor = lax.rsqrt(column / FEATURES + 1e-6)
        out_ref[rows] = (mixed[rows] * gain_ref[...] * factor).astype(BF16)

    for r in range(1, 8):
        square_copy(r).wait_send()
        for c in range(CHUNKS):
            part_copy(c, r).wait_send()
    for d in (1, 2):

        @pl.when(p + d < PLANE)
        def _():
            halo(d, 0).wait_send()
            halo(d, 1).wait_send()

    @pl.when(z < PLANES - 1)
    def _():
        edge_copy().wait_send()

    for source in range(PLANE):

        @pl.when((z > 0) & (p == source))
        def _(source=source):
            each_pass(source, lambda s, t: pass_copy(s, t).wait_send(), lambda s: None)

    for step, into, onward, send, recv, target in (
        (z, ups, ups_out, up_send, up_recv, above),
        (PLANES - 1 - z, downs, downs_out, down_send, down_recv, below),
    ):

        @pl.when(step < PLANES - 1)
        def _():
            def sent(g, carry):
                span = pl.ds(g * group, group)
                for c in range(CHUNKS):
                    pltpu.make_async_remote_copy(
                        src_ref=onward[c].at[span],
                        dst_ref=into[c].at[span],
                        send_sem=send.at[c, g],
                        recv_sem=recv.at[c, g],
                        device_id=target,
                        device_id_type=MESH,
                    ).wait_send()
                return carry

            lax.fori_loop(floor_at(step), cap_at(step), sent, 0)


def attend(tier, collective_id, table, gate, q, k, v, gain, *pools):
    slots = tier[0][-1]
    groups = slots // tier[1]
    ring = [pltpu.VMEM((slots, ROWS, HD), BF16)] * CHUNKS
    hand = [pltpu.VMEM((PLANE, REQ, ROWS, HD), BF16)] * CHUNKS
    dma = pltpu.SemaphoreType.DMA
    return pl.pallas_call(
        functools.partial(attend_kernel, tier),
        out_shape=jax.ShapeDtypeStruct((TOK, HEADS_HERE * HD), BF16),
        in_specs=[SMEM, HBM, HBM, HBM, HBM, HBM] + [pl.BlockSpec(memory_space=pl.ANY)] * (CHUNKS + 1),
        out_specs=VMEM,
        scratch_shapes=[
            pltpu.VMEM((1, HEADS_HERE), F32),
            pltpu.VMEM((TOK, HEADS_HERE * HD), BF16),
            pltpu.VMEM((1, HEADS_HERE * HD), F32),
            pltpu.VMEM((3 * TOK, HEADS_HERE * HD), BF16),
            pltpu.VMEM((3 * TOK, HEADS_HERE * HD), BF16),
            pltpu.VMEM((TOK, HEADS_HERE * HD), F32),
            *[pltpu.VMEM((LOCAL, ROWS, HD), BF16)] * CHUNKS,
            *ring,
            *ring,
            *ring,
            *ring,
            *hand,
            *hand,
            pltpu.VMEM((16, HD), F32),
            pltpu.VMEM((8, 16, HD), F32),
            pltpu.VMEM((2 * TOK, HD), BF16),
            dma((CHUNKS,)),
            dma((5,)),
            dma((4,)),
            dma((4,)),
            dma((CHUNKS, groups)),
            dma((CHUNKS, groups)),
            dma((CHUNKS, groups)),
            dma((CHUNKS, groups)),
            dma((CHUNKS, 8)),
            dma((CHUNKS, 8)),
            dma((8,)),
            dma((8,)),
            dma((2,)),
            dma((2,)),
            dma((8,)),
        ],
        compiler_params=pltpu.CompilerParams(
            collective_id=collective_id, has_side_effects=True, vmem_limit_bytes=60 << 20
        ),
        name="attend_" + str(slots),
    )(table, gate, q, k, v, gain, *pools)


def shards(queries, keys, values, memory_keys, memory_values, retrieval, gate, gain):
    *pools, edge, table = spread(retrieval, memory_keys, memory_values, keys, values)
    operands = (
        table,
        gate.reshape(1, -1),
        queries,
        keys,
        values,
        gain.reshape(1, -1),
        *pools,
        edge,
    )
    return lax.switch(
        table[1, 4, 0],
        [functools.partial(attend, tier, 1 + i) for i, tier in enumerate(TIERS)],
        *operands,
    )


def solution(mesh):
    in_specs = (
        P("ctx", "mem"),
        P("ctx", "mem"),
        P("ctx", "mem"),
        P("ctx", None, "mem"),
        P("ctx", None, "mem"),
        P("ctx", None),
        P("mem"),
        P("mem"),
    )
    return jax.shard_map(
        shards, mesh=mesh, in_specs=in_specs, out_specs=P("ctx", "mem"), check_vma=False
    )
```

```python
import functools
import math

import jax
import jax.numpy as jnp
from jax import lax
from jax.experimental import pallas as pl
from jax.experimental.pallas import tpu as pltpu
from jax.sharding import PartitionSpec as P

MESH = pl.DeviceIdType.MESH
HBM = pl.BlockSpec(memory_space=pltpu.HBM)
VMEM = pl.BlockSpec(memory_space=pltpu.VMEM)
SMEM = pl.BlockSpec(memory_space=pltpu.SMEM)
F32 = jnp.float32
BF16 = jnp.bfloat16

HD = 128
HEADS_HERE = 4
FEATURES = 4096
PLANES = 8
PLANE = 8
REQ = 8
BLK = 64
LOCAL = 64
TOK = 256
CHUNKS = 2
ROWS = BLK // CHUNKS
SCALE = 1.0 / math.sqrt(HD)

SHORT = ((56, 88, 104, 112), 8, (3, 7, 10, 11), 16, 128)
LONG = ((64, 128, 192, 256), 16, (2, 4, 6, 8), 0, 256)
REACHES = (7, 1, 2, 3, 4, 5, 6)


def iota(shape, dim):
    return lax.broadcasted_iota(jnp.int32, shape, dim).astype(F32)


def greet(peers):
    barrier = pltpu.get_barrier_semaphore()
    total = 0
    for device, present in peers:
        if present is None:
            pl.semaphore_signal(barrier, inc=1, device_id=device, device_id_type=MESH)
            total = total + 1
        else:

            @pl.when(present)
            def _(device=device):
                pl.semaphore_signal(barrier, inc=1, device_id=device, device_id_type=MESH)

            total = total + present.astype(jnp.int32)
    pl.semaphore_wait(barrier, total)


def schedule(tier, lists, my_z, table_ref):
    caps, _, _, left_out, known = tier
    block = iota((1, PLANES * LOCAL), 1)
    asker_z = jnp.floor(iota((PLANES * PLANE, 1), 0) / PLANE)
    top = jnp.full((1, PLANES * LOCAL), -1.0, F32)
    low = jnp.full((1, PLANES * LOCAL), 8.0, F32)
    for j in range(REQ):
        hit = lists[:, j : j + 1] == block
        top = jnp.maximum(top, jnp.max(jnp.where(hit, asker_z, -1.0), axis=0, keepdims=True))
        low = jnp.minimum(low, jnp.min(jnp.where(hit, asker_z, 8.0), axis=0, keepdims=True))
    before_lane = (iota((LOCAL, LOCAL), 0) < iota((LOCAL, LOCAL), 1)).astype(BF16)
    after_row = (iota((known, known), 1) > iota((known, known), 0)).astype(BF16)
    before_kind = (iota((8, 8), 1) < iota((8, 8), 0)).astype(BF16)
    slot_column = iota((known, 1), 0)
    kind = jnp.full((8, 1), -1.0, F32)
    for i, reach in enumerate(REACHES):
        kind = jnp.where(iota((8, 1), 0) == i, reach, kind)
    lane = iota((1, LOCAL), 1)
    fits = jnp.ones((1, 1), F32)
    injected, arrived = [], []
    for up in (True, False):
        height = jnp.zeros((1, 1), F32)
        end = jnp.full((known, 1), -1.0, F32)
        held = jnp.full((known, 1), -1.0, F32)
        mine_in = jnp.full((known, 1), -1.0, F32)
        mine_arrived = jnp.full((known, 1), -1.0, F32)
        for step in range(PLANES - 1):
            z = step if up else PLANES - 1 - step
            reach = top[:, z * LOCAL : (z + 1) * LOCAL]
            if not up:
                reach = (PLANES - 1) - low[:, z * LOCAL : (z + 1) * LOCAL]
            fresh = (reach > step).astype(F32)
            kinds = (reach == kind).astype(F32) * fresh
            of_kind = jnp.dot(kinds.astype(BF16), before_lane, preferred_element_type=F32)
            earlier = jnp.dot(
                before_kind,
                jnp.broadcast_to(jnp.sum(kinds, axis=1, keepdims=True), (8, HD)).astype(BF16),
                preferred_element_type=F32,
            )[:, 0:1]
            fresh_rank = jnp.sum(kinds * (of_kind + earlier), axis=0, keepdims=True)
            load = jnp.sum((end > step).astype(F32), axis=0, keepdims=True) + jnp.sum(
                fresh, axis=1, keepdims=True
            )
            height = jnp.maximum(height, load)
            free = ((end <= step) & (slot_column < height)).astype(F32)
            free_rank = jnp.dot(
                after_row, jnp.broadcast_to(free, (known, HD)).astype(BF16), preferred_element_type=F32
            )[:, 0:1]
            pair = (free_rank == fresh_rank) & (free > 0.5) & (fresh > 0.5)
            code = jnp.sum(jnp.where(pair, 1.0 + lane + LOCAL * reach, 0.0), axis=1, keepdims=True)
            taken = code > 0.5
            new_end = jnp.floor((code - 1.0) / LOCAL)
            new_block = code - 1.0 - LOCAL * new_end
            inject = jnp.where(taken, new_block, -1.0)
            held = jnp.where(taken, z * LOCAL + new_block, jnp.where(end <= step, -1.0, held))
            end = jnp.where(taken, new_end, end)
            fits = fits * (load <= caps[min(step, 3)]).astype(F32)
            if step == PLANES - 2:
                lowest = jnp.min(
                    jnp.where(end > step, slot_column, known), axis=0, keepdims=True
                )
                fits = fits * (lowest >= left_out).astype(F32)
            mine_in = jnp.where(my_z == z, inject, mine_in)
            mine_arrived = jnp.where(my_z == (z + 1 if up else z - 1), held, mine_arrived)
        injected.append(mine_in)
        arrived.append(mine_arrived)
    diagonal = iota((known, known), 0) == iota((known, known), 1)

    def as_row(column):
        return jnp.sum(jnp.where(diagonal, column, 0.0), axis=0, keepdims=True)

    in_up, in_down = as_row(injected[0]), as_row(injected[1])
    at_up, at_down = as_row(arrived[0]), as_row(arrived[1])
    rows = iota((8, HD), 0)
    out = jnp.where(rows == 4, fits, 0.0)
    for i in range(known // HD):
        out = jnp.where(rows == i, in_up[:, i * HD : (i + 1) * HD], out)
        out = jnp.where(rows == 2 + i, in_down[:, i * HD : (i + 1) * HD], out)
    table_ref[1] = out.astype(jnp.int32)

    slot = iota((1, known), 1)
    mine = jnp.zeros((PLANE, HD), F32)
    for z in range(PLANES):
        mine = jnp.where(my_z == z, lists[z * PLANE : (z + 1) * PLANE], mine)
    place = jnp.zeros((PLANE, HD), F32)
    lanes = iota((PLANE, HD), 1)
    z_here = my_z.astype(F32)
    for j in range(REQ):
        wanted = mine[:, j : j + 1]
        owner_z = jnp.floor(wanted / LOCAL)
        slot_up = jnp.sum(jnp.where(at_up == wanted, slot, 0.0), axis=1, keepdims=True)
        slot_down = jnp.sum(jnp.where(at_down == wanted, slot, 0.0), axis=1, keepdims=True)
        found = jnp.where(owner_z == z_here, wanted - LOCAL * owner_z, LOCAL + known + slot_down)
        found = jnp.where(owner_z < z_here, LOCAL + slot_up, found)
        place = jnp.where(lanes == j, found, place)
    table_ref[0] = place.astype(jnp.int32)


def attend_kernel(tier, *refs):
    caps, group, lags, left_out, known = tier
    slots = caps[-1]
    groups = slots // group
    ids_ref, gate_hbm, gain_hbm, q_hbm, k_ref, v_ref, mk_ref, mv_ref = refs[:8]
    out_ref, fits_ref = refs[8:10]
    rest = list(refs[10:])

    def take(n):
        got = rest[:n]
        del rest[:n]
        return got

    table_out, table, line, lists = take(4)
    gate_ref, q_ref, gain_ref, near_k, near_v, mixed = take(6)
    pools, ups, downs = take(CHUNKS), take(CHUNKS), take(CHUNKS)
    ups_out, downs_out = take(CHUNKS), take(CHUNKS)
    parts_out, parts = take(CHUNKS), take(CHUNKS)
    squares_out, squares, edge_ref, edge_in = take(4)
    table_sem, send1, recv1, send2, recv2, send_a, recv_a, edge_send, edge_recv = take(9)
    (
        pool_sem,
        own_sem,
        halo_send,
        halo_recv,
        up_send,
        up_recv,
        down_send,
        down_recv,
        part_send,
        part_recv,
        sq_send,
        sq_recv,
        edge_sem,
        pass_send,
        pass_recv,
    ) = rest

    me = lax.axis_index("ctx")
    mem = lax.axis_index("mem")
    z, p = me // PLANE, me % PLANE
    x, core = p // 2, p % 2

    def in_plane(r):
        return {"ctx": z * PLANE + (p + r) % PLANE}

    def on_line(r):
        return {"ctx": ((z + r) % PLANES) * PLANE + p}

    def mem_peer(r):
        return {"mem": (mem + r) % 8}

    above, below = {"ctx": me + PLANE}, {"ctx": me - PLANE}
    loads = [
        pltpu.make_async_copy(k_ref, near_k.at[pl.ds(2 * TOK, TOK)], own_sem.at[0]),
        pltpu.make_async_copy(v_ref, near_v.at[pl.ds(2 * TOK, TOK)], own_sem.at[1]),
        pltpu.make_async_copy(q_hbm, q_ref, own_sem.at[2]),
        pltpu.make_async_copy(gate_hbm, gate_ref, own_sem.at[3]),
        pltpu.make_async_copy(gain_hbm, gain_ref, own_sem.at[4]),
    ]
    for load in loads:
        load.start()

    greet(
        [(in_plane(r), None) for r in range(1, 8)]
        + [(mem_peer(r), None) for r in range(1, 8)]
        + [(on_line(r), None) for r in range(1, 8)]
    )

    def edge_copy():
        return pltpu.make_async_remote_copy(
            src_ref=edge_ref,
            dst_ref=edge_in,
            send_sem=edge_sem.at[0],
            recv_sem=edge_sem.at[1],
            device_id=above,
            device_id_type=MESH,
        )

    def edge_here():
        for source in range(2):

            @pl.when((z < PLANES - 1) & (p == 6 + source))
            def _(source=source):
                edge_own(0).wait()

            @pl.when((z < PLANES - 1) & (p != 6 + source))
            def _(source=source):
                edge_arrival(source).wait_recv()

        @pl.when(z < PLANES - 1)
        def _():
            edge_copy().start()

    def passed(source, to):
        near = near_v if source % 2 else near_k
        columns = pl.ds(source // 2 * HD, HD)
        came = edge_in if to == 0 else edge_in.at[pl.ds(TOK, TOK)]
        return came, near.at[pl.ds(0, 2 * TOK if to == 0 else TOK), columns]

    def pass_copy(source, to):
        came, near = passed(source, to)
        return pltpu.make_async_remote_copy(
            src_ref=came,
            dst_ref=near,
            send_sem=pass_send.at[to],
            recv_sem=pass_recv.at[source],
            device_id={"ctx": z * PLANE + to},
            device_id_type=MESH,
        )

    def pass_own(source):
        came, near = passed(source, source)
        return pltpu.make_async_copy(came, near, pass_recv.at[source])

    def each_pass(source, remote, local):
        for to in range(2):
            if source == to:
                local(source)
            else:
                remote(source, to)

    def pass_on():
        edge_copy().wait_recv()
        for source in range(PLANE):

            @pl.when(p == source)
            def _(source=source):
                each_pass(
                    source,
                    lambda s, t: pass_copy(s, t).start(),
                    lambda s: pass_own(s).start(),
                )

    lanes = lax.broadcasted_iota(jnp.int32, (8, HD), 1)
    row = jnp.zeros((8, HD), jnp.int32)
    for j in range(REQ):
        row = jnp.where(lanes == j, ids_ref[j // 4, j % 4], row)
    line[p] = row

    def copy1(r):
        return pltpu.make_async_remote_copy(
            src_ref=line.at[p],
            dst_ref=line.at[p],
            send_sem=send1.at[r],
            recv_sem=recv1.at[p],
            device_id=in_plane(r),
            device_id_type=MESH,
        )

    def arrival1(r):
        q = (p + r) % PLANE
        return pltpu.make_async_remote_copy(
            src_ref=line.at[q],
            dst_ref=line.at[q],
            send_sem=send1.at[r],
            recv_sem=recv1.at[q],
            device_id=in_plane(r),
            device_id_type=MESH,
        )

    for r in range(1, 8):
        copy1(r).start()

    def part(r, chunk, ref):
        q = (p + r) % PLANE
        return ref.at[:, pl.ds(chunk * ROWS, ROWS), pl.ds(pl.multiple_of((q // 2) * HD, HD), HD)]

    def copy_a(r, chunk, ref):
        return pltpu.make_async_remote_copy(
            src_ref=part(r, chunk, ref),
            dst_ref=pools[chunk].at[pl.ds(p * 8, 8)],
            send_sem=send_a.at[chunk, r],
            recv_sem=recv_a.at[chunk, p],
            device_id=in_plane(r),
            device_id_type=MESH,
        )

    def arrival_a(r, chunk):
        q = (p + r) % PLANE
        return pltpu.make_async_remote_copy(
            src_ref=part(r, chunk, mk_ref),
            dst_ref=pools[chunk].at[pl.ds(q * 8, 8)],
            send_sem=send_a.at[chunk, r],
            recv_sem=recv_a.at[chunk, q],
            device_id=in_plane(r),
            device_id_type=MESH,
        )

    def own_a(ref, chunk):
        return pltpu.make_async_copy(
            part(0, chunk, ref), pools[chunk].at[pl.ds(p * 8, 8)], pool_sem.at[chunk]
        )

    def spread_blocks(chunk):
        for r in (4, 3, 5, 2, 6, 1, 7):
            to_core = (core + r) % 2

            @pl.when(to_core == 0)
            def _():
                copy_a(r, chunk, mk_ref).start()

            @pl.when(to_core == 1)
            def _():
                copy_a(r, chunk, mv_ref).start()

        @pl.when(core == 0)
        def _():
            own_a(mk_ref, chunk).start()

        @pl.when(core == 1)
        def _():
            own_a(mv_ref, chunk).start()

    def blocks_here(chunk):
        own_a(mk_ref, chunk).wait()
        for r in range(1, 8):
            arrival_a(r, chunk).wait_recv()

    spread_blocks(0)

    def edge_part(q):
        ref = v_ref if q % 2 else k_ref
        return ref.at[:, pl.ds(q // 2 * HD, HD)]

    def spread_edge(q):
        return pltpu.make_async_remote_copy(
            src_ref=edge_part(q),
            dst_ref=edge_ref.at[pl.ds(core * TOK, TOK)],
            send_sem=edge_send.at[q],
            recv_sem=edge_recv.at[core],
            device_id={"ctx": z * PLANE + q},
            device_id_type=MESH,
        )

    def edge_arrival(source):
        return pltpu.make_async_remote_copy(
            src_ref=edge_part(0),
            dst_ref=edge_ref.at[pl.ds(source * TOK, TOK)],
            send_sem=edge_send.at[0],
            recv_sem=edge_recv.at[source],
            device_id=in_plane(1),
            device_id_type=MESH,
        )

    def edge_own(q):
        return pltpu.make_async_copy(
            edge_part(q), edge_ref.at[pl.ds(core * TOK, TOK)], pool_sem.at[CHUNKS]
        )

    sends_edge = (x == 3) & (z < PLANES - 1)
    for q in range(PLANE):

        @pl.when(sends_edge & (p != q))
        def _(q=q):
            spread_edge(q).start()

        @pl.when(sends_edge & (p == q))
        def _(q=q):
            edge_own(q).start()

    for chunk in range(1, CHUNKS):
        spread_blocks(chunk)
    def halo(d, which):
        ref, near = ((k_ref, near_k), (v_ref, near_v))[which]
        return pltpu.make_async_remote_copy(
            src_ref=ref,
            dst_ref=near.at[pl.ds((2 - d) * TOK, TOK)],
            send_sem=halo_send.at[2 * d - 2 + which],
            recv_sem=halo_recv.at[2 * d - 2 + which],
            device_id={"ctx": me + d},
            device_id_type=MESH,
        )

    for d in (1, 2):

        @pl.when(p + d < PLANE)
        def _():
            halo(d, 0).start()
            halo(d, 1).start()

        @pl.when((z == 0) & (p < d))
        def _():
            near_k[pl.ds((2 - d) * TOK, TOK)] = jnp.zeros((TOK, HEADS_HERE * HD), BF16)
            near_v[pl.ds((2 - d) * TOK, TOK)] = jnp.zeros((TOK, HEADS_HERE * HD), BF16)

    for r in range(1, 8):
        arrival1(r).wait_recv()
    rows = lax.broadcasted_iota(jnp.int32, (8, HD), 0)
    whole = jnp.zeros((8, HD), jnp.int32)
    for q in range(PLANE):
        whole = jnp.where(rows == q, line[q], whole)
    lists[z] = whole

    def copy2(r):
        return pltpu.make_async_remote_copy(
            src_ref=lists.at[z],
            dst_ref=lists.at[z],
            send_sem=send2.at[r],
            recv_sem=recv2.at[z],
            device_id=on_line(r),
            device_id_type=MESH,
        )

    def arrival2(r):
        q = (z + r) % PLANES
        return pltpu.make_async_remote_copy(
            src_ref=lists.at[q],
            dst_ref=lists.at[q],
            send_sem=send2.at[r],
            recv_sem=recv2.at[q],
            device_id=on_line(r),
            device_id_type=MESH,
        )

    for r in range(1, 8):
        copy2(r).start()
    for r in range(1, 8):
        arrival2(r).wait_recv()
    schedule(tier, lists[...].reshape(PLANES * PLANE, HD).astype(F32), z, table_out)
    to_scalars = pltpu.make_async_copy(table_out, table, table_sem)
    to_scalars.start()
    to_scalars.wait()
    fits_ref[0] = table[1, 4, 0]
    edge_here()
    for load in loads:
        load.wait()
    blocks_here(0)

    caps_g = [c // group for c in caps]

    def cap_at(step):
        value = jnp.int32(caps_g[3])
        for i in (2, 1, 0):
            value = jnp.where(step == i, caps_g[i], value)
        return value

    def floor_at(step):
        return jnp.where(step >= PLANES - 2, left_out // group, 0)

    def lag_at(step):
        value = jnp.int32(0)
        for i in range(4):
            value = jnp.where(step == 4 + i, lags[i], value)
        return value

    def conveyor(k, step, target, pool, into, onward, send, recv, row):
        cap = cap_at(step)
        position = jnp.where(step <= 3, k + groups - cap, k - lag_at(step))
        inside = (position >= 0) & (position < CHUNKS * groups)
        at = jnp.maximum(position, 0)
        chunk = at // groups
        g = groups - 1 - at % groups
        active = inside & (g < cap)
        incoming = (step > 0) & (g < cap_at(step - 1)) & (g >= floor_at(step - 1))

        def copy(c):
            span = pl.ds(g * group, group)
            return pltpu.make_async_remote_copy(
                src_ref=onward[c].at[span],
                dst_ref=into[c].at[span],
                send_sem=send.at[c, g],
                recv_sem=recv.at[c, g],
                device_id=target,
                device_id_type=MESH,
            )

        for c in range(CHUNKS):

            @pl.when(active & (chunk == c))
            def _(c=c):
                @pl.when(incoming)
                def _():
                    copy(c).wait_recv()

                @pl.when((step < PLANES - 1) & (g >= floor_at(step)))
                def _():
                    for i in range(group):
                        slot = g * group + i
                        inject = table[1, row + slot // HD, slot % HD]
                        local = pool[c][jnp.clip(inject, 0, LOCAL - 1)]
                        onward[c][slot] = jnp.where(inject >= 0, local, into[c][slot])
                    copy(c).start()

    def part_copy(c, r):
        q = (p + r) % PLANE
        return pltpu.make_async_remote_copy(
            src_ref=parts_out[c].at[q],
            dst_ref=parts[c].at[p],
            send_sem=part_send.at[c, r],
            recv_sem=part_recv.at[c, p],
            device_id=in_plane(r),
            device_id_type=MESH,
        )

    def part_arrival(c, r):
        q = (p + r) % PLANE
        return pltpu.make_async_remote_copy(
            src_ref=parts_out[c].at[q],
            dst_ref=parts[c].at[q],
            send_sem=part_send.at[c, r],
            recv_sem=part_recv.at[c, q],
            device_id=in_plane(r),
            device_id_type=MESH,
        )

    def hand_out(c):
        def pick(q, j):
            place = table[0, q, j]
            own = pools[c][jnp.clip(place, 0, LOCAL - 1)]
            from_below = ups[c][jnp.clip(place - LOCAL, 0, slots - 1)]
            from_above = downs[c][jnp.clip(place - LOCAL - known, 0, slots - 1)]
            return jnp.where(
                place < LOCAL, own, jnp.where(place < LOCAL + known, from_below, from_above)
            )

        for r in (4, 3, 5, 2, 6, 1, 7):
            q = (p + r) % PLANE
            for j in range(REQ):
                parts_out[c][q, j] = pick(q, j)
            part_copy(c, r).start()
        for j in range(REQ):
            parts[c][p, j] = pick(p, j)

    def window_piece(head, tile):
        columns = pl.ds(pl.multiple_of(head * HD, HD), HD)
        rows = pl.ds(pl.multiple_of(tile * 128, 128), 128)
        near = pl.ds(pl.multiple_of(tile * 128, 128), 640)
        scores = lax.dot_general(
            q_ref[rows, columns],
            near_k[near, columns],
            (((1,), (1,)), ((), ())),
            preferred_element_type=F32,
        )
        key = lax.broadcasted_iota(jnp.int32, (128, 640), 1)
        ahead = key - lax.broadcasted_iota(jnp.int32, (128, 640), 0)
        first = me * TOK - 2 * TOK + tile * 128
        allowed = (ahead > 0) & (ahead <= 512) & (key >= -first)
        scores = jnp.where(allowed, scores * SCALE, -jnp.inf)
        weights = jnp.exp(scores - jnp.max(scores, axis=1, keepdims=True))
        total = jnp.sum(weights, axis=1, keepdims=True)
        product = jnp.dot(weights.astype(BF16), near_v[near, columns], preferred_element_type=F32)
        mixed[rows, columns] = product / total

    steps = CHUNKS * groups + max(lags[2], lags[3] - left_out // group)
    far = jnp.maximum(z, PLANES - 1 - z)
    far = lag_at(far) - floor_at(far - 1)
    pieces = 2 * HEADS_HERE
    every = max(1, (steps - 12) // (pieces + 2))
    pass_step = 5
    first_piece = steps - 4 - every * pieces

    def step_body(k, carry):
        for chunk in range(1, CHUNKS):

            @pl.when(k == (chunk - 1) * groups + caps_g[0])
            def _(chunk=chunk):
                blocks_here(chunk)

        conveyor(k, z, above, pools, ups, ups_out, up_send, up_recv, 0)
        conveyor(k, PLANES - 1 - z, below, pools, downs, downs_out, down_send, down_recv, 2)
        for c in range(CHUNKS):

            @pl.when(k == (c + 1) * groups - 1 + far)
            def _(c=c):
                hand_out(c)

        @pl.when((k == pass_step) & (z > 0))
        def _():
            pass_on()

        @pl.when(k == first_piece)
        def _():
            for d in (1, 2):

                @pl.when(p >= d)
                def _():
                    halo(d, 0).wait_recv()
                    halo(d, 1).wait_recv()

            for to in range(2):

                @pl.when((z > 0) & (p == to))
                def _(to=to):
                    for source in range(PLANE):
                        if source == to:
                            pass_own(source).wait()
                        else:
                            pass_copy(source, to).wait_recv()

        since = k - first_piece
        piece = jnp.maximum(since, 0) // every

        @pl.when((since >= 0) & (since % every == 0) & (piece < pieces))
        def _():
            window_piece(piece // 2, piece % 2)

        return carry

    lax.fori_loop(0, steps, step_body, 0)

    for c in range(CHUNKS):
        for r in range(1, 8):
            part_arrival(c, r).wait_recv()

    opened = 1.0 / (1.0 + jnp.exp(-gate_ref[...]))
    eye = lax.broadcasted_iota(jnp.int32, (128, 128), 0) == lax.broadcasted_iota(
        jnp.int32, (128, 128), 1
    )
    for tile in range(2):
        rows = pl.ds(tile * 128, 128)
        total_square = jnp.zeros((128, 1), F32)
        for head in range(HEADS_HERE):
            columns = pl.ds(head * HD, HD)
            keys = [parts[c][2 * head, 4 * tile : 4 * tile + 4].reshape(4 * ROWS, HD) for c in range(CHUNKS)]
            vals = [parts[c][2 * head + 1, 4 * tile : 4 * tile + 4].reshape(4 * ROWS, HD) for c in range(CHUNKS)]
            scores = lax.dot_general(
                q_ref[rows, columns],
                jnp.concatenate(keys, axis=0),
                (((1,), (1,)), ((), ())),
                preferred_element_type=F32,
            ) * SCALE
            weights = jnp.exp(scores - jnp.max(scores, axis=1, keepdims=True))
            total = jnp.sum(weights, axis=1, keepdims=True)
            product = jnp.dot(
                weights.astype(BF16), jnp.concatenate(vals, axis=0), preferred_element_type=F32
            )
            share = opened[:, head : head + 1]
            both = share * (product / total) + (1.0 - share) * mixed[rows, columns]
            mixed[rows, columns] = both
            total_square += jnp.sum(both * both, axis=1, keepdims=True)
        squares_out[pl.ds(tile * 8, 8)] = jnp.broadcast_to(
            jnp.sum(jnp.where(eye, total_square, 0.0), axis=0, keepdims=True), (8, 128)
        )

    def square_copy(r):
        return pltpu.make_async_remote_copy(
            src_ref=squares_out,
            dst_ref=squares.at[mem],
            send_sem=sq_send.at[r],
            recv_sem=sq_recv.at[mem],
            device_id=mem_peer(r),
            device_id_type=MESH,
        )

    def square_arrival(r):
        return pltpu.make_async_remote_copy(
            src_ref=squares_out,
            dst_ref=squares.at[(mem + r) % 8],
            send_sem=sq_send.at[r],
            recv_sem=sq_recv.at[(mem + r) % 8],
            device_id=mem_peer(r),
            device_id_type=MESH,
        )

    for r in (4, 1, 2, 3, 5, 6, 7):
        square_copy(r).start()
    squares[mem] = squares_out[...]
    for r in range(1, 8):
        square_arrival(r).wait_recv()
    summed = squares[0]
    for m in range(1, 8):
        summed = summed + squares[m]
    for tile in range(2):
        rows = pl.ds(tile * 128, 128)
        column = jnp.sum(
            jnp.where(eye, summed[tile * 8 : tile * 8 + 1], 0.0), axis=1, keepdims=True
        )
        factor = lax.rsqrt(column / FEATURES + 1e-6)
        out_ref[rows] = (mixed[rows] * gain_ref[...] * factor).astype(BF16)

    for r in range(1, 8):
        square_copy(r).wait_send()
        for c in range(CHUNKS):
            part_copy(c, r).wait_send()
        copy1(r).wait_send()
        copy2(r).wait_send()
        for chunk in range(CHUNKS):
            copy_a(r, chunk, mk_ref).wait_send()
    for q in range(PLANE):

        @pl.when(sends_edge & (p != q))
        def _(q=q):
            spread_edge(q).wait_send()

    for d in (1, 2):

        @pl.when(p + d < PLANE)
        def _():
            halo(d, 0).wait_send()
            halo(d, 1).wait_send()

    @pl.when(z < PLANES - 1)
    def _():
        edge_copy().wait_send()

    for source in range(PLANE):

        @pl.when((z > 0) & (p == source))
        def _(source=source):
            each_pass(source, lambda s, t: pass_copy(s, t).wait_send(), lambda s: None)

    for step, into, onward, send, recv, target in (
        (z, ups, ups_out, up_send, up_recv, above),
        (PLANES - 1 - z, downs, downs_out, down_send, down_recv, below),
    ):

        @pl.when(step < PLANES - 1)
        def _():
            def sent(g, carry):
                span = pl.ds(g * group, group)
                for c in range(CHUNKS):
                    pltpu.make_async_remote_copy(
                        src_ref=onward[c].at[span],
                        dst_ref=into[c].at[span],
                        send_sem=send.at[c, g],
                        recv_sem=recv.at[c, g],
                        device_id=target,
                        device_id_type=MESH,
                    ).wait_send()
                return carry

            lax.fori_loop(floor_at(step), cap_at(step), sent, 0)


def attend(tier, collective_id, ids, gate, gain, q, k, v, mk, mv):
    slots = tier[0][-1]
    groups = slots // tier[1]
    ring = [pltpu.VMEM((slots, ROWS, HD), BF16)] * CHUNKS
    hand = [pltpu.VMEM((PLANE, REQ, ROWS, HD), BF16)] * CHUNKS
    dma = pltpu.SemaphoreType.DMA
    return pl.pallas_call(
        functools.partial(attend_kernel, tier),
        out_shape=[
            jax.ShapeDtypeStruct((TOK, HEADS_HERE * HD), BF16),
            jax.ShapeDtypeStruct((1,), jnp.int32),
        ],
        in_specs=[SMEM] + [HBM] * 7,
        out_specs=[VMEM, SMEM],
        scratch_shapes=[
            pltpu.VMEM((2, 8, HD), jnp.int32),
            pltpu.SMEM((2, 8, HD), jnp.int32),
            pltpu.VMEM((PLANE, 8, HD), jnp.int32),
            pltpu.VMEM((PLANES, 8, HD), jnp.int32),
            pltpu.VMEM((1, HEADS_HERE), F32),
            pltpu.VMEM((TOK, HEADS_HERE * HD), BF16),
            pltpu.VMEM((1, HEADS_HERE * HD), F32),
            pltpu.VMEM((3 * TOK, HEADS_HERE * HD), BF16),
            pltpu.VMEM((3 * TOK, HEADS_HERE * HD), BF16),
            pltpu.VMEM((TOK, HEADS_HERE * HD), F32),
            *[pltpu.VMEM((LOCAL, ROWS, HD), BF16)] * CHUNKS,
            *ring,
            *ring,
            *ring,
            *ring,
            *hand,
            *hand,
            pltpu.VMEM((16, HD), F32),
            pltpu.VMEM((8, 16, HD), F32),
            pltpu.VMEM((2 * TOK, HD), BF16),
            pltpu.VMEM((2 * TOK, HD), BF16),
            dma(()),
            dma((8,)),
            dma((8,)),
            dma((8,)),
            dma((8,)),
            dma((CHUNKS, 8)),
            dma((CHUNKS, 8)),
            dma((8,)),
            dma((2,)),
            dma((CHUNKS + 1,)),
            dma((5,)),
            dma((4,)),
            dma((4,)),
            dma((CHUNKS, groups)),
            dma((CHUNKS, groups)),
            dma((CHUNKS, groups)),
            dma((CHUNKS, groups)),
            dma((CHUNKS, 8)),
            dma((CHUNKS, 8)),
            dma((8,)),
            dma((8,)),
            dma((2,)),
            dma((2,)),
            dma((8,)),
        ],
        compiler_params=pltpu.CompilerParams(
            collective_id=collective_id, has_side_effects=True, vmem_limit_bytes=60 << 20
        ),
        name="attend_" + str(slots),
    )(ids, gate, gain, q, k, v, mk, mv)


def shards(queries, keys, values, memory_keys, memory_values, retrieval, gate, gain):
    operands = (
        retrieval,
        gate.reshape(1, -1),
        gain.reshape(1, -1),
        queries,
        keys,
        values,
        memory_keys,
        memory_values,
    )
    out, fits = attend(SHORT, 0, *operands)
    return lax.cond(
        fits[0] > 0,
        lambda out, *_: out,
        lambda _, *operands: attend(LONG, 1, *operands)[0],
        out,
        *operands,
    )


def solution(mesh):
    in_specs = (
        P("ctx", "mem"),
        P("ctx", "mem"),
        P("ctx", "mem"),
        P("ctx", None, "mem"),
        P("ctx", None, "mem"),
        P("ctx", None),
        P("mem"),
        P("mem"),
    )
    return jax.shard_map(
        shards, mesh=mesh, in_specs=in_specs, out_specs=P("ctx", "mem"), check_vma=False
    )
```

```python
import functools
import math

import jax
import jax.numpy as jnp
from jax import lax
from jax.experimental import pallas as pl
from jax.experimental.pallas import tpu as pltpu
from jax.sharding import PartitionSpec as P

MESH = pl.DeviceIdType.MESH
HBM = pl.BlockSpec(memory_space=pltpu.HBM)
VMEM = pl.BlockSpec(memory_space=pltpu.VMEM)
SMEM = pl.BlockSpec(memory_space=pltpu.SMEM)
F32 = jnp.float32
BF16 = jnp.bfloat16

HD = 128
HEADS_HERE = 4
FEATURES = 4096
PLANES = 8
PLANE = 8
REQ = 8
BLK = 64
LOCAL = 64
TOK = 256
CHUNKS = 2
ROWS = BLK // CHUNKS
SCALE = 1.0 / math.sqrt(HD)

SHORT = ((56, 88, 104, 112), 8, (3, 7, 10, 11), 16, 128)
LONG = ((64, 128, 192, 256), 16, (2, 4, 6, 8), 0, 256)
REACHES = (7, 1, 2, 3, 4, 5, 6)


def iota(shape, dim):
    return lax.broadcasted_iota(jnp.int32, shape, dim).astype(F32)


def greet(peers):
    barrier = pltpu.get_barrier_semaphore()
    total = 0
    for device, present in peers:
        if present is None:
            pl.semaphore_signal(barrier, inc=1, device_id=device, device_id_type=MESH)
            total = total + 1
        else:

            @pl.when(present)
            def _(device=device):
                pl.semaphore_signal(barrier, inc=1, device_id=device, device_id_type=MESH)

            total = total + present.astype(jnp.int32)
    pl.semaphore_wait(barrier, total)


def schedule(tier, lists, my_z, table_ref):
    caps, _, _, left_out, known = tier
    block = iota((1, PLANES * LOCAL), 1)
    asker_z = jnp.floor(iota((PLANES * PLANE, 1), 0) / PLANE)
    top = jnp.full((1, PLANES * LOCAL), -1.0, F32)
    low = jnp.full((1, PLANES * LOCAL), 8.0, F32)
    for j in range(REQ):
        hit = lists[:, j : j + 1] == block
        top = jnp.maximum(top, jnp.max(jnp.where(hit, asker_z, -1.0), axis=0, keepdims=True))
        low = jnp.minimum(low, jnp.min(jnp.where(hit, asker_z, 8.0), axis=0, keepdims=True))
    kind = jnp.full((8, 1), -1.0, F32)
    for i, reach in enumerate(REACHES):
        kind = jnp.where(iota((8, 1), 0) == i, reach, kind)
    turns = [(way, step) for step in range(PLANES - 1) for way in range(2)]

    def plane(way, step):
        return step if way == 0 else PLANES - 1 - step

    reaches = {}
    for way in range(2):
        for step in range(PLANES):
            z = plane(way, step)
            span = slice(z * LOCAL, (z + 1) * LOCAL)
            reaches[way, step] = top[:, span] if way == 0 else (PLANES - 1) - low[:, span]
    stacked = [
        jnp.concatenate([reaches[way, step] for step in range(PLANES)], axis=0) for way in range(2)
    ]
    step_of_row = iota((PLANES, LOCAL), 0)
    fits = jnp.ones((1, 1), F32)
    heights = {}
    for way in range(2):
        height = jnp.zeros((1, 1), F32)
        for step in range(PLANES - 1):
            over = (stacked[way] > step) & (step_of_row <= step)
            load = jnp.sum(
                jnp.sum(over.astype(F32), axis=1, keepdims=True), axis=0, keepdims=True
            )
            height = jnp.maximum(height, load)
            heights[way, step] = height
            fits = fits * (load <= caps[min(step, 3)]).astype(F32)

    kinds = jnp.concatenate(
        [
            ((reaches[turn] == kind) & (reaches[turn] > turn[1])).astype(F32)
            for turn in turns
        ],
        axis=0,
    )
    many = 8 * len(turns)
    before_lane = (iota((LOCAL, LOCAL), 0) < iota((LOCAL, LOCAL), 1)).astype(BF16)
    turn_row, turn_column = (
        jnp.floor(iota((many, many), 0) / 8),
        jnp.floor(iota((many, many), 1) / 8),
    )
    before_kind = (
        (turn_row == turn_column) & (iota((many, many), 1) < iota((many, many), 0))
    ).astype(BF16)
    of_kind = jnp.dot(kinds.astype(BF16), before_lane, preferred_element_type=F32)
    earlier = jnp.dot(
        before_kind,
        jnp.broadcast_to(jnp.sum(kinds, axis=1, keepdims=True), (many, HD)).astype(BF16),
        preferred_element_type=F32,
    )[:, 0:1]
    ranked = kinds * (of_kind + earlier)
    ranks = {
        turn: jnp.sum(ranked[8 * i : 8 * i + 8], axis=0, keepdims=True)
        for i, turn in enumerate(turns)
    }

    eye = (iota((LOCAL, LOCAL), 0) == iota((LOCAL, LOCAL), 1)).astype(BF16)

    def as_columns(rows):
        return lax.dot_general(
            eye, rows.astype(BF16), (((1,), (1,)), ((), ())), preferred_element_type=F32
        )

    reach_columns = [as_columns(rows) for rows in stacked]
    rank_columns = as_columns(
        jnp.concatenate([ranks[turn] for turn in turns] + [ranks[turns[0]]] * 2, axis=0)
    )
    place_column = iota((LOCAL, 1), 0)
    after_lane = (iota((known, known), 0) > iota((known, known), 1)).astype(BF16)
    slot_row = iota((1, known), 1)
    nothing = jnp.full((1, known), -1.0, F32)
    ends, helds = [nothing, nothing], [nothing, nothing]
    injected, arrived = [nothing, nothing], [nothing, nothing]
    for i, (way, step) in enumerate(turns):
        z = plane(way, step)
        reach = reach_columns[way][:, step : step + 1]
        rank = jnp.where(reach > step, rank_columns[:, i : i + 1], -2.0)
        end = ends[way]
        free = (end <= step) & (slot_row < heights[way, step])
        free_rank = jnp.dot(
            jnp.broadcast_to(free.astype(F32), (8, known)).astype(BF16),
            after_lane,
            preferred_element_type=F32,
        )[0:1]
        pair = rank == jnp.where(free, free_rank, -1.0)
        code = jnp.sum(
            jnp.where(pair, 1.0 + place_column + LOCAL * reach, 0.0), axis=0, keepdims=True
        )
        taken = code > 0.5
        new_end = jnp.floor((code - 1.0) / LOCAL)
        new_block = code - 1.0 - LOCAL * new_end
        helds[way] = jnp.where(
            taken, z * LOCAL + new_block, jnp.where(end <= step, -1.0, helds[way])
        )
        ends[way] = jnp.where(taken, new_end, end)
        injected[way] = jnp.where(my_z == z, jnp.where(taken, new_block, -1.0), injected[way])
        arrived[way] = jnp.where(my_z == plane(way, step + 1), helds[way], arrived[way])
        if step == PLANES - 2:
            lowest = jnp.min(
                jnp.where(ends[way] > step, slot_row, known), axis=1, keepdims=True
            )
            fits = fits * (lowest >= left_out).astype(F32)
    in_up, in_down = injected
    at_up, at_down = arrived
    rows = iota((8, HD), 0)
    out = jnp.where(rows == 4, fits, 0.0)
    for i in range(known // HD):
        out = jnp.where(rows == i, in_up[:, i * HD : (i + 1) * HD], out)
        out = jnp.where(rows == 2 + i, in_down[:, i * HD : (i + 1) * HD], out)
    table_ref[1] = out.astype(jnp.int32)

    slot = iota((1, known), 1)
    mine = jnp.zeros((PLANE, HD), F32)
    for z in range(PLANES):
        mine = jnp.where(my_z == z, lists[z * PLANE : (z + 1) * PLANE], mine)
    place = jnp.zeros((PLANE, HD), F32)
    lanes = iota((PLANE, HD), 1)
    z_here = my_z.astype(F32)
    for j in range(REQ):
        wanted = mine[:, j : j + 1]
        owner_z = jnp.floor(wanted / LOCAL)
        slot_up = jnp.sum(jnp.where(at_up == wanted, slot, 0.0), axis=1, keepdims=True)
        slot_down = jnp.sum(jnp.where(at_down == wanted, slot, 0.0), axis=1, keepdims=True)
        found = jnp.where(owner_z == z_here, wanted - LOCAL * owner_z, LOCAL + known + slot_down)
        found = jnp.where(owner_z < z_here, LOCAL + slot_up, found)
        place = jnp.where(lanes == j, found, place)
    table_ref[0] = place.astype(jnp.int32)


def attend_kernel(tier, *refs):
    caps, group, lags, left_out, known = tier
    slots = caps[-1]
    groups = slots // group
    ids_ref, gate_hbm, gain_hbm, q_hbm, k_ref, v_ref, mk_ref, mv_ref = refs[:8]
    out_ref, fits_ref = refs[8:10]
    rest = list(refs[10:])

    def take(n):
        got = rest[:n]
        del rest[:n]
        return got

    table_out, table, line, lists = take(4)
    gate_ref, q_ref, gain_ref, near_k, near_v, mixed = take(6)
    pools, ups, downs = take(CHUNKS), take(CHUNKS), take(CHUNKS)
    ups_out, downs_out = take(CHUNKS), take(CHUNKS)
    parts_out, parts = take(CHUNKS), take(CHUNKS)
    squares_out, squares, edge_ref, edge_in = take(4)
    table_sem, send1, recv1, send2, recv2, send_a, recv_a, edge_send, edge_recv = take(9)
    (
        pool_sem,
        own_sem,
        halo_send,
        halo_recv,
        up_send,
        up_recv,
        down_send,
        down_recv,
        part_send,
        part_recv,
        sq_send,
        sq_recv,
        edge_sem,
        pass_send,
        pass_recv,
    ) = rest

    me = lax.axis_index("ctx")
    mem = lax.axis_index("mem")
    z, p = me // PLANE, me % PLANE
    x, core = p // 2, p % 2

    def in_plane(r):
        return {"ctx": z * PLANE + (p + r) % PLANE}

    def on_line(r):
        return {"ctx": ((z + r) % PLANES) * PLANE + p}

    def mem_peer(r):
        return {"mem": (mem + r) % 8}

    above, below = {"ctx": me + PLANE}, {"ctx": me - PLANE}
    loads = [
        pltpu.make_async_copy(k_ref, near_k.at[pl.ds(2 * TOK, TOK)], own_sem.at[0]),
        pltpu.make_async_copy(v_ref, near_v.at[pl.ds(2 * TOK, TOK)], own_sem.at[1]),
        pltpu.make_async_copy(q_hbm, q_ref, own_sem.at[2]),
        pltpu.make_async_copy(gate_hbm, gate_ref, own_sem.at[3]),
        pltpu.make_async_copy(gain_hbm, gain_ref, own_sem.at[4]),
    ]
    for load in loads:
        load.start()

    greet(
        [(in_plane(r), None) for r in range(1, 8)]
        + [(mem_peer(r), None) for r in range(1, 8)]
        + [(on_line(r), None) for r in range(1, 8)]
    )

    def edge_copy():
        return pltpu.make_async_remote_copy(
            src_ref=edge_ref,
            dst_ref=edge_in,
            send_sem=edge_sem.at[0],
            recv_sem=edge_sem.at[1],
            device_id=above,
            device_id_type=MESH,
        )

    def edge_here():
        for source in range(2):

            @pl.when((z < PLANES - 1) & (p == 6 + source))
            def _(source=source):
                edge_own(0).wait()

            @pl.when((z < PLANES - 1) & (p != 6 + source))
            def _(source=source):
                edge_arrival(source).wait_recv()

        @pl.when(z < PLANES - 1)
        def _():
            edge_copy().start()

    def passed(source, to):
        near = near_v if source % 2 else near_k
        columns = pl.ds(source // 2 * HD, HD)
        came = edge_in if to == 0 else edge_in.at[pl.ds(TOK, TOK)]
        return came, near.at[pl.ds(0, 2 * TOK if to == 0 else TOK), columns]

    def pass_copy(source, to):
        came, near = passed(source, to)
        return pltpu.make_async_remote_copy(
            src_ref=came,
            dst_ref=near,
            send_sem=pass_send.at[to],
            recv_sem=pass_recv.at[source],
            device_id={"ctx": z * PLANE + to},
            device_id_type=MESH,
        )

    def pass_own(source):
        came, near = passed(source, source)
        return pltpu.make_async_copy(came, near, pass_recv.at[source])

    def each_pass(source, remote, local):
        for to in range(2):
            if source == to:
                local(source)
            else:
                remote(source, to)

    def pass_on():
        edge_copy().wait_recv()
        for source in range(PLANE):

            @pl.when(p == source)
            def _(source=source):
                each_pass(
                    source,
                    lambda s, t: pass_copy(s, t).start(),
                    lambda s: pass_own(s).start(),
                )

    lanes = lax.broadcasted_iota(jnp.int32, (8, HD), 1)
    row = jnp.zeros((8, HD), jnp.int32)
    for j in range(REQ):
        row = jnp.where(lanes == j, ids_ref[j // 4, j % 4], row)
    line[p] = row

    def copy1(r):
        return pltpu.make_async_remote_copy(
            src_ref=line.at[p],
            dst_ref=line.at[p],
            send_sem=send1.at[r],
            recv_sem=recv1.at[p],
            device_id=in_plane(r),
            device_id_type=MESH,
        )

    def arrival1(r):
        q = (p + r) % PLANE
        return pltpu.make_async_remote_copy(
            src_ref=line.at[q],
            dst_ref=line.at[q],
            send_sem=send1.at[r],
            recv_sem=recv1.at[q],
            device_id=in_plane(r),
            device_id_type=MESH,
        )

    for r in range(1, 8):
        copy1(r).start()

    def part(r, chunk, ref):
        q = (p + r) % PLANE
        return ref.at[:, pl.ds(chunk * ROWS, ROWS), pl.ds(pl.multiple_of((q // 2) * HD, HD), HD)]

    def copy_a(r, chunk, ref):
        return pltpu.make_async_remote_copy(
            src_ref=part(r, chunk, ref),
            dst_ref=pools[chunk].at[pl.ds(p * 8, 8)],
            send_sem=send_a.at[chunk, r],
            recv_sem=recv_a.at[chunk, p],
            device_id=in_plane(r),
            device_id_type=MESH,
        )

    def arrival_a(r, chunk):
        q = (p + r) % PLANE
        return pltpu.make_async_remote_copy(
            src_ref=part(r, chunk, mk_ref),
            dst_ref=pools[chunk].at[pl.ds(q * 8, 8)],
            send_sem=send_a.at[chunk, r],
            recv_sem=recv_a.at[chunk, q],
            device_id=in_plane(r),
            device_id_type=MESH,
        )

    def own_a(ref, chunk):
        return pltpu.make_async_copy(
            part(0, chunk, ref), pools[chunk].at[pl.ds(p * 8, 8)], pool_sem.at[chunk]
        )

    def spread_blocks(chunk):
        for r in (4, 3, 5, 2, 6, 1, 7):
            to_core = (core + r) % 2

            @pl.when(to_core == 0)
            def _():
                copy_a(r, chunk, mk_ref).start()

            @pl.when(to_core == 1)
            def _():
                copy_a(r, chunk, mv_ref).start()

        @pl.when(core == 0)
        def _():
            own_a(mk_ref, chunk).start()

        @pl.when(core == 1)
        def _():
            own_a(mv_ref, chunk).start()

    def blocks_here(chunk):
        own_a(mk_ref, chunk).wait()
        for r in range(1, 8):
            arrival_a(r, chunk).wait_recv()

    spread_blocks(0)

    def edge_part(q):
        ref = v_ref if q % 2 else k_ref
        return ref.at[:, pl.ds(q // 2 * HD, HD)]

    def spread_edge(q):
        return pltpu.make_async_remote_copy(
            src_ref=edge_part(q),
            dst_ref=edge_ref.at[pl.ds(core * TOK, TOK)],
            send_sem=edge_send.at[q],
            recv_sem=edge_recv.at[core],
            device_id={"ctx": z * PLANE + q},
            device_id_type=MESH,
        )

    def edge_arrival(source):
        return pltpu.make_async_remote_copy(
            src_ref=edge_part(0),
            dst_ref=edge_ref.at[pl.ds(source * TOK, TOK)],
            send_sem=edge_send.at[0],
            recv_sem=edge_recv.at[source],
            device_id=in_plane(1),
            device_id_type=MESH,
        )

    def edge_own(q):
        return pltpu.make_async_copy(
            edge_part(q), edge_ref.at[pl.ds(core * TOK, TOK)], pool_sem.at[CHUNKS]
        )

    sends_edge = (x == 3) & (z < PLANES - 1)
    for q in range(PLANE):

        @pl.when(sends_edge & (p != q))
        def _(q=q):
            spread_edge(q).start()

        @pl.when(sends_edge & (p == q))
        def _(q=q):
            edge_own(q).start()

    for chunk in range(1, CHUNKS):
        spread_blocks(chunk)
    def halo(d, which):
        ref, near = ((k_ref, near_k), (v_ref, near_v))[which]
        return pltpu.make_async_remote_copy(
            src_ref=ref,
            dst_ref=near.at[pl.ds((2 - d) * TOK, TOK)],
            send_sem=halo_send.at[2 * d - 2 + which],
            recv_sem=halo_recv.at[2 * d - 2 + which],
            device_id={"ctx": me + d},
            device_id_type=MESH,
        )

    for d in (1, 2):

        @pl.when(p + d < PLANE)
        def _():
            halo(d, 0).start()
            halo(d, 1).start()

        @pl.when((z == 0) & (p < d))
        def _():
            near_k[pl.ds((2 - d) * TOK, TOK)] = jnp.zeros((TOK, HEADS_HERE * HD), BF16)
            near_v[pl.ds((2 - d) * TOK, TOK)] = jnp.zeros((TOK, HEADS_HERE * HD), BF16)

    for r in range(1, 8):
        arrival1(r).wait_recv()
    rows = lax.broadcasted_iota(jnp.int32, (8, HD), 0)
    whole = jnp.zeros((8, HD), jnp.int32)
    for q in range(PLANE):
        whole = jnp.where(rows == q, line[q], whole)
    lists[z] = whole

    def copy2(r):
        return pltpu.make_async_remote_copy(
            src_ref=lists.at[z],
            dst_ref=lists.at[z],
            send_sem=send2.at[r],
            recv_sem=recv2.at[z],
            device_id=on_line(r),
            device_id_type=MESH,
        )

    def arrival2(r):
        q = (z + r) % PLANES
        return pltpu.make_async_remote_copy(
            src_ref=lists.at[q],
            dst_ref=lists.at[q],
            send_sem=send2.at[r],
            recv_sem=recv2.at[q],
            device_id=on_line(r),
            device_id_type=MESH,
        )

    for r in range(1, 8):
        copy2(r).start()
    for r in range(1, 8):
        arrival2(r).wait_recv()
    schedule(tier, lists[...].reshape(PLANES * PLANE, HD).astype(F32), z, table_out)
    to_scalars = pltpu.make_async_copy(table_out, table, table_sem)
    to_scalars.start()
    to_scalars.wait()
    fits_ref[0] = table[1, 4, 0]
    edge_here()
    for load in loads:
        load.wait()
    blocks_here(0)

    caps_g = [c // group for c in caps]

    def cap_at(step):
        value = jnp.int32(caps_g[3])
        for i in (2, 1, 0):
            value = jnp.where(step == i, caps_g[i], value)
        return value

    def floor_at(step):
        return jnp.where(step >= PLANES - 2, left_out // group, 0)

    def lag_at(step):
        value = jnp.int32(0)
        for i in range(4):
            value = jnp.where(step == 4 + i, lags[i], value)
        return value

    def conveyor(k, step, target, pool, into, onward, send, recv, row):
        cap = cap_at(step)
        position = jnp.where(step <= 3, k + groups - cap, k - lag_at(step))
        inside = (position >= 0) & (position < CHUNKS * groups)
        at = jnp.maximum(position, 0)
        chunk = at // groups
        g = groups - 1 - at % groups
        active = inside & (g < cap)
        incoming = (step > 0) & (g < cap_at(step - 1)) & (g >= floor_at(step - 1))

        def copy(c):
            span = pl.ds(g * group, group)
            return pltpu.make_async_remote_copy(
                src_ref=onward[c].at[span],
                dst_ref=into[c].at[span],
                send_sem=send.at[c, g],
                recv_sem=recv.at[c, g],
                device_id=target,
                device_id_type=MESH,
            )

        for c in range(CHUNKS):

            @pl.when(active & (chunk == c))
            def _(c=c):
                @pl.when(incoming)
                def _():
                    copy(c).wait_recv()

                @pl.when((step < PLANES - 1) & (g >= floor_at(step)))
                def _():
                    for i in range(group):
                        slot = g * group + i
                        inject = table[1, row + slot // HD, slot % HD]
                        local = pool[c][jnp.clip(inject, 0, LOCAL - 1)]
                        onward[c][slot] = jnp.where(inject >= 0, local, into[c][slot])
                    copy(c).start()

    def part_copy(c, r):
        q = (p + r) % PLANE
        return pltpu.make_async_remote_copy(
            src_ref=parts_out[c].at[q],
            dst_ref=parts[c].at[p],
            send_sem=part_send.at[c, r],
            recv_sem=part_recv.at[c, p],
            device_id=in_plane(r),
            device_id_type=MESH,
        )

    def part_arrival(c, r):
        q = (p + r) % PLANE
        return pltpu.make_async_remote_copy(
            src_ref=parts_out[c].at[q],
            dst_ref=parts[c].at[q],
            send_sem=part_send.at[c, r],
            recv_sem=part_recv.at[c, q],
            device_id=in_plane(r),
            device_id_type=MESH,
        )

    def hand_out(c):
        def pick(q, j):
            place = table[0, q, j]
            own = pools[c][jnp.clip(place, 0, LOCAL - 1)]
            from_below = ups[c][jnp.clip(place - LOCAL, 0, slots - 1)]
            from_above = downs[c][jnp.clip(place - LOCAL - known, 0, slots - 1)]
            return jnp.where(
                place < LOCAL, own, jnp.where(place < LOCAL + known, from_below, from_above)
            )

        for r in (4, 3, 5, 2, 6, 1, 7):
            q = (p + r) % PLANE
            for j in range(REQ):
                parts_out[c][q, j] = pick(q, j)
            part_copy(c, r).start()
        for j in range(REQ):
            parts[c][p, j] = pick(p, j)

    def window_piece(head, tile):
        columns = pl.ds(pl.multiple_of(head * HD, HD), HD)
        rows = pl.ds(pl.multiple_of(tile * 128, 128), 128)
        near = pl.ds(pl.multiple_of(tile * 128, 128), 640)
        scores = lax.dot_general(
            q_ref[rows, columns],
            near_k[near, columns],
            (((1,), (1,)), ((), ())),
            preferred_element_type=F32,
        )
        key = lax.broadcasted_iota(jnp.int32, (128, 640), 1)
        ahead = key - lax.broadcasted_iota(jnp.int32, (128, 640), 0)
        first = me * TOK - 2 * TOK + tile * 128
        allowed = (ahead > 0) & (ahead <= 512) & (key >= -first)
        scores = jnp.where(allowed, scores * SCALE, -jnp.inf)
        weights = jnp.exp(scores - jnp.max(scores, axis=1, keepdims=True))
        total = jnp.sum(weights, axis=1, keepdims=True)
        product = jnp.dot(weights.astype(BF16), near_v[near, columns], preferred_element_type=F32)
        mixed[rows, columns] = product / total

    steps = CHUNKS * groups + max(lags[2], lags[3] - left_out // group)
    far = jnp.maximum(z, PLANES - 1 - z)
    far = lag_at(far) - floor_at(far - 1)
    pieces = 2 * HEADS_HERE
    pass_step = 5
    early, every, first_piece = 3, 2, groups + 6

    def step_body(k, carry):
        for chunk in range(1, CHUNKS):

            @pl.when(k == (chunk - 1) * groups + caps_g[0])
            def _(chunk=chunk):
                blocks_here(chunk)

        conveyor(k, z, above, pools, ups, ups_out, up_send, up_recv, 0)
        conveyor(k, PLANES - 1 - z, below, pools, downs, downs_out, down_send, down_recv, 2)
        for c in range(CHUNKS):

            @pl.when(k == (c + 1) * groups - 1 + far)
            def _(c=c):
                hand_out(c)

        @pl.when((k == pass_step) & (z > 0))
        def _():
            pass_on()

        @pl.when(k == first_piece)
        def _():
            for d in (1, 2):

                @pl.when(p >= d)
                def _():
                    halo(d, 0).wait_recv()
                    halo(d, 1).wait_recv()

            for to in range(2):

                @pl.when((z > 0) & (p == to))
                def _(to=to):
                    for source in range(PLANE):
                        if source == to:
                            pass_own(source).wait()
                        else:
                            pass_copy(source, to).wait_recv()

        since = k - first_piece
        piece = jnp.maximum(since, 0) // every

        @pl.when((since >= 0) & (since % every == 0) & (piece < early))
        def _():
            window_piece(piece // 2, piece % 2)

        return carry

    lax.fori_loop(0, steps, step_body, 0)

    def late_piece(piece, carry):
        window_piece(piece // 2, piece % 2)
        return carry

    lax.fori_loop(early, pieces, late_piece, 0)

    for c in range(CHUNKS):
        for r in range(1, 8):
            part_arrival(c, r).wait_recv()

    opened = 1.0 / (1.0 + jnp.exp(-gate_ref[...]))
    eye = lax.broadcasted_iota(jnp.int32, (128, 128), 0) == lax.broadcasted_iota(
        jnp.int32, (128, 128), 1
    )
    for tile in range(2):
        rows = pl.ds(tile * 128, 128)
        total_square = jnp.zeros((128, 1), F32)
        for head in range(HEADS_HERE):
            columns = pl.ds(head * HD, HD)
            keys = [parts[c][2 * head, 4 * tile : 4 * tile + 4].reshape(4 * ROWS, HD) for c in range(CHUNKS)]
            vals = [parts[c][2 * head + 1, 4 * tile : 4 * tile + 4].reshape(4 * ROWS, HD) for c in range(CHUNKS)]
            scores = lax.dot_general(
                q_ref[rows, columns],
                jnp.concatenate(keys, axis=0),
                (((1,), (1,)), ((), ())),
                preferred_element_type=F32,
            ) * SCALE
            weights = jnp.exp(scores - jnp.max(scores, axis=1, keepdims=True))
            total = jnp.sum(weights, axis=1, keepdims=True)
            product = jnp.dot(
                weights.astype(BF16), jnp.concatenate(vals, axis=0), preferred_element_type=F32
            )
            share = opened[:, head : head + 1]
            both = share * (product / total) + (1.0 - share) * mixed[rows, columns]
            mixed[rows, columns] = both
            total_square += jnp.sum(both * both, axis=1, keepdims=True)
        squares_out[pl.ds(tile * 8, 8)] = jnp.broadcast_to(
            jnp.sum(jnp.where(eye, total_square, 0.0), axis=0, keepdims=True), (8, 128)
        )

    def square_copy(r):
        return pltpu.make_async_remote_copy(
            src_ref=squares_out,
            dst_ref=squares.at[mem],
            send_sem=sq_send.at[r],
            recv_sem=sq_recv.at[mem],
            device_id=mem_peer(r),
            device_id_type=MESH,
        )

    def square_arrival(r):
        return pltpu.make_async_remote_copy(
            src_ref=squares_out,
            dst_ref=squares.at[(mem + r) % 8],
            send_sem=sq_send.at[r],
            recv_sem=sq_recv.at[(mem + r) % 8],
            device_id=mem_peer(r),
            device_id_type=MESH,
        )

    for r in (4, 1, 2, 3, 5, 6, 7):
        square_copy(r).start()
    squares[mem] = squares_out[...]
    for r in range(1, 8):
        square_arrival(r).wait_recv()
    summed = squares[0]
    for m in range(1, 8):
        summed = summed + squares[m]
    for tile in range(2):
        rows = pl.ds(tile * 128, 128)
        column = jnp.sum(
            jnp.where(eye, summed[tile * 8 : tile * 8 + 1], 0.0), axis=1, keepdims=True
        )
        factor = lax.rsqrt(column / FEATURES + 1e-6)
        out_ref[rows] = (mixed[rows] * gain_ref[...] * factor).astype(BF16)

    for r in range(1, 8):
        square_copy(r).wait_send()
        for c in range(CHUNKS):
            part_copy(c, r).wait_send()
        copy1(r).wait_send()
        copy2(r).wait_send()
        for chunk in range(CHUNKS):
            copy_a(r, chunk, mk_ref).wait_send()
    for q in range(PLANE):

        @pl.when(sends_edge & (p != q))
        def _(q=q):
            spread_edge(q).wait_send()

    for d in (1, 2):

        @pl.when(p + d < PLANE)
        def _():
            halo(d, 0).wait_send()
            halo(d, 1).wait_send()

    @pl.when(z < PLANES - 1)
    def _():
        edge_copy().wait_send()

    for source in range(PLANE):

        @pl.when((z > 0) & (p == source))
        def _(source=source):
            each_pass(source, lambda s, t: pass_copy(s, t).wait_send(), lambda s: None)

    for step, into, onward, send, recv, target in (
        (z, ups, ups_out, up_send, up_recv, above),
        (PLANES - 1 - z, downs, downs_out, down_send, down_recv, below),
    ):

        @pl.when(step < PLANES - 1)
        def _():
            def sent(g, carry):
                span = pl.ds(g * group, group)
                for c in range(CHUNKS):
                    pltpu.make_async_remote_copy(
                        src_ref=onward[c].at[span],
                        dst_ref=into[c].at[span],
                        send_sem=send.at[c, g],
                        recv_sem=recv.at[c, g],
                        device_id=target,
                        device_id_type=MESH,
                    ).wait_send()
                return carry

            lax.fori_loop(floor_at(step), cap_at(step), sent, 0)


def attend(tier, collective_id, ids, gate, gain, q, k, v, mk, mv):
    slots = tier[0][-1]
    groups = slots // tier[1]
    ring = [pltpu.VMEM((slots, ROWS, HD), BF16)] * CHUNKS
    hand = [pltpu.VMEM((PLANE, REQ, ROWS, HD), BF16)] * CHUNKS
    dma = pltpu.SemaphoreType.DMA
    return pl.pallas_call(
        functools.partial(attend_kernel, tier),
        out_shape=[
            jax.ShapeDtypeStruct((TOK, HEADS_HERE * HD), BF16),
            jax.ShapeDtypeStruct((1,), jnp.int32),
        ],
        in_specs=[SMEM] + [HBM] * 7,
        out_specs=[VMEM, SMEM],
        scratch_shapes=[
            pltpu.VMEM((2, 8, HD), jnp.int32),
            pltpu.SMEM((2, 8, HD), jnp.int32),
            pltpu.VMEM((PLANE, 8, HD), jnp.int32),
            pltpu.VMEM((PLANES, 8, HD), jnp.int32),
            pltpu.VMEM((1, HEADS_HERE), F32),
            pltpu.VMEM((TOK, HEADS_HERE * HD), BF16),
            pltpu.VMEM((1, HEADS_HERE * HD), F32),
            pltpu.VMEM((3 * TOK, HEADS_HERE * HD), BF16),
            pltpu.VMEM((3 * TOK, HEADS_HERE * HD), BF16),
            pltpu.VMEM((TOK, HEADS_HERE * HD), F32),
            *[pltpu.VMEM((LOCAL, ROWS, HD), BF16)] * CHUNKS,
            *ring,
            *ring,
            *ring,
            *ring,
            *hand,
            *hand,
            pltpu.VMEM((16, HD), F32),
            pltpu.VMEM((8, 16, HD), F32),
            pltpu.VMEM((2 * TOK, HD), BF16),
            pltpu.VMEM((2 * TOK, HD), BF16),
            dma(()),
            dma((8,)),
            dma((8,)),
            dma((8,)),
            dma((8,)),
            dma((CHUNKS, 8)),
            dma((CHUNKS, 8)),
            dma((8,)),
            dma((2,)),
            dma((CHUNKS + 1,)),
            dma((5,)),
            dma((4,)),
            dma((4,)),
            dma((CHUNKS, groups)),
            dma((CHUNKS, groups)),
            dma((CHUNKS, groups)),
            dma((CHUNKS, groups)),
            dma((CHUNKS, 8)),
            dma((CHUNKS, 8)),
            dma((8,)),
            dma((8,)),
            dma((2,)),
            dma((2,)),
            dma((8,)),
        ],
        compiler_params=pltpu.CompilerParams(
            collective_id=collective_id, has_side_effects=True, vmem_limit_bytes=60 << 20
        ),
        name="attend_" + str(slots),
    )(ids, gate, gain, q, k, v, mk, mv)


def shards(queries, keys, values, memory_keys, memory_values, retrieval, gate, gain):
    operands = (
        retrieval,
        gate.reshape(1, -1),
        gain.reshape(1, -1),
        queries,
        keys,
        values,
        memory_keys,
        memory_values,
    )
    out, fits = attend(SHORT, 0, *operands)
    return lax.cond(
        fits[0] > 0,
        lambda out, *_: out,
        lambda _, *operands: attend(LONG, 1, *operands)[0],
        out,
        *operands,
    )


def solution(mesh):
    in_specs = (
        P("ctx", "mem"),
        P("ctx", "mem"),
        P("ctx", "mem"),
        P("ctx", None, "mem"),
        P("ctx", None, "mem"),
        P("ctx", None),
        P("mem"),
        P("mem"),
    )
    return jax.shard_map(
        shards, mesh=mesh, in_specs=in_specs, out_specs=P("ctx", "mem"), check_vma=False
    )
```

```python
import functools
import math

import jax
import jax.numpy as jnp
from jax import lax
from jax.experimental import pallas as pl
from jax.experimental.pallas import tpu as pltpu
from jax.sharding import PartitionSpec as P

MESH = pl.DeviceIdType.MESH
HBM = pl.BlockSpec(memory_space=pltpu.HBM)
VMEM = pl.BlockSpec(memory_space=pltpu.VMEM)
SMEM = pl.BlockSpec(memory_space=pltpu.SMEM)
F32 = jnp.float32
BF16 = jnp.bfloat16

HD = 128
HEADS_HERE = 4
FEATURES = 4096
PLANES = 8
PLANE = 8
REQ = 8
BLK = 64
LOCAL = 64
TOK = 256
CHUNKS = 2
ROWS = BLK // CHUNKS
SCALE = 1.0 / math.sqrt(HD)

SHORT = ((56, 80, 104, 112), 8, (3, 7, 10, 11), 16, 128)
LONG = ((64, 128, 192, 256), 16, (2, 4, 6, 8), 0, 256)
REACHES = (7, 1, 2, 3, 4, 5, 6)


def iota(shape, dim):
    return lax.broadcasted_iota(jnp.int32, shape, dim).astype(F32)


def greet(peers):
    barrier = pltpu.get_barrier_semaphore()
    total = 0
    for device, present in peers:
        if present is None:
            pl.semaphore_signal(barrier, inc=1, device_id=device, device_id_type=MESH)
            total = total + 1
        else:

            @pl.when(present)
            def _(device=device):
                pl.semaphore_signal(barrier, inc=1, device_id=device, device_id_type=MESH)

            total = total + present.astype(jnp.int32)
    pl.semaphore_wait(barrier, total)


def schedule(tier, lists, my_z, table_ref):
    caps, _, _, left_out, known = tier
    block = iota((1, PLANES * LOCAL), 1)
    asker_z = jnp.floor(iota((PLANES * PLANE, 1), 0) / PLANE)
    top = jnp.full((1, PLANES * LOCAL), -1.0, F32)
    low = jnp.full((1, PLANES * LOCAL), 8.0, F32)
    for j in range(REQ):
        hit = lists[:, j : j + 1] == block
        top = jnp.maximum(top, jnp.max(jnp.where(hit, asker_z, -1.0), axis=0, keepdims=True))
        low = jnp.minimum(low, jnp.min(jnp.where(hit, asker_z, 8.0), axis=0, keepdims=True))
    kind = jnp.full((8, 1), -1.0, F32)
    for i, reach in enumerate(REACHES):
        kind = jnp.where(iota((8, 1), 0) == i, reach, kind)
    turns = [(way, step) for step in range(PLANES - 1) for way in range(2)]

    def plane(way, step):
        return step if way == 0 else PLANES - 1 - step

    reaches = {}
    for way in range(2):
        for step in range(PLANES):
            z = plane(way, step)
            span = slice(z * LOCAL, (z + 1) * LOCAL)
            reaches[way, step] = top[:, span] if way == 0 else (PLANES - 1) - low[:, span]
    stacked = [
        jnp.concatenate([reaches[way, step] for step in range(PLANES)], axis=0) for way in range(2)
    ]
    step_of_row = iota((PLANES, LOCAL), 0)
    fits = jnp.ones((1, 1), F32)
    heights = {}
    for way in range(2):
        height = jnp.zeros((1, 1), F32)
        for step in range(PLANES - 1):
            over = (stacked[way] > step) & (step_of_row <= step)
            load = jnp.sum(
                jnp.sum(over.astype(F32), axis=1, keepdims=True), axis=0, keepdims=True
            )
            height = jnp.maximum(height, load)
            heights[way, step] = height
            fits = fits * (load <= caps[min(step, 3)]).astype(F32)

    kinds = jnp.concatenate(
        [
            ((reaches[turn] == kind) & (reaches[turn] > turn[1])).astype(F32)
            for turn in turns
        ],
        axis=0,
    )
    many = 8 * len(turns)
    before_lane = (iota((LOCAL, LOCAL), 0) < iota((LOCAL, LOCAL), 1)).astype(BF16)
    turn_row, turn_column = (
        jnp.floor(iota((many, many), 0) / 8),
        jnp.floor(iota((many, many), 1) / 8),
    )
    before_kind = (
        (turn_row == turn_column) & (iota((many, many), 1) < iota((many, many), 0))
    ).astype(BF16)
    of_kind = jnp.dot(kinds.astype(BF16), before_lane, preferred_element_type=F32)
    earlier = jnp.dot(
        before_kind,
        jnp.broadcast_to(jnp.sum(kinds, axis=1, keepdims=True), (many, HD)).astype(BF16),
        preferred_element_type=F32,
    )[:, 0:1]
    ranked = kinds * (of_kind + earlier)
    ranks = {
        turn: jnp.sum(ranked[8 * i : 8 * i + 8], axis=0, keepdims=True)
        for i, turn in enumerate(turns)
    }

    eye = (iota((LOCAL, LOCAL), 0) == iota((LOCAL, LOCAL), 1)).astype(BF16)

    def as_columns(rows):
        return lax.dot_general(
            eye, rows.astype(BF16), (((1,), (1,)), ((), ())), preferred_element_type=F32
        )

    reach_columns = [as_columns(rows) for rows in stacked]
    rank_columns = as_columns(
        jnp.concatenate([ranks[turn] for turn in turns] + [ranks[turns[0]]] * 2, axis=0)
    )
    place_column = iota((LOCAL, 1), 0)
    after_lane = (iota((known, known), 0) > iota((known, known), 1)).astype(BF16)
    slot_row = iota((1, known), 1)
    nothing = jnp.full((1, known), -1.0, F32)
    ends, helds = [nothing, nothing], [nothing, nothing]
    injected, arrived = [nothing, nothing], [nothing, nothing]
    for i, (way, step) in enumerate(turns):
        z = plane(way, step)
        reach = reach_columns[way][:, step : step + 1]
        rank = jnp.where(reach > step, rank_columns[:, i : i + 1], -2.0)
        end = ends[way]
        free = (end <= step) & (slot_row < heights[way, step])
        free_rank = jnp.dot(
            jnp.broadcast_to(free.astype(F32), (8, known)).astype(BF16),
            after_lane,
            preferred_element_type=F32,
        )[0:1]
        pair = rank == jnp.where(free, free_rank, -1.0)
        code = jnp.sum(
            jnp.where(pair, 1.0 + place_column + LOCAL * reach, 0.0), axis=0, keepdims=True
        )
        taken = code > 0.5
        new_end = jnp.floor((code - 1.0) / LOCAL)
        new_block = code - 1.0 - LOCAL * new_end
        helds[way] = jnp.where(
            taken, z * LOCAL + new_block, jnp.where(end <= step, -1.0, helds[way])
        )
        ends[way] = jnp.where(taken, new_end, end)
        injected[way] = jnp.where(my_z == z, jnp.where(taken, new_block, -1.0), injected[way])
        arrived[way] = jnp.where(my_z == plane(way, step + 1), helds[way], arrived[way])
        if step == PLANES - 2:
            lowest = jnp.min(
                jnp.where(ends[way] > step, slot_row, known), axis=1, keepdims=True
            )
            fits = fits * (lowest >= left_out).astype(F32)
    in_up, in_down = injected
    at_up, at_down = arrived
    rows = iota((8, HD), 0)
    out = jnp.where(rows == 4, fits, 0.0)
    for i in range(known // HD):
        out = jnp.where(rows == i, in_up[:, i * HD : (i + 1) * HD], out)
        out = jnp.where(rows == 2 + i, in_down[:, i * HD : (i + 1) * HD], out)
    table_ref[1] = out.astype(jnp.int32)

    slot = iota((1, known), 1)
    mine = jnp.zeros((PLANE, HD), F32)
    for z in range(PLANES):
        mine = jnp.where(my_z == z, lists[z * PLANE : (z + 1) * PLANE], mine)
    place = jnp.zeros((PLANE, HD), F32)
    lanes = iota((PLANE, HD), 1)
    z_here = my_z.astype(F32)
    for j in range(REQ):
        wanted = mine[:, j : j + 1]
        owner_z = jnp.floor(wanted / LOCAL)
        slot_up = jnp.sum(jnp.where(at_up == wanted, slot, 0.0), axis=1, keepdims=True)
        slot_down = jnp.sum(jnp.where(at_down == wanted, slot, 0.0), axis=1, keepdims=True)
        found = jnp.where(owner_z == z_here, wanted - LOCAL * owner_z, LOCAL + known + slot_down)
        found = jnp.where(owner_z < z_here, LOCAL + slot_up, found)
        place = jnp.where(lanes == j, found, place)
    table_ref[0] = place.astype(jnp.int32)


def attend_kernel(tier, *refs):
    caps, group, lags, left_out, known = tier
    slots = caps[-1]
    groups = slots // group
    ids_ref, gate_hbm, gain_hbm, q_hbm, k_ref, v_ref, mk_ref, mv_ref = refs[:8]
    out_ref, fits_ref = refs[8:10]
    rest = list(refs[10:])

    def take(n):
        got = rest[:n]
        del rest[:n]
        return got

    table_out, table, line, lists = take(4)
    gate_ref, q_ref, gain_ref, near_k, near_v, mixed = take(6)
    pools, ups, downs = take(CHUNKS), take(CHUNKS), take(CHUNKS)
    ups_out, downs_out = take(CHUNKS), take(CHUNKS)
    parts_out, parts = take(CHUNKS), take(CHUNKS)
    squares_out, squares, edge_ref, edge_in = take(4)
    table_sem, send1, recv1, send2, recv2, send_a, recv_a, edge_send, edge_recv = take(9)
    (
        pool_sem,
        own_sem,
        halo_send,
        halo_recv,
        up_send,
        up_recv,
        down_send,
        down_recv,
        part_send,
        part_recv,
        sq_send,
        sq_recv,
        edge_sem,
        pass_send,
        pass_recv,
    ) = rest

    me = lax.axis_index("ctx")
    mem = lax.axis_index("mem")
    z, p = me // PLANE, me % PLANE
    x, core = p // 2, p % 2

    def in_plane(r):
        return {"ctx": z * PLANE + (p + r) % PLANE}

    def on_line(r):
        return {"ctx": ((z + r) % PLANES) * PLANE + p}

    def mem_peer(r):
        return {"mem": (mem + r) % 8}

    above, below = {"ctx": me + PLANE}, {"ctx": me - PLANE}
    loads = [
        pltpu.make_async_copy(k_ref, near_k.at[pl.ds(2 * TOK, TOK)], own_sem.at[0]),
        pltpu.make_async_copy(v_ref, near_v.at[pl.ds(2 * TOK, TOK)], own_sem.at[1]),
        pltpu.make_async_copy(q_hbm, q_ref, own_sem.at[2]),
        pltpu.make_async_copy(gate_hbm, gate_ref, own_sem.at[3]),
        pltpu.make_async_copy(gain_hbm, gain_ref, own_sem.at[4]),
    ]
    for load in loads:
        load.start()

    greet(
        [(in_plane(r), None) for r in range(1, 8)]
        + [(mem_peer(r), None) for r in range(1, 8)]
        + [(on_line(r), None) for r in range(1, 8)]
    )

    def edge_copy():
        return pltpu.make_async_remote_copy(
            src_ref=edge_ref,
            dst_ref=edge_in,
            send_sem=edge_sem.at[0],
            recv_sem=edge_sem.at[1],
            device_id=above,
            device_id_type=MESH,
        )

    def edge_here():
        for source in range(2):

            @pl.when((z < PLANES - 1) & (p == 6 + source))
            def _(source=source):
                edge_own(0).wait()

            @pl.when((z < PLANES - 1) & (p != 6 + source))
            def _(source=source):
                edge_arrival(source).wait_recv()

        @pl.when(z < PLANES - 1)
        def _():
            edge_copy().start()

    def passed(source, to):
        near = near_v if source % 2 else near_k
        columns = pl.ds(source // 2 * HD, HD)
        came = edge_in if to == 0 else edge_in.at[pl.ds(TOK, TOK)]
        return came, near.at[pl.ds(0, 2 * TOK if to == 0 else TOK), columns]

    def pass_copy(source, to):
        came, near = passed(source, to)
        return pltpu.make_async_remote_copy(
            src_ref=came,
            dst_ref=near,
            send_sem=pass_send.at[to],
            recv_sem=pass_recv.at[source],
            device_id={"ctx": z * PLANE + to},
            device_id_type=MESH,
        )

    def pass_own(source):
        came, near = passed(source, source)
        return pltpu.make_async_copy(came, near, pass_recv.at[source])

    def each_pass(source, remote, local):
        for to in range(2):
            if source == to:
                local(source)
            else:
                remote(source, to)

    def pass_on():
        edge_copy().wait_recv()
        for source in range(PLANE):

            @pl.when(p == source)
            def _(source=source):
                each_pass(
                    source,
                    lambda s, t: pass_copy(s, t).start(),
                    lambda s: pass_own(s).start(),
                )

    lanes = lax.broadcasted_iota(jnp.int32, (8, HD), 1)
    row = jnp.zeros((8, HD), jnp.int32)
    for j in range(REQ):
        row = jnp.where(lanes == j, ids_ref[j // 4, j % 4], row)
    line[p] = row

    def copy1(r):
        return pltpu.make_async_remote_copy(
            src_ref=line.at[p],
            dst_ref=line.at[p],
            send_sem=send1.at[r],
            recv_sem=recv1.at[p],
            device_id=in_plane(r),
            device_id_type=MESH,
        )

    def arrival1(r):
        q = (p + r) % PLANE
        return pltpu.make_async_remote_copy(
            src_ref=line.at[q],
            dst_ref=line.at[q],
            send_sem=send1.at[r],
            recv_sem=recv1.at[q],
            device_id=in_plane(r),
            device_id_type=MESH,
        )

    for r in range(1, 8):
        copy1(r).start()

    def part(r, chunk, ref):
        q = (p + r) % PLANE
        return ref.at[:, pl.ds(chunk * ROWS, ROWS), pl.ds(pl.multiple_of((q // 2) * HD, HD), HD)]

    def copy_a(r, chunk, ref):
        return pltpu.make_async_remote_copy(
            src_ref=part(r, chunk, ref),
            dst_ref=pools[chunk].at[pl.ds(p * 8, 8)],
            send_sem=send_a.at[chunk, r],
            recv_sem=recv_a.at[chunk, p],
            device_id=in_plane(r),
            device_id_type=MESH,
        )

    def arrival_a(r, chunk):
        q = (p + r) % PLANE
        return pltpu.make_async_remote_copy(
            src_ref=part(r, chunk, mk_ref),
            dst_ref=pools[chunk].at[pl.ds(q * 8, 8)],
            send_sem=send_a.at[chunk, r],
            recv_sem=recv_a.at[chunk, q],
            device_id=in_plane(r),
            device_id_type=MESH,
        )

    def own_a(ref, chunk):
        return pltpu.make_async_copy(
            part(0, chunk, ref), pools[chunk].at[pl.ds(p * 8, 8)], pool_sem.at[chunk]
        )

    def spread_blocks(chunk):
        for r in (4, 3, 5, 2, 6, 1, 7):
            to_core = (core + r) % 2

            @pl.when(to_core == 0)
            def _():
                copy_a(r, chunk, mk_ref).start()

            @pl.when(to_core == 1)
            def _():
                copy_a(r, chunk, mv_ref).start()

        @pl.when(core == 0)
        def _():
            own_a(mk_ref, chunk).start()

        @pl.when(core == 1)
        def _():
            own_a(mv_ref, chunk).start()

    def blocks_here(chunk):
        own_a(mk_ref, chunk).wait()
        for r in range(1, 8):
            arrival_a(r, chunk).wait_recv()

    spread_blocks(0)

    def edge_part(q):
        ref = v_ref if q % 2 else k_ref
        return ref.at[:, pl.ds(q // 2 * HD, HD)]

    def spread_edge(q):
        return pltpu.make_async_remote_copy(
            src_ref=edge_part(q),
            dst_ref=edge_ref.at[pl.ds(core * TOK, TOK)],
            send_sem=edge_send.at[q],
            recv_sem=edge_recv.at[core],
            device_id={"ctx": z * PLANE + q},
            device_id_type=MESH,
        )

    def edge_arrival(source):
        return pltpu.make_async_remote_copy(
            src_ref=edge_part(0),
            dst_ref=edge_ref.at[pl.ds(source * TOK, TOK)],
            send_sem=edge_send.at[0],
            recv_sem=edge_recv.at[source],
            device_id=in_plane(1),
            device_id_type=MESH,
        )

    def edge_own(q):
        return pltpu.make_async_copy(
            edge_part(q), edge_ref.at[pl.ds(core * TOK, TOK)], pool_sem.at[CHUNKS]
        )

    sends_edge = (x == 3) & (z < PLANES - 1)
    for q in range(PLANE):

        @pl.when(sends_edge & (p != q))
        def _(q=q):
            spread_edge(q).start()

        @pl.when(sends_edge & (p == q))
        def _(q=q):
            edge_own(q).start()

    for chunk in range(1, CHUNKS):
        spread_blocks(chunk)
    def halo(d, which):
        ref, near = ((k_ref, near_k), (v_ref, near_v))[which]
        return pltpu.make_async_remote_copy(
            src_ref=ref,
            dst_ref=near.at[pl.ds((2 - d) * TOK, TOK)],
            send_sem=halo_send.at[2 * d - 2 + which],
            recv_sem=halo_recv.at[2 * d - 2 + which],
            device_id={"ctx": me + d},
            device_id_type=MESH,
        )

    for d in (1, 2):

        @pl.when(p + d < PLANE)
        def _():
            halo(d, 0).start()
            halo(d, 1).start()

        @pl.when((z == 0) & (p < d))
        def _():
            near_k[pl.ds((2 - d) * TOK, TOK)] = jnp.zeros((TOK, HEADS_HERE * HD), BF16)
            near_v[pl.ds((2 - d) * TOK, TOK)] = jnp.zeros((TOK, HEADS_HERE * HD), BF16)

    for r in range(1, 8):
        arrival1(r).wait_recv()
    rows = lax.broadcasted_iota(jnp.int32, (8, HD), 0)
    whole = jnp.zeros((8, HD), jnp.int32)
    for q in range(PLANE):
        whole = jnp.where(rows == q, line[q], whole)
    lists[z] = whole

    def copy2(r):
        return pltpu.make_async_remote_copy(
            src_ref=lists.at[z],
            dst_ref=lists.at[z],
            send_sem=send2.at[r],
            recv_sem=recv2.at[z],
            device_id=on_line(r),
            device_id_type=MESH,
        )

    def arrival2(r):
        q = (z + r) % PLANES
        return pltpu.make_async_remote_copy(
            src_ref=lists.at[q],
            dst_ref=lists.at[q],
            send_sem=send2.at[r],
            recv_sem=recv2.at[q],
            device_id=on_line(r),
            device_id_type=MESH,
        )

    for r in range(1, 8):
        copy2(r).start()
    for r in range(1, 8):
        arrival2(r).wait_recv()
    schedule(tier, lists[...].reshape(PLANES * PLANE, HD).astype(F32), z, table_out)
    to_scalars = pltpu.make_async_copy(table_out, table, table_sem)
    to_scalars.start()
    to_scalars.wait()
    fits_ref[0] = table[1, 4, 0]
    edge_here()
    for load in loads:
        load.wait()
    blocks_here(0)

    caps_g = [c // group for c in caps]

    def cap_at(step):
        value = jnp.int32(caps_g[3])
        for i in (2, 1, 0):
            value = jnp.where(step == i, caps_g[i], value)
        return value

    def floor_at(step):
        return jnp.where(step >= PLANES - 2, left_out // group, 0)

    def lag_at(step):
        value = jnp.int32(0)
        for i in range(4):
            value = jnp.where(step == 4 + i, lags[i], value)
        return value

    def conveyor(k, step, target, pool, into, onward, send, recv, row):
        cap = cap_at(step)
        position = jnp.where(step <= 3, k + groups - cap, k - lag_at(step))
        inside = (position >= 0) & (position < CHUNKS * groups)
        at = jnp.maximum(position, 0)
        chunk = at // groups
        g = groups - 1 - at % groups
        active = inside & (g < cap)
        incoming = (step > 0) & (g < cap_at(step - 1)) & (g >= floor_at(step - 1))

        def copy(c):
            span = pl.ds(g * group, group)
            return pltpu.make_async_remote_copy(
                src_ref=onward[c].at[span],
                dst_ref=into[c].at[span],
                send_sem=send.at[c, g],
                recv_sem=recv.at[c, g],
                device_id=target,
                device_id_type=MESH,
            )

        for c in range(CHUNKS):

            @pl.when(active & (chunk == c))
            def _(c=c):
                @pl.when(incoming)
                def _():
                    copy(c).wait_recv()

                @pl.when((step < PLANES - 1) & (g >= floor_at(step)))
                def _():
                    for i in range(group):
                        slot = g * group + i
                        inject = table[1, row + slot // HD, slot % HD]
                        local = pool[c][jnp.clip(inject, 0, LOCAL - 1)]
                        onward[c][slot] = jnp.where(inject >= 0, local, into[c][slot])
                    copy(c).start()

    def part_copy(c, r):
        q = (p + r) % PLANE
        return pltpu.make_async_remote_copy(
            src_ref=parts_out[c].at[q],
            dst_ref=parts[c].at[p],
            send_sem=part_send.at[c, r],
            recv_sem=part_recv.at[c, p],
            device_id=in_plane(r),
            device_id_type=MESH,
        )

    def part_arrival(c, r):
        q = (p + r) % PLANE
        return pltpu.make_async_remote_copy(
            src_ref=parts_out[c].at[q],
            dst_ref=parts[c].at[q],
            send_sem=part_send.at[c, r],
            recv_sem=part_recv.at[c, q],
            device_id=in_plane(r),
            device_id_type=MESH,
        )

    def hand_out(c):
        def pick(q, j):
            place = table[0, q, j]
            own = pools[c][jnp.clip(place, 0, LOCAL - 1)]
            from_below = ups[c][jnp.clip(place - LOCAL, 0, slots - 1)]
            from_above = downs[c][jnp.clip(place - LOCAL - known, 0, slots - 1)]
            return jnp.where(
                place < LOCAL, own, jnp.where(place < LOCAL + known, from_below, from_above)
            )

        for r in (4, 3, 5, 2, 6, 1, 7):
            q = (p + r) % PLANE
            for j in range(REQ):
                parts_out[c][q, j] = pick(q, j)
            part_copy(c, r).start()
        for j in range(REQ):
            parts[c][p, j] = pick(p, j)

    def window_piece(head, tile):
        columns = pl.ds(pl.multiple_of(head * HD, HD), HD)
        rows = pl.ds(pl.multiple_of(tile * 128, 128), 128)
        near = pl.ds(pl.multiple_of(tile * 128, 128), 640)
        scores = lax.dot_general(
            q_ref[rows, columns],
            near_k[near, columns],
            (((1,), (1,)), ((), ())),
            preferred_element_type=F32,
        )
        key = lax.broadcasted_iota(jnp.int32, (128, 640), 1)
        ahead = key - lax.broadcasted_iota(jnp.int32, (128, 640), 0)
        first = me * TOK - 2 * TOK + tile * 128
        allowed = (ahead > 0) & (ahead <= 512) & (key >= -first)
        scores = jnp.where(allowed, scores * SCALE, -jnp.inf)
        weights = jnp.exp(scores - jnp.max(scores, axis=1, keepdims=True))
        total = jnp.sum(weights, axis=1, keepdims=True)
        product = jnp.dot(weights.astype(BF16), near_v[near, columns], preferred_element_type=F32)
        mixed[rows, columns] = product / total

    steps = CHUNKS * groups + max(lags[2], lags[3] - left_out // group)
    far = jnp.maximum(z, PLANES - 1 - z)
    far = lag_at(far) - floor_at(far - 1)
    pieces = 2 * HEADS_HERE
    pass_step = 5
    early, every, first_piece = 3, 2, groups + 6

    def step_body(k, carry):
        for chunk in range(1, CHUNKS):

            @pl.when(k == (chunk - 1) * groups + caps_g[0])
            def _(chunk=chunk):
                blocks_here(chunk)

        conveyor(k, z, above, pools, ups, ups_out, up_send, up_recv, 0)
        conveyor(k, PLANES - 1 - z, below, pools, downs, downs_out, down_send, down_recv, 2)
        for c in range(CHUNKS):

            @pl.when(k == (c + 1) * groups - 1 + far)
            def _(c=c):
                hand_out(c)

        @pl.when((k == pass_step) & (z > 0))
        def _():
            pass_on()

        @pl.when(k == first_piece)
        def _():
            for d in (1, 2):

                @pl.when(p >= d)
                def _():
                    halo(d, 0).wait_recv()
                    halo(d, 1).wait_recv()

            for to in range(2):

                @pl.when((z > 0) & (p == to))
                def _(to=to):
                    for source in range(PLANE):
                        if source == to:
                            pass_own(source).wait()
                        else:
                            pass_copy(source, to).wait_recv()

        since = k - first_piece
        piece = jnp.maximum(since, 0) // every

        @pl.when((since >= 0) & (since % every == 0) & (piece < early))
        def _():
            window_piece(piece // 2, piece % 2)

        return carry

    lax.fori_loop(0, steps, step_body, 0)

    def late_piece(piece, carry):
        window_piece(piece // 2, piece % 2)
        return carry

    lax.fori_loop(early, pieces, late_piece, 0)

    for c in range(CHUNKS):
        for r in range(1, 8):
            part_arrival(c, r).wait_recv()

    opened = 1.0 / (1.0 + jnp.exp(-gate_ref[...]))
    eye = lax.broadcasted_iota(jnp.int32, (128, 128), 0) == lax.broadcasted_iota(
        jnp.int32, (128, 128), 1
    )
    for tile in range(2):
        rows = pl.ds(tile * 128, 128)
        total_square = jnp.zeros((128, 1), F32)
        for head in range(HEADS_HERE):
            columns = pl.ds(head * HD, HD)
            keys = [parts[c][2 * head, 4 * tile : 4 * tile + 4].reshape(4 * ROWS, HD) for c in range(CHUNKS)]
            vals = [parts[c][2 * head + 1, 4 * tile : 4 * tile + 4].reshape(4 * ROWS, HD) for c in range(CHUNKS)]
            scores = lax.dot_general(
                q_ref[rows, columns],
                jnp.concatenate(keys, axis=0),
                (((1,), (1,)), ((), ())),
                preferred_element_type=F32,
            ) * SCALE
            weights = jnp.exp(scores - jnp.max(scores, axis=1, keepdims=True))
            total = jnp.sum(weights, axis=1, keepdims=True)
            product = jnp.dot(
                weights.astype(BF16), jnp.concatenate(vals, axis=0), preferred_element_type=F32
            )
            share = opened[:, head : head + 1]
            both = share * (product / total) + (1.0 - share) * mixed[rows, columns]
            mixed[rows, columns] = both
            total_square += jnp.sum(both * both, axis=1, keepdims=True)
        squares_out[pl.ds(tile * 8, 8)] = jnp.broadcast_to(
            jnp.sum(jnp.where(eye, total_square, 0.0), axis=0, keepdims=True), (8, 128)
        )

    def square_copy(r):
        return pltpu.make_async_remote_copy(
            src_ref=squares_out,
            dst_ref=squares.at[mem],
            send_sem=sq_send.at[r],
            recv_sem=sq_recv.at[mem],
            device_id=mem_peer(r),
            device_id_type=MESH,
        )

    def square_arrival(r):
        return pltpu.make_async_remote_copy(
            src_ref=squares_out,
            dst_ref=squares.at[(mem + r) % 8],
            send_sem=sq_send.at[r],
            recv_sem=sq_recv.at[(mem + r) % 8],
            device_id=mem_peer(r),
            device_id_type=MESH,
        )

    for r in (4, 1, 2, 3, 5, 6, 7):
        square_copy(r).start()
    squares[mem] = squares_out[...]
    for r in range(1, 8):
        square_arrival(r).wait_recv()
    summed = squares[0]
    for m in range(1, 8):
        summed = summed + squares[m]
    for tile in range(2):
        rows = pl.ds(tile * 128, 128)
        column = jnp.sum(
            jnp.where(eye, summed[tile * 8 : tile * 8 + 1], 0.0), axis=1, keepdims=True
        )
        factor = lax.rsqrt(column / FEATURES + 1e-6)
        out_ref[rows] = (mixed[rows] * gain_ref[...] * factor).astype(BF16)

    for r in range(1, 8):
        square_copy(r).wait_send()
        for c in range(CHUNKS):
            part_copy(c, r).wait_send()
        copy1(r).wait_send()
        copy2(r).wait_send()
        for chunk in range(CHUNKS):
            copy_a(r, chunk, mk_ref).wait_send()
    for q in range(PLANE):

        @pl.when(sends_edge & (p != q))
        def _(q=q):
            spread_edge(q).wait_send()

    for d in (1, 2):

        @pl.when(p + d < PLANE)
        def _():
            halo(d, 0).wait_send()
            halo(d, 1).wait_send()

    @pl.when(z < PLANES - 1)
    def _():
        edge_copy().wait_send()

    for source in range(PLANE):

        @pl.when((z > 0) & (p == source))
        def _(source=source):
            each_pass(source, lambda s, t: pass_copy(s, t).wait_send(), lambda s: None)

    for step, into, onward, send, recv, target in (
        (z, ups, ups_out, up_send, up_recv, above),
        (PLANES - 1 - z, downs, downs_out, down_send, down_recv, below),
    ):

        @pl.when(step < PLANES - 1)
        def _():
            def sent(g, carry):
                span = pl.ds(g * group, group)
                for c in range(CHUNKS):
                    pltpu.make_async_remote_copy(
                        src_ref=onward[c].at[span],
                        dst_ref=into[c].at[span],
                        send_sem=send.at[c, g],
                        recv_sem=recv.at[c, g],
                        device_id=target,
                        device_id_type=MESH,
                    ).wait_send()
                return carry

            lax.fori_loop(floor_at(step), cap_at(step), sent, 0)


def attend(tier, collective_id, ids, gate, gain, q, k, v, mk, mv):
    slots = tier[0][-1]
    groups = slots // tier[1]
    ring = [pltpu.VMEM((slots, ROWS, HD), BF16)] * CHUNKS
    hand = [pltpu.VMEM((PLANE, REQ, ROWS, HD), BF16)] * CHUNKS
    dma = pltpu.SemaphoreType.DMA
    return pl.pallas_call(
        functools.partial(attend_kernel, tier),
        out_shape=[
            jax.ShapeDtypeStruct((TOK, HEADS_HERE * HD), BF16),
            jax.ShapeDtypeStruct((1,), jnp.int32),
        ],
        in_specs=[SMEM] + [HBM] * 7,
        out_specs=[VMEM, SMEM],
        scratch_shapes=[
            pltpu.VMEM((2, 8, HD), jnp.int32),
            pltpu.SMEM((2, 8, HD), jnp.int32),
            pltpu.VMEM((PLANE, 8, HD), jnp.int32),
            pltpu.VMEM((PLANES, 8, HD), jnp.int32),
            pltpu.VMEM((1, HEADS_HERE), F32),
            pltpu.VMEM((TOK, HEADS_HERE * HD), BF16),
            pltpu.VMEM((1, HEADS_HERE * HD), F32),
            pltpu.VMEM((3 * TOK, HEADS_HERE * HD), BF16),
            pltpu.VMEM((3 * TOK, HEADS_HERE * HD), BF16),
            pltpu.VMEM((TOK, HEADS_HERE * HD), F32),
            *[pltpu.VMEM((LOCAL, ROWS, HD), BF16)] * CHUNKS,
            *ring,
            *ring,
            *ring,
            *ring,
            *hand,
            *hand,
            pltpu.VMEM((16, HD), F32),
            pltpu.VMEM((8, 16, HD), F32),
            pltpu.VMEM((2 * TOK, HD), BF16),
            pltpu.VMEM((2 * TOK, HD), BF16),
            dma(()),
            dma((8,)),
            dma((8,)),
            dma((8,)),
            dma((8,)),
            dma((CHUNKS, 8)),
            dma((CHUNKS, 8)),
            dma((8,)),
            dma((2,)),
            dma((CHUNKS + 1,)),
            dma((5,)),
            dma((4,)),
            dma((4,)),
            dma((CHUNKS, groups)),
            dma((CHUNKS, groups)),
            dma((CHUNKS, groups)),
            dma((CHUNKS, groups)),
            dma((CHUNKS, 8)),
            dma((CHUNKS, 8)),
            dma((8,)),
            dma((8,)),
            dma((2,)),
            dma((2,)),
            dma((8,)),
        ],
        compiler_params=pltpu.CompilerParams(
            collective_id=collective_id, has_side_effects=True, vmem_limit_bytes=60 << 20
        ),
        name="attend_" + str(slots),
    )(ids, gate, gain, q, k, v, mk, mv)


def shards(queries, keys, values, memory_keys, memory_values, retrieval, gate, gain):
    operands = (
        retrieval,
        gate.reshape(1, -1),
        gain.reshape(1, -1),
        queries,
        keys,
        values,
        memory_keys,
        memory_values,
    )
    out, fits = attend(SHORT, 0, *operands)
    return lax.cond(
        fits[0] > 0,
        lambda out, *_: out,
        lambda _, *operands: attend(LONG, 1, *operands)[0],
        out,
        *operands,
    )


def solution(mesh):
    in_specs = (
        P("ctx", "mem"),
        P("ctx", "mem"),
        P("ctx", "mem"),
        P("ctx", None, "mem"),
        P("ctx", None, "mem"),
        P("ctx", None),
        P("mem"),
        P("mem"),
    )
    return jax.shard_map(
        shards, mesh=mesh, in_specs=in_specs, out_specs=P("ctx", "mem"), check_vma=False
    )
```

```python
import functools
import math

import jax
import jax.numpy as jnp
from jax import lax
from jax.experimental import pallas as pl
from jax.experimental.pallas import tpu as pltpu
from jax.sharding import PartitionSpec as P

MESH = pl.DeviceIdType.MESH
HBM = pl.BlockSpec(memory_space=pltpu.HBM)
VMEM = pl.BlockSpec(memory_space=pltpu.VMEM)
SMEM = pl.BlockSpec(memory_space=pltpu.SMEM)
F32 = jnp.float32
BF16 = jnp.bfloat16

HD = 128
HEADS_HERE = 4
FEATURES = 4096
PLANES = 8
PLANE = 8
REQ = 8
BLK = 64
LOCAL = 64
TOK = 256
CHUNKS = 2
ROWS = BLK // CHUNKS
SCALE = 1.0 / math.sqrt(HD)

SHORT = ((56, 80, 104, 112), 8, (3, 7, 10, 11), 16, 128)
LONG = ((64, 128, 192, 256), 16, (2, 4, 6, 8), 0, 256)
REACHES = (7, 1, 2, 3, 4, 5, 6)


def iota(shape, dim):
    return lax.broadcasted_iota(jnp.int32, shape, dim).astype(F32)


def greet(peers):
    barrier = pltpu.get_barrier_semaphore()
    total = 0
    for device, present in peers:
        if present is None:
            pl.semaphore_signal(barrier, inc=1, device_id=device, device_id_type=MESH)
            total = total + 1
        else:

            @pl.when(present)
            def _(device=device):
                pl.semaphore_signal(barrier, inc=1, device_id=device, device_id_type=MESH)

            total = total + present.astype(jnp.int32)
    pl.semaphore_wait(barrier, total)


def schedule(tier, lists, my_z, table_ref):
    caps, _, _, left_out, known = tier
    block = iota((1, PLANES * LOCAL), 1)
    asker_z = jnp.floor(iota((PLANES * PLANE, 1), 0) / PLANE)
    top = jnp.full((1, PLANES * LOCAL), -1.0, F32)
    low = jnp.full((1, PLANES * LOCAL), 8.0, F32)
    for j in range(REQ):
        hit = lists[:, j : j + 1] == block
        top = jnp.maximum(top, jnp.max(jnp.where(hit, asker_z, -1.0), axis=0, keepdims=True))
        low = jnp.minimum(low, jnp.min(jnp.where(hit, asker_z, 8.0), axis=0, keepdims=True))
    kind = jnp.full((8, 1), -1.0, F32)
    for i, reach in enumerate(REACHES):
        kind = jnp.where(iota((8, 1), 0) == i, reach, kind)
    turns = [(way, step) for step in range(PLANES - 1) for way in range(2)]

    def plane(way, step):
        return step if way == 0 else PLANES - 1 - step

    reaches = {}
    for way in range(2):
        for step in range(PLANES):
            z = plane(way, step)
            span = slice(z * LOCAL, (z + 1) * LOCAL)
            reaches[way, step] = top[:, span] if way == 0 else (PLANES - 1) - low[:, span]
    stacked = [
        jnp.concatenate([reaches[way, step] for step in range(PLANES)], axis=0) for way in range(2)
    ]
    step_of_row = iota((PLANES, LOCAL), 0)
    fits = jnp.ones((1, 1), F32)
    heights = {}
    for way in range(2):
        height = jnp.zeros((1, 1), F32)
        for step in range(PLANES - 1):
            over = (stacked[way] > step) & (step_of_row <= step)
            load = jnp.sum(
                jnp.sum(over.astype(F32), axis=1, keepdims=True), axis=0, keepdims=True
            )
            height = jnp.maximum(height, load)
            heights[way, step] = height
            fits = fits * (load <= caps[min(step, 3)]).astype(F32)

    kinds = jnp.concatenate(
        [
            ((reaches[turn] == kind) & (reaches[turn] > turn[1])).astype(F32)
            for turn in turns
        ],
        axis=0,
    )
    many = 8 * len(turns)
    before_lane = (iota((LOCAL, LOCAL), 0) < iota((LOCAL, LOCAL), 1)).astype(BF16)
    turn_row, turn_column = (
        jnp.floor(iota((many, many), 0) / 8),
        jnp.floor(iota((many, many), 1) / 8),
    )
    before_kind = (
        (turn_row == turn_column) & (iota((many, many), 1) < iota((many, many), 0))
    ).astype(BF16)
    of_kind = jnp.dot(kinds.astype(BF16), before_lane, preferred_element_type=F32)
    earlier = jnp.dot(
        before_kind,
        jnp.broadcast_to(jnp.sum(kinds, axis=1, keepdims=True), (many, HD)).astype(BF16),
        preferred_element_type=F32,
    )[:, 0:1]
    ranked = kinds * (of_kind + earlier)
    ranks = {
        turn: jnp.sum(ranked[8 * i : 8 * i + 8], axis=0, keepdims=True)
        for i, turn in enumerate(turns)
    }

    eye = (iota((LOCAL, LOCAL), 0) == iota((LOCAL, LOCAL), 1)).astype(BF16)

    def as_columns(rows):
        return lax.dot_general(
            eye, rows.astype(BF16), (((1,), (1,)), ((), ())), preferred_element_type=F32
        )

    reach_columns = [as_columns(rows) for rows in stacked]
    rank_columns = as_columns(
        jnp.concatenate([ranks[turn] for turn in turns] + [ranks[turns[0]]] * 2, axis=0)
    )
    place_column = iota((LOCAL, 1), 0)
    after_lane = (iota((known, known), 0) > iota((known, known), 1)).astype(BF16)
    slot_row = iota((1, known), 1)
    nothing = jnp.full((1, known), -1.0, F32)
    ends, helds = [nothing, nothing], [nothing, nothing]
    injected, arrived = [nothing, nothing], [nothing, nothing]
    for i, (way, step) in enumerate(turns):
        z = plane(way, step)
        reach = reach_columns[way][:, step : step + 1]
        rank = jnp.where(reach > step, rank_columns[:, i : i + 1], -2.0)
        end = ends[way]
        free = (end <= step) & (slot_row < heights[way, step])
        free_rank = jnp.dot(
            jnp.broadcast_to(free.astype(F32), (8, known)).astype(BF16),
            after_lane,
            preferred_element_type=F32,
        )[0:1]
        pair = rank == jnp.where(free, free_rank, -1.0)
        code = jnp.sum(
            jnp.where(pair, 1.0 + place_column + LOCAL * reach, 0.0), axis=0, keepdims=True
        )
        taken = code > 0.5
        new_end = jnp.floor((code - 1.0) / LOCAL)
        new_block = code - 1.0 - LOCAL * new_end
        helds[way] = jnp.where(
            taken, z * LOCAL + new_block, jnp.where(end <= step, -1.0, helds[way])
        )
        ends[way] = jnp.where(taken, new_end, end)
        injected[way] = jnp.where(my_z == z, jnp.where(taken, new_block, -1.0), injected[way])
        arrived[way] = jnp.where(my_z == plane(way, step + 1), helds[way], arrived[way])
        if step == PLANES - 2:
            lowest = jnp.min(
                jnp.where(ends[way] > step, slot_row, known), axis=1, keepdims=True
            )
            fits = fits * (lowest >= left_out).astype(F32)
    in_up, in_down = injected
    at_up, at_down = arrived
    rows = iota((8, HD), 0)
    out = jnp.where(rows == 4, fits, 0.0)
    for i in range(known // HD):
        out = jnp.where(rows == i, in_up[:, i * HD : (i + 1) * HD], out)
        out = jnp.where(rows == 2 + i, in_down[:, i * HD : (i + 1) * HD], out)
    table_ref[1] = out.astype(jnp.int32)

    slot = iota((1, known), 1)
    mine = jnp.zeros((PLANE, HD), F32)
    for z in range(PLANES):
        mine = jnp.where(my_z == z, lists[z * PLANE : (z + 1) * PLANE], mine)
    place = jnp.zeros((PLANE, HD), F32)
    lanes = iota((PLANE, HD), 1)
    z_here = my_z.astype(F32)
    for j in range(REQ):
        wanted = mine[:, j : j + 1]
        owner_z = jnp.floor(wanted / LOCAL)
        slot_up = jnp.sum(jnp.where(at_up == wanted, slot, 0.0), axis=1, keepdims=True)
        slot_down = jnp.sum(jnp.where(at_down == wanted, slot, 0.0), axis=1, keepdims=True)
        found = jnp.where(owner_z == z_here, wanted - LOCAL * owner_z, LOCAL + known + slot_down)
        found = jnp.where(owner_z < z_here, LOCAL + slot_up, found)
        place = jnp.where(lanes == j, found, place)
    table_ref[0] = place.astype(jnp.int32)


def attend_kernel(tier, *refs):
    caps, group, lags, left_out, known = tier
    slots = caps[-1]
    groups = slots // group
    ids_ref, gate_hbm, gain_hbm, q_hbm, k_ref, v_ref, mk_ref, mv_ref = refs[:8]
    out_ref, fits_ref = refs[8:10]
    rest = list(refs[10:])

    def take(n):
        got = rest[:n]
        del rest[:n]
        return got

    table_out, table, line, lists = take(4)
    gate_ref, q_ref, gain_ref, near_k, near_v, mixed = take(6)
    pools, ups, downs = take(CHUNKS), take(CHUNKS), take(CHUNKS)
    ups_out, downs_out = take(CHUNKS), take(CHUNKS)
    parts_out, parts = take(CHUNKS), take(CHUNKS)
    squares_out, squares, edge_ref, edge_in = take(4)
    table_sem, send1, recv1, send2, recv2, send_a, recv_a, edge_send, edge_recv = take(9)
    (
        pool_sem,
        own_sem,
        halo_send,
        halo_recv,
        up_send,
        up_recv,
        down_send,
        down_recv,
        part_send,
        part_recv,
        sq_send,
        sq_recv,
        edge_sem,
        pass_send,
        pass_recv,
    ) = rest

    me = lax.axis_index("ctx")
    mem = lax.axis_index("mem")
    z, p = me // PLANE, me % PLANE
    x, core = p // 2, p % 2

    def in_plane(r):
        return {"ctx": z * PLANE + (p + r) % PLANE}

    def on_line(r):
        return {"ctx": ((z + r) % PLANES) * PLANE + p}

    def mem_peer(r):
        return {"mem": (mem + r) % 8}

    above, below = on_line(1), on_line(PLANES - 1)
    loads = [
        pltpu.make_async_copy(k_ref, near_k.at[pl.ds(2 * TOK, TOK)], own_sem.at[0]),
        pltpu.make_async_copy(v_ref, near_v.at[pl.ds(2 * TOK, TOK)], own_sem.at[1]),
        pltpu.make_async_copy(q_hbm, q_ref, own_sem.at[2]),
        pltpu.make_async_copy(gate_hbm, gate_ref, own_sem.at[3]),
        pltpu.make_async_copy(gain_hbm, gain_ref, own_sem.at[4]),
    ]
    for load in loads:
        load.start()

    greet(
        [(in_plane(r), None) for r in range(1, 8)]
        + [(mem_peer(r), None) for r in range(1, 8)]
        + [(on_line(r), None) for r in range(1, 8)]
    )

    def edge_copy():
        return pltpu.make_async_remote_copy(
            src_ref=edge_ref,
            dst_ref=edge_in,
            send_sem=edge_sem.at[0],
            recv_sem=edge_sem.at[1],
            device_id=above,
            device_id_type=MESH,
        )

    def edge_here():
        for source in range(2):

            @pl.when((z < PLANES - 1) & (p == 6 + source))
            def _(source=source):
                edge_own(0).wait()

            @pl.when((z < PLANES - 1) & (p != 6 + source))
            def _(source=source):
                edge_arrival(source).wait_recv()

        @pl.when(z < PLANES - 1)
        def _():
            edge_copy().start()

    def passed(source, to):
        near = near_v if source % 2 else near_k
        columns = pl.ds(source // 2 * HD, HD)
        came = edge_in if to == 0 else edge_in.at[pl.ds(TOK, TOK)]
        return came, near.at[pl.ds(0, 2 * TOK if to == 0 else TOK), columns]

    def pass_copy(source, to):
        came, near = passed(source, to)
        return pltpu.make_async_remote_copy(
            src_ref=came,
            dst_ref=near,
            send_sem=pass_send.at[to],
            recv_sem=pass_recv.at[source],
            device_id={"ctx": z * PLANE + to},
            device_id_type=MESH,
        )

    def pass_own(source):
        came, near = passed(source, source)
        return pltpu.make_async_copy(came, near, pass_recv.at[source])

    def each_pass(source, remote, local):
        for to in range(2):
            if source == to:
                local(source)
            else:
                remote(source, to)

    def pass_on():
        edge_copy().wait_recv()
        for source in range(PLANE):

            @pl.when(p == source)
            def _(source=source):
                each_pass(
                    source,
                    lambda s, t: pass_copy(s, t).start(),
                    lambda s: pass_own(s).start(),
                )

    lanes = lax.broadcasted_iota(jnp.int32, (8, HD), 1)
    row = jnp.zeros((8, HD), jnp.int32)
    for j in range(REQ):
        row = jnp.where(lanes == j, ids_ref[j // 4, j % 4], row)
    line[p] = row

    def copy1(r):
        return pltpu.make_async_remote_copy(
            src_ref=line.at[p],
            dst_ref=line.at[p],
            send_sem=send1.at[r],
            recv_sem=recv1.at[p],
            device_id=in_plane(r),
            device_id_type=MESH,
        )

    def arrival1(r):
        q = (p + r) % PLANE
        return pltpu.make_async_remote_copy(
            src_ref=line.at[q],
            dst_ref=line.at[q],
            send_sem=send1.at[r],
            recv_sem=recv1.at[q],
            device_id=in_plane(r),
            device_id_type=MESH,
        )

    for r in range(1, 8):
        copy1(r).start()

    def part(r, chunk, ref):
        q = (p + r) % PLANE
        return ref.at[:, pl.ds(chunk * ROWS, ROWS), pl.ds(pl.multiple_of((q // 2) * HD, HD), HD)]

    def copy_a(r, chunk, ref):
        return pltpu.make_async_remote_copy(
            src_ref=part(r, chunk, ref),
            dst_ref=pools[chunk].at[pl.ds(p * 8, 8)],
            send_sem=send_a.at[chunk, r],
            recv_sem=recv_a.at[chunk, p],
            device_id=in_plane(r),
            device_id_type=MESH,
        )

    def arrival_a(r, chunk):
        q = (p + r) % PLANE
        return pltpu.make_async_remote_copy(
            src_ref=part(r, chunk, mk_ref),
            dst_ref=pools[chunk].at[pl.ds(q * 8, 8)],
            send_sem=send_a.at[chunk, r],
            recv_sem=recv_a.at[chunk, q],
            device_id=in_plane(r),
            device_id_type=MESH,
        )

    def own_a(ref, chunk):
        return pltpu.make_async_copy(
            part(0, chunk, ref), pools[chunk].at[pl.ds(p * 8, 8)], pool_sem.at[chunk]
        )

    def spread_blocks(chunk):
        for r in (4, 3, 5, 2, 6, 1, 7):
            to_core = (core + r) % 2

            @pl.when(to_core == 0)
            def _():
                copy_a(r, chunk, mk_ref).start()

            @pl.when(to_core == 1)
            def _():
                copy_a(r, chunk, mv_ref).start()

        @pl.when(core == 0)
        def _():
            own_a(mk_ref, chunk).start()

        @pl.when(core == 1)
        def _():
            own_a(mv_ref, chunk).start()

    def blocks_here(chunk):
        own_a(mk_ref, chunk).wait()
        for r in range(1, 8):
            arrival_a(r, chunk).wait_recv()

    spread_blocks(0)

    def edge_part(q):
        ref = v_ref if q % 2 else k_ref
        return ref.at[:, pl.ds(q // 2 * HD, HD)]

    def spread_edge(q):
        return pltpu.make_async_remote_copy(
            src_ref=edge_part(q),
            dst_ref=edge_ref.at[pl.ds(core * TOK, TOK)],
            send_sem=edge_send.at[q],
            recv_sem=edge_recv.at[core],
            device_id={"ctx": z * PLANE + q},
            device_id_type=MESH,
        )

    def edge_arrival(source):
        return pltpu.make_async_remote_copy(
            src_ref=edge_part(0),
            dst_ref=edge_ref.at[pl.ds(source * TOK, TOK)],
            send_sem=edge_send.at[0],
            recv_sem=edge_recv.at[source],
            device_id=in_plane(1),
            device_id_type=MESH,
        )

    def edge_own(q):
        return pltpu.make_async_copy(
            edge_part(q), edge_ref.at[pl.ds(core * TOK, TOK)], pool_sem.at[CHUNKS]
        )

    sends_edge = (x == 3) & (z < PLANES - 1)
    for q in range(PLANE):

        @pl.when(sends_edge & (p != q))
        def _(q=q):
            spread_edge(q).start()

        @pl.when(sends_edge & (p == q))
        def _(q=q):
            edge_own(q).start()

    for chunk in range(1, CHUNKS):
        spread_blocks(chunk)
    def halo(d, which):
        ref, near = ((k_ref, near_k), (v_ref, near_v))[which]
        return pltpu.make_async_remote_copy(
            src_ref=ref,
            dst_ref=near.at[pl.ds((2 - d) * TOK, TOK)],
            send_sem=halo_send.at[2 * d - 2 + which],
            recv_sem=halo_recv.at[2 * d - 2 + which],
            device_id={"ctx": me + d},
            device_id_type=MESH,
        )

    for d in (1, 2):

        @pl.when(p + d < PLANE)
        def _():
            halo(d, 0).start()
            halo(d, 1).start()

        @pl.when((z == 0) & (p < d))
        def _():
            near_k[pl.ds((2 - d) * TOK, TOK)] = jnp.zeros((TOK, HEADS_HERE * HD), BF16)
            near_v[pl.ds((2 - d) * TOK, TOK)] = jnp.zeros((TOK, HEADS_HERE * HD), BF16)

    for r in range(1, 8):
        arrival1(r).wait_recv()
    rows = lax.broadcasted_iota(jnp.int32, (8, HD), 0)
    whole = jnp.zeros((8, HD), jnp.int32)
    for q in range(PLANE):
        whole = jnp.where(rows == q, line[q], whole)
    lists[z] = whole

    def copy2(r):
        return pltpu.make_async_remote_copy(
            src_ref=lists.at[z],
            dst_ref=lists.at[z],
            send_sem=send2.at[r],
            recv_sem=recv2.at[z],
            device_id=on_line(r),
            device_id_type=MESH,
        )

    def arrival2(r):
        q = (z + r) % PLANES
        return pltpu.make_async_remote_copy(
            src_ref=lists.at[q],
            dst_ref=lists.at[q],
            send_sem=send2.at[r],
            recv_sem=recv2.at[q],
            device_id=on_line(r),
            device_id_type=MESH,
        )

    for r in range(1, 8):
        copy2(r).start()
    for r in range(1, 8):
        arrival2(r).wait_recv()
    schedule(tier, lists[...].reshape(PLANES * PLANE, HD).astype(F32), z, table_out)
    to_scalars = pltpu.make_async_copy(table_out, table, table_sem)
    to_scalars.start()
    to_scalars.wait()
    fits_ref[0] = table[1, 4, 0]
    edge_here()
    for load in loads:
        load.wait()
    blocks_here(0)

    caps_g = [c // group for c in caps]

    def cap_at(step):
        value = jnp.int32(caps_g[3])
        for i in (2, 1, 0):
            value = jnp.where(step == i, caps_g[i], value)
        return value

    def floor_at(step):
        return jnp.where(step >= PLANES - 2, left_out // group, 0)

    def lag_at(step):
        value = jnp.int32(0)
        for i in range(4):
            value = jnp.where(step == 4 + i, lags[i], value)
        return value

    def conveyor(k, step, target, pool, into, onward, send, recv, row):
        cap = cap_at(step)
        position = jnp.where(step <= 3, k + groups - cap, k - lag_at(step))
        inside = (position >= 0) & (position < CHUNKS * groups)
        at = jnp.maximum(position, 0)
        chunk = at // groups
        g = groups - 1 - at % groups
        active = inside & (g < cap)
        incoming = (step > 0) & (g < cap_at(step - 1)) & (g >= floor_at(step - 1))

        def copy(c):
            span = pl.ds(g * group, group)
            return pltpu.make_async_remote_copy(
                src_ref=onward[c].at[span],
                dst_ref=into[c].at[span],
                send_sem=send.at[c, g],
                recv_sem=recv.at[c, g],
                device_id=target,
                device_id_type=MESH,
            )

        for c in range(CHUNKS):

            @pl.when(active & (chunk == c))
            def _(c=c):
                @pl.when(incoming)
                def _():
                    copy(c).wait_recv()

                @pl.when((step < PLANES - 1) & (g >= floor_at(step)))
                def _():
                    for i in range(group):
                        slot = g * group + i
                        inject = table[1, row + slot // HD, slot % HD]
                        local = pool[c][jnp.clip(inject, 0, LOCAL - 1)]
                        onward[c][slot] = jnp.where(inject >= 0, local, into[c][slot])
                    copy(c).start()

    def part_copy(c, r):
        q = (p + r) % PLANE
        return pltpu.make_async_remote_copy(
            src_ref=parts_out[c].at[q],
            dst_ref=parts[c].at[p],
            send_sem=part_send.at[c, r],
            recv_sem=part_recv.at[c, p],
            device_id=in_plane(r),
            device_id_type=MESH,
        )

    def part_arrival(c, r):
        q = (p + r) % PLANE
        return pltpu.make_async_remote_copy(
            src_ref=parts_out[c].at[q],
            dst_ref=parts[c].at[q],
            send_sem=part_send.at[c, r],
            recv_sem=part_recv.at[c, q],
            device_id=in_plane(r),
            device_id_type=MESH,
        )

    def hand_out(c):
        def pick(q, j):
            place = table[0, q, j]
            own = pools[c][jnp.clip(place, 0, LOCAL - 1)]
            from_below = ups[c][jnp.clip(place - LOCAL, 0, slots - 1)]
            from_above = downs[c][jnp.clip(place - LOCAL - known, 0, slots - 1)]
            return jnp.where(
                place < LOCAL, own, jnp.where(place < LOCAL + known, from_below, from_above)
            )

        for r in (4, 3, 5, 2, 6, 1, 7):
            q = (p + r) % PLANE
            for j in range(REQ):
                parts_out[c][q, j] = pick(q, j)
            part_copy(c, r).start()
        for j in range(REQ):
            parts[c][p, j] = pick(p, j)

    def window_piece(head, tile):
        columns = pl.ds(pl.multiple_of(head * HD, HD), HD)
        rows = pl.ds(pl.multiple_of(tile * 128, 128), 128)
        near = pl.ds(pl.multiple_of(tile * 128, 128), 640)
        scores = lax.dot_general(
            q_ref[rows, columns],
            near_k[near, columns],
            (((1,), (1,)), ((), ())),
            preferred_element_type=F32,
        )
        key = lax.broadcasted_iota(jnp.int32, (128, 640), 1)
        ahead = key - lax.broadcasted_iota(jnp.int32, (128, 640), 0)
        first = me * TOK - 2 * TOK + tile * 128
        allowed = (ahead > 0) & (ahead <= 512) & (key >= -first)
        scores = jnp.where(allowed, scores * SCALE, -jnp.inf)
        weights = jnp.exp(scores - jnp.max(scores, axis=1, keepdims=True))
        total = jnp.sum(weights, axis=1, keepdims=True)
        product = jnp.dot(weights.astype(BF16), near_v[near, columns], preferred_element_type=F32)
        mixed[rows, columns] = product / total

    steps = CHUNKS * groups + max(lags[2], lags[3] - left_out // group)
    far = jnp.maximum(z, PLANES - 1 - z)
    far = lag_at(far) - floor_at(far - 1)
    pieces = 2 * HEADS_HERE
    pass_step = 5
    early, every, first_piece = 3, 2, groups + 6

    def step_body(k, carry):
        for chunk in range(1, CHUNKS):

            @pl.when(k == (chunk - 1) * groups + caps_g[0])
            def _(chunk=chunk):
                blocks_here(chunk)

        conveyor(k, z, above, pools, ups, ups_out, up_send, up_recv, 0)
        conveyor(k, PLANES - 1 - z, below, pools, downs, downs_out, down_send, down_recv, 2)
        for c in range(CHUNKS):

            @pl.when(k == (c + 1) * groups - 1 + far)
            def _(c=c):
                hand_out(c)

        @pl.when((k == pass_step) & (z > 0))
        def _():
            pass_on()

        @pl.when(k == first_piece)
        def _():
            for d in (1, 2):

                @pl.when(p >= d)
                def _():
                    halo(d, 0).wait_recv()
                    halo(d, 1).wait_recv()

            for to in range(2):

                @pl.when((z > 0) & (p == to))
                def _(to=to):
                    for source in range(PLANE):
                        if source == to:
                            pass_own(source).wait()
                        else:
                            pass_copy(source, to).wait_recv()

        since = k - first_piece
        piece = jnp.maximum(since, 0) // every

        @pl.when((since >= 0) & (since % every == 0) & (piece < early))
        def _():
            window_piece(piece // 2, piece % 2)

        return carry

    lax.fori_loop(0, steps, step_body, 0)

    def late_piece(piece, carry):
        window_piece(piece // 2, piece % 2)
        return carry

    lax.fori_loop(early, pieces, late_piece, 0)

    for c in range(CHUNKS):
        for r in range(1, 8):
            part_arrival(c, r).wait_recv()

    opened = 1.0 / (1.0 + jnp.exp(-gate_ref[...]))
    eye = lax.broadcasted_iota(jnp.int32, (128, 128), 0) == lax.broadcasted_iota(
        jnp.int32, (128, 128), 1
    )
    for tile in range(2):
        rows = pl.ds(tile * 128, 128)
        total_square = jnp.zeros((128, 1), F32)
        for head in range(HEADS_HERE):
            columns = pl.ds(head * HD, HD)
            keys = [parts[c][2 * head, 4 * tile : 4 * tile + 4].reshape(4 * ROWS, HD) for c in range(CHUNKS)]
            vals = [parts[c][2 * head + 1, 4 * tile : 4 * tile + 4].reshape(4 * ROWS, HD) for c in range(CHUNKS)]
            scores = lax.dot_general(
                q_ref[rows, columns],
                jnp.concatenate(keys, axis=0),
                (((1,), (1,)), ((), ())),
                preferred_element_type=F32,
            ) * SCALE
            weights = jnp.exp(scores - jnp.max(scores, axis=1, keepdims=True))
            total = jnp.sum(weights, axis=1, keepdims=True)
            product = jnp.dot(
                weights.astype(BF16), jnp.concatenate(vals, axis=0), preferred_element_type=F32
            )
            share = opened[:, head : head + 1]
            both = share * (product / total) + (1.0 - share) * mixed[rows, columns]
            mixed[rows, columns] = both
            total_square += jnp.sum(both * both, axis=1, keepdims=True)
        squares_out[pl.ds(tile * 8, 8)] = jnp.broadcast_to(
            jnp.sum(jnp.where(eye, total_square, 0.0), axis=0, keepdims=True), (8, 128)
        )

    def square_copy(r):
        return pltpu.make_async_remote_copy(
            src_ref=squares_out,
            dst_ref=squares.at[mem],
            send_sem=sq_send.at[r],
            recv_sem=sq_recv.at[mem],
            device_id=mem_peer(r),
            device_id_type=MESH,
        )

    def square_arrival(r):
        return pltpu.make_async_remote_copy(
            src_ref=squares_out,
            dst_ref=squares.at[(mem + r) % 8],
            send_sem=sq_send.at[r],
            recv_sem=sq_recv.at[(mem + r) % 8],
            device_id=mem_peer(r),
            device_id_type=MESH,
        )

    for r in (4, 1, 2, 3, 5, 6, 7):
        square_copy(r).start()
    squares[mem] = squares_out[...]
    for r in range(1, 8):
        square_arrival(r).wait_recv()
    summed = squares[0]
    for m in range(1, 8):
        summed = summed + squares[m]
    for tile in range(2):
        rows = pl.ds(tile * 128, 128)
        column = jnp.sum(
            jnp.where(eye, summed[tile * 8 : tile * 8 + 1], 0.0), axis=1, keepdims=True
        )
        factor = lax.rsqrt(column / FEATURES + 1e-6)
        out_ref[rows] = (mixed[rows] * gain_ref[...] * factor).astype(BF16)

    for r in range(1, 8):
        square_copy(r).wait_send()
        for c in range(CHUNKS):
            part_copy(c, r).wait_send()
        copy1(r).wait_send()
        copy2(r).wait_send()
        for chunk in range(CHUNKS):
            copy_a(r, chunk, mk_ref).wait_send()
    for q in range(PLANE):

        @pl.when(sends_edge & (p != q))
        def _(q=q):
            spread_edge(q).wait_send()

    for d in (1, 2):

        @pl.when(p + d < PLANE)
        def _():
            halo(d, 0).wait_send()
            halo(d, 1).wait_send()

    @pl.when(z < PLANES - 1)
    def _():
        edge_copy().wait_send()

    for source in range(PLANE):

        @pl.when((z > 0) & (p == source))
        def _(source=source):
            each_pass(source, lambda s, t: pass_copy(s, t).wait_send(), lambda s: None)

    for step, into, onward, send, recv, target in (
        (z, ups, ups_out, up_send, up_recv, above),
        (PLANES - 1 - z, downs, downs_out, down_send, down_recv, below),
    ):

        @pl.when(step < PLANES - 1)
        def _():
            def sent(g, carry):
                span = pl.ds(g * group, group)
                for c in range(CHUNKS):
                    pltpu.make_async_remote_copy(
                        src_ref=onward[c].at[span],
                        dst_ref=into[c].at[span],
                        send_sem=send.at[c, g],
                        recv_sem=recv.at[c, g],
                        device_id=target,
                        device_id_type=MESH,
                    ).wait_send()
                return carry

            lax.fori_loop(floor_at(step), cap_at(step), sent, 0)


def attend(tier, collective_id, ids, gate, gain, q, k, v, mk, mv):
    slots = tier[0][-1]
    groups = slots // tier[1]
    ring = [pltpu.VMEM((slots, ROWS, HD), BF16)] * CHUNKS
    hand = [pltpu.VMEM((PLANE, REQ, ROWS, HD), BF16)] * CHUNKS
    dma = pltpu.SemaphoreType.DMA
    return pl.pallas_call(
        functools.partial(attend_kernel, tier),
        out_shape=[
            jax.ShapeDtypeStruct((TOK, HEADS_HERE * HD), BF16),
            jax.ShapeDtypeStruct((1,), jnp.int32),
        ],
        in_specs=[SMEM] + [HBM] * 7,
        out_specs=[VMEM, SMEM],
        scratch_shapes=[
            pltpu.VMEM((2, 8, HD), jnp.int32),
            pltpu.SMEM((2, 8, HD), jnp.int32),
            pltpu.VMEM((PLANE, 8, HD), jnp.int32),
            pltpu.VMEM((PLANES, 8, HD), jnp.int32),
            pltpu.VMEM((1, HEADS_HERE), F32),
            pltpu.VMEM((TOK, HEADS_HERE * HD), BF16),
            pltpu.VMEM((1, HEADS_HERE * HD), F32),
            pltpu.VMEM((3 * TOK, HEADS_HERE * HD), BF16),
            pltpu.VMEM((3 * TOK, HEADS_HERE * HD), BF16),
            pltpu.VMEM((TOK, HEADS_HERE * HD), F32),
            *[pltpu.VMEM((LOCAL, ROWS, HD), BF16)] * CHUNKS,
            *ring,
            *ring,
            *ring,
            *ring,
            *hand,
            *hand,
            pltpu.VMEM((16, HD), F32),
            pltpu.VMEM((8, 16, HD), F32),
            pltpu.VMEM((2 * TOK, HD), BF16),
            pltpu.VMEM((2 * TOK, HD), BF16),
            dma(()),
            dma((8,)),
            dma((8,)),
            dma((8,)),
            dma((8,)),
            dma((CHUNKS, 8)),
            dma((CHUNKS, 8)),
            dma((8,)),
            dma((2,)),
            dma((CHUNKS + 1,)),
            dma((5,)),
            dma((4,)),
            dma((4,)),
            dma((CHUNKS, groups)),
            dma((CHUNKS, groups)),
            dma((CHUNKS, groups)),
            dma((CHUNKS, groups)),
            dma((CHUNKS, 8)),
            dma((CHUNKS, 8)),
            dma((8,)),
            dma((8,)),
            dma((2,)),
            dma((2,)),
            dma((8,)),
        ],
        compiler_params=pltpu.CompilerParams(
            collective_id=collective_id, has_side_effects=True, vmem_limit_bytes=60 << 20
        ),
        name="attend_" + str(slots),
    )(ids, gate, gain, q, k, v, mk, mv)


def shards(queries, keys, values, memory_keys, memory_values, retrieval, gate, gain):
    operands = (
        retrieval,
        gate.reshape(1, -1),
        gain.reshape(1, -1),
        queries,
        keys,
        values,
        memory_keys,
        memory_values,
    )
    out, fits = attend(SHORT, 0, *operands)
    return lax.cond(
        fits[0] > 0,
        lambda out, *_: out,
        lambda _, *operands: attend(LONG, 1, *operands)[0],
        out,
        *operands,
    )


def solution(mesh):
    in_specs = (
        P("ctx", "mem"),
        P("ctx", "mem"),
        P("ctx", "mem"),
        P("ctx", None, "mem"),
        P("ctx", None, "mem"),
        P("ctx", None),
        P("mem"),
        P("mem"),
    )
    return jax.shard_map(
        shards, mesh=mesh, in_specs=in_specs, out_specs=P("ctx", "mem"), check_vma=False
    )
```
